32 devices in a mesh: fsdp: 8 (over z, x), dp: 4 (over y, core).
Axes of the slice: x: 2, y: 2, z: 4, core: 2. Of those that a mesh axis runs over, the one named last changes fastest.
Arguments:
- inputs: bfloat16 [32768, 1024], P(('fsdp', 'dp')), may hold values from -6 to 6
- encoder: bfloat16 [32768, 1024], P(('fsdp', 'dp')), may hold values from -6 to 6
- cotangent: bfloat16 [32768, 1024], P(('fsdp', 'dp')), may hold values from -6 to 6
- buckets: int32 [32], P(('fsdp', 'dp')), may hold values from 0 to 2, as said below
- lengths: int32 [32, 4], P(('fsdp', 'dp')), may hold values from 0 to 1024, as said below
- self_query: bfloat16 [1024, 1024], P('fsdp'), may hold values from -0.1875 to 0.1875
- self_key: bfloat16 [1024, 1024], P('fsdp'), may hold values from -0.1875 to 0.1875
- self_value: bfloat16 [1024, 1024], P('fsdp'), may hold values from -0.1875 to 0.1875
- self_output: bfloat16 [1024, 1024], P('fsdp'), may hold values from -1.5 to 1.5
- cross_query: bfloat16 [1024, 1024], P('fsdp'), may hold values from -0.1875 to 0.1875
- cross_key: bfloat16 [1024, 1024], P('fsdp'), may hold values from -0.1875 to 0.1875
- cross_value: bfloat16 [1024, 1024], P('fsdp'), may hold values from -0.1875 to 0.1875
- cross_output: bfloat16 [1024, 1024], P('fsdp'), may hold values from -1.5 to 1.5
- fc_first: bfloat16 [1024, 4096], P('fsdp'), may hold values from -0.1875 to 0.1875
- fc_second: bfloat16 [4096, 1024], P('fsdp'), may hold values from -0.09375 to 0.09375
- norm_gains: float32 [3, 1024], replicated, may hold values from 0.5 to 1.5
- down_master: float32 [1024, 512], replicated, may hold values from -0.1875 to 0.1875
- up_master: float32 [512, 1024], replicated, may hold values from -0.0625 to 0.0625
- down_first: float32 [1024, 512], replicated, may hold values from -48 to 48
- down_second: float32 [1024, 512], replicated, may hold values from 2.62144 to 42.5984
- up_first: float32 [512, 1024], replicated, may hold values from -128 to 128
- up_second: float32 [512, 1024], replicated, may hold values from 22.9376 to 360.448
Outputs:
- outputs: bfloat16 [32768, 1024], P(('fsdp', 'dp'))
- input_grad: bfloat16 [32768, 1024], P(('fsdp', 'dp'))
- encoder_grad: bfloat16 [32768, 1024], P(('fsdp', 'dp'))
- down_grad: float32 [1024, 512], replicated
- up_grad: float32 [512, 1024], replicated
- down_first_new: float32 [1024, 512], replicated
- down_second_new: float32 [1024, 512], replicated
- up_first_new: float32 [512, 1024], replicated
- up_second_new: float32 [512, 1024], replicated
- down_master_new: float32 [1024, 512], replicated
- up_master_new: float32 [512, 1024], replicated
- down_weight: bfloat16 [1024, 512], replicated
- up_weight: bfloat16 [512, 1024], replicated
The draws below stay inside these ranges and needn't reach their ends.
Inputs may be any that keep to these rules, and one draw needn't show every extreme that they name: `buckets`: bucket 0 holds four items of 256 slots, bucket 1 two of 512, bucket 2 one of 1024; item i of a block takes its slots i * S to (i + 1) * S - 1. 32 // 6 blocks hold bucket 0, as many hold bucket 1, the rest bucket 2. `lengths`: for the items that a block's bucket has, the length lies between max(1, S // 4) and the item size S; the other entries are 0. Some item fills all 1024 slots of its block.
All inputs are finite; a program needn't handle non-finite values.
Results may differ from the reference program's by a relative error of at most 0.02.
Values may be sent and summed in bfloat16 or wider, within the bound.
No kernel may reach another device: no remote copies, remote signals or barrier semaphores. Data moves between devices by JAX's collectives and lax.ppermute only.
A program may use at most 320 MiB of HBM per device.

```python
import math
import jax
import jax.numpy as jnp
from jax import lax

D = 1024
HEADS = 16
HEAD_DIM = 64
FF = 4096
ADAPTER = 512
STEP = 10
TOK_DEV = 1024
BLOCKS = 32
TOKENS = 32768


def bucket_layout(key):
    ranking = jax.random.permutation(key, BLOCKS).astype(jnp.int32)
    share_count = BLOCKS // 6
    layout = jnp.where(ranking < share_count, 0, jnp.where(ranking < 2 * share_count, 1, 2)).astype(jnp.int32)
    return (layout, ranking)


def draw_buckets(key, part):
    layout, ranking = bucket_layout(key)
    return layout


def draw_lengths(key, part):
    layout, ranking = bucket_layout(key)
    key = jax.random.fold_in(key, 5)
    item_size = jnp.right_shift(jnp.int32(TOK_DEV), 2 - layout)[:, None]
    item_count = jnp.left_shift(jnp.int32(1), 2 - layout)[:, None]
    lowest = jnp.maximum(item_size // 4, 1)
    random_bits = jax.random.randint(key, (BLOCKS, 4), 0, 1 << 20, dtype=jnp.int32)
    lengths_drawn = lowest + random_bits % (item_size - lowest + 1)
    slot_index = jnp.arange(4, dtype=jnp.int32)[None, :]
    lengths_drawn = jnp.where(slot_index < item_count, lengths_drawn, 0)
    longest = (ranking == BLOCKS - 1)[:, None] & (slot_index == 0)
    return jnp.where(longest, TOK_DEV, lengths_drawn).astype(jnp.int32)


def block_scale(stream_key, extent, cuts, least, high):
    loudness, own = 1.0, jax.random.fold_in(stream_key, 6)
    for dim, parts in cuts:
        heights = jnp.exp(jax.random.uniform(jax.random.fold_in(own, dim), (parts,), jnp.float32, least / len(cuts), high / len(cuts)))
        loudness = loudness * jnp.repeat(heights, extent[dim] // parts).reshape([-1 if axis == dim else 1 for axis in range(len(extent))])
    return loudness


def scatter_about(key, extent, width, most, shards=(), held_as=jnp.bfloat16):
    drawn = jax.random.normal(key, extent, jnp.float32) * width
    if len(shards) > 0:
        drawn = block_scale(key, extent, shards, -0.22, 0.18) * drawn
    return jnp.clip(drawn, min=-most, max=most).astype(held_as)


def setup_inputs(seed: int = 0) -> dict:
    key_of = jax.random.split(jax.random.key(seed), 23)
    return {
        "inputs": scatter_about(key_of[0], (TOKENS, D), 1.0, 6.0, ((0, 32),)),
        "encoder": scatter_about(key_of[1], (TOKENS, D), 1.0, 6.0, ((0, 32),)),
        "cotangent": scatter_about(key_of[2], (TOKENS, D), 1.0, 6.0, ((0, 32),)),
        "buckets": draw_buckets(jax.random.fold_in(key_of[22], 71), 0),
        "lengths": draw_lengths(jax.random.fold_in(key_of[22], 71), 0),
        "self_query": scatter_about(key_of[5], (D, D), D ** -0.5, 0.1875, ((0, 8),)),
        "self_key": scatter_about(key_of[6], (D, D), D ** -0.5, 0.1875, ((0, 8),)),
        "self_value": scatter_about(key_of[7], (D, D), D ** -0.5, 0.1875, ((0, 8),)),
        "self_output": scatter_about(key_of[8], (D, D), (D // 64) ** -0.5, 1.5, ((0, 8),)),
        "cross_query": scatter_about(key_of[9], (D, D), D ** -0.5, 0.1875, ((0, 8),)),
        "cross_key": scatter_about(key_of[10], (D, D), D ** -0.5, 0.1875, ((0, 8),)),
        "cross_value": scatter_about(key_of[11], (D, D), D ** -0.5, 0.1875, ((0, 8),)),
        "cross_output": scatter_about(key_of[12], (D, D), (D // 64) ** -0.5, 1.5, ((0, 8),)),
        "fc_first": scatter_about(key_of[13], (D, FF), D ** -0.5, 0.1875, ((0, 8),)),
        "fc_second": scatter_about(key_of[14], (FF, D), FF ** -0.5, 0.09375, ((0, 8),)),
        "norm_gains": jnp.clip(1.0 + 0.1 * jax.random.normal(key_of[15], (3, D), jnp.float32), 0.5, 1.5),
        "down_master": scatter_about(key_of[16], (D, ADAPTER), D ** -0.5, 0.1875, (), jnp.float32),
        "up_master": scatter_about(key_of[17], (ADAPTER, D), (16 * ADAPTER) ** -0.5, 0.0625, (), jnp.float32),
        "down_first": scatter_about(key_of[18], (D, ADAPTER), (0.045 * TOKENS ** 0.5), 48.0, (), jnp.float32),
        "down_second": jnp.clip(jnp.exp(jax.random.uniform(key_of[19], (D, ADAPTER), jnp.float32, math.log(2.62144), math.log(42.5984))), 2.62144, 42.5984),
        "up_first": scatter_about(key_of[20], (ADAPTER, D), (0.13 * TOKENS ** 0.5), 128.0, (), jnp.float32),
        "up_second": jnp.clip(jnp.exp(jax.random.uniform(key_of[21], (ADAPTER, D), jnp.float32, math.log(22.9376), math.log(360.448))), 22.9376, 360.448),
    }


@jax.custom_vjp
def low(v):
    return lax.optimization_barrier(v.astype(jnp.bfloat16)).astype(jnp.float32)

@jax.custom_vjp
def low_back(v):
    return v

def low_keep(v):
    return (low(v), None)

def low_pass(kept, grad):
    return (grad,)

def back_keep(v):
    return (v, None)

def back_low(kept, grad):
    return (low(grad),)
low.defvjp(low_keep, low_pass)
low_back.defvjp(back_keep, back_low)
precise = lax.Precision.HIGHEST
epsilon_norm = 1e-05
beta_first = 0.9
beta_second = 0.999
learn_rate = 0.05
weight_decay = 0.01
epsilon_adam = 1e-08

def matmul(left, right):
    return jnp.dot(left, right, precision=precise, preferred_element_type=jnp.float32)

def layer_norm(values, gain):
    centre = values - lax.optimization_barrier(jnp.mean(values, axis=-1, keepdims=True))
    variance = lax.optimization_barrier(jnp.mean(centre * centre, axis=-1, keepdims=True))
    return centre * lax.rsqrt(variance + epsilon_norm) * gain

def gelu_exact(values):
    return jax.nn.gelu(values, approximate=False)

def attention(queries, keys, values, allowed):
    tokens = queries.shape[0]
    query_heads = queries.reshape(tokens, HEADS, HEAD_DIM)
    key_heads = keys.reshape(tokens, HEADS, HEAD_DIM)
    value_heads = values.reshape(tokens, HEADS, HEAD_DIM)
    scores = jnp.einsum('qhd,khd->hqk', query_heads, key_heads, precision=precise) * HEAD_DIM ** (-0.5)
    scores = low_back(scores)
    scores = jnp.where(allowed[None], scores, -1e+30)
    largest = lax.optimization_barrier(jnp.max(scores, axis=-1, keepdims=True))
    weights_exp = jnp.exp(scores - largest)
    probability = low(weights_exp / lax.optimization_barrier(jnp.sum(weights_exp, axis=-1, keepdims=True)))
    attended = jnp.einsum('hqk,khd->qhd', probability, value_heads, precision=precise)
    return attended.reshape(tokens, HEADS * HEAD_DIM)

def block_masks(bucket, item_lengths):
    positions = jnp.arange(TOK_DEV, dtype=jnp.int32)
    item_size = jnp.right_shift(jnp.int32(TOK_DEV), (2 - bucket).astype(jnp.int32))
    item_of = positions // item_size
    within = positions - item_of * item_size
    row_length = item_lengths[item_of]
    valid_rows = within < row_length
    cross_mask = (item_of[:, None] == item_of[None, :]) & valid_rows[None, :]
    self_mask = cross_mask & (positions[None, :] <= positions[:, None])
    return (valid_rows, self_mask, cross_mask)

def forward(inputs, encoder, down_master, up_master, frozen, norm_gains, self_mask, cross_mask):
    self_query, self_key, self_value, self_output, cross_query, cross_key, cross_value, cross_output, fc_first, fc_second = frozen
    query_self = low_back(low(matmul(inputs, self_query)))
    key_self = low_back(low(matmul(inputs, self_key)))
    value_self = low_back(low(matmul(inputs, self_value)))
    self_out = low_back(low(attention(query_self, key_self, value_self, self_mask)))
    first = layer_norm(inputs + low_back(matmul(self_out, self_output)), norm_gains[0])
    first_low = low(first)
    query_cross = low_back(low(matmul(first_low, cross_query)))
    key_cross = low_back(low(matmul(encoder, cross_key)))
    value_cross = low_back(low(matmul(encoder, cross_value)))
    cross_out = low_back(low(attention(query_cross, key_cross, value_cross, cross_mask)))
    second = layer_norm(first + low_back(matmul(cross_out, cross_output)), norm_gains[1])
    second_low = low(second)
    inner_pre = low_back(matmul(second_low, fc_first))
    activated = low(gelu_exact(inner_pre))
    feed_out = low_back(matmul(activated, fc_second))
    adapter_pre = low_back(matmul(second_low, low(down_master)))
    adapter_act = low(gelu_exact(adapter_pre))
    adapter_out = low_back(matmul(adapter_act, low(up_master)))
    return layer_norm(second + feed_out + 4.0 * adapter_out, norm_gains[2])

def adamw(master, first_moment, second_moment, gradient):
    first_new = beta_first * first_moment + (1.0 - beta_first) * gradient
    second_new = beta_second * second_moment + (1.0 - beta_second) * gradient * gradient
    first_hat = first_new / (1.0 - beta_first ** STEP)
    second_hat = second_new / (1.0 - beta_second ** STEP)
    master_new = master - learn_rate * (first_hat / (jnp.sqrt(second_hat) + epsilon_adam) + weight_decay * master)
    return (first_new, second_new, master_new)

def reference(inputs, encoder, cotangent, buckets, lengths, self_query, self_key, self_value, self_output, cross_query, cross_key, cross_value, cross_output, fc_first, fc_second, norm_gains, down_master, up_master, down_first, down_second, up_first, up_second):
    frozen = tuple((matrix.astype(jnp.float32) for matrix in (self_query, self_key, self_value, self_output, cross_query, cross_key, cross_value, cross_output, fc_first, fc_second)))
    block_count = TOKENS // TOK_DEV

    def shaped(array):
        return array.reshape(block_count, TOK_DEV, D)

    def one_block(running, pieces):
        block_inputs, block_encoder, block_cotangent, bucket, item_lengths = pieces
        valid_rows, self_mask, cross_mask = block_masks(bucket, item_lengths)

        def local(block_x, block_e, down_w, up_w):
            return forward(block_x, block_e, down_w, up_w, frozen, norm_gains, self_mask, cross_mask)
        result, pullback = jax.vjp(local, block_inputs.astype(jnp.float32), block_encoder.astype(jnp.float32), down_master, up_master)
        gradients = pullback(block_cotangent.astype(jnp.float32) * valid_rows[:, None].astype(jnp.float32))
        summed = (running[0] + gradients[2], running[1] + gradients[3])
        return (summed, (result.astype(jnp.bfloat16), gradients[0].astype(jnp.bfloat16), gradients[1].astype(jnp.bfloat16)))
    start = (jnp.zeros((D, ADAPTER), jnp.float32), jnp.zeros((ADAPTER, D), jnp.float32))
    (down_grad, up_grad), (outputs, input_grad, encoder_grad) = lax.scan(one_block, start, (shaped(inputs), shaped(encoder), shaped(cotangent), buckets, lengths))
    down_first_new, down_second_new, down_master_new = adamw(down_master, down_first, down_second, down_grad)
    up_first_new, up_second_new, up_master_new = adamw(up_master, up_first, up_second, up_grad)
    return (outputs.reshape(TOKENS, D), input_grad.reshape(TOKENS, D), encoder_grad.reshape(TOKENS, D), down_grad, up_grad, down_first_new, down_second_new, up_first_new, up_second_new, down_master_new, up_master_new, down_master_new.astype(jnp.bfloat16), up_master_new.astype(jnp.bfloat16))
```

```python
import functools
import math

import jax
import jax.numpy as jnp
from jax import lax
from jax.experimental import pallas as pl
from jax.experimental.pallas import tpu as pltpu
from jax.sharding import PartitionSpec as P

HEAD_DIM = 64
PAIR = 2 * HEAD_DIM
STEP = 10
SLOTS = 4

epsilon_norm = 1e-05
beta_first = 0.9
beta_second = 0.999
learn_rate = 0.05
weight_decay = 0.01
epsilon_adam = 1e-08

f32, bf16 = jnp.float32, jnp.bfloat16
query_scale = HEAD_DIM ** (-0.5) * math.log2(math.e)
forbidden = -(2.0**100)
score_limit = 64.0

params = pltpu.CompilerParams(vmem_limit_bytes=58 * 2**20)


def contract(left, right, left_dim, right_dim):
    return lax.dot_general(
        left, right, (((left_dim,), (right_dim,)), ((), ())), preferred_element_type=f32
    )


def whole(ref):
    values = ref[...]
    return values.reshape(-1, values.shape[-1])


def part(ref, i):
    values = ref[:, i]
    return values.reshape(-1, values.shape[-1])


def quarter(ref, i):
    devices, blocks = ref.shape[:2]
    if devices == 1:
        return part(ref, i)
    values = ref[i * devices // blocks : (i + 1) * devices // blocks]
    return values.reshape(-1, values.shape[-1])


def cost(flops, moved):
    return pl.CostEstimate(flops=int(flops), bytes_accessed=int(moved), transcendentals=0)


def weight_spec(weights, count, at, buffers=None):
    block = (weights.shape[0], count) + weights.shape[2:]
    if buffers is None:
        return pl.BlockSpec(block, lambda *i: (0, at, 0, 0))
    return pl.BlockSpec(block, lambda *i: (0, at, 0, 0), pipeline_mode=pl.Buffered(buffers))


smem = functools.partial(pl.BlockSpec, memory_space=pltpu.SMEM)


def normalise(values):
    centre = values - jnp.mean(values, axis=-1, keepdims=True)
    inverse = lax.rsqrt(jnp.mean(centre * centre, axis=-1, keepdims=True) + epsilon_norm)
    return centre * inverse, inverse


def normalise_back(scaled, normal, inverse):
    return inverse * (
        scaled
        - jnp.mean(scaled, axis=-1, keepdims=True)
        - normal * jnp.mean(scaled * normal, axis=-1, keepdims=True)
    )


def gelu_and_slope(u):
    bell = jnp.exp2(u * u * (-0.5 * math.log2(math.e)))
    t = 1.0 / (1.0 + (0.3275911 * math.sqrt(0.5)) * jnp.abs(u))
    tail = t * (
        0.5 * 0.254829592
        + t
        * (
            0.5 * -0.284496736
            + t * (0.5 * 1.421413741 + t * (0.5 * -1.453152027 + t * (0.5 * 1.061405429)))
        )
    )
    tail = tail * bell
    below = jnp.where(u > 0, 1.0 - tail, tail)
    return u * below, below + u * bell * (1.0 / math.sqrt(2.0 * math.pi))


def head_squares(values):
    wide = values.astype(f32)
    width = values.shape[1]
    member = (
        lax.broadcasted_iota(jnp.int32, (width, PAIR), 0) >> 6
        == lax.broadcasted_iota(jnp.int32, (width, PAIR), 1)
    ).astype(bf16)
    return jnp.max(contract((wide * wide).astype(bf16), member, 1, 0), axis=0, keepdims=True)


def project_kernel(scale, x_ref, w_ref, out_ref, square_ref):
    out = contract(x_ref[...], whole(w_ref), 1, 0)
    if scale != 1.0:
        out = out * jnp.where(pl.program_id(0) == 0, scale, 1.0)
    out = out.astype(bf16)
    out_ref[0] = out
    square_ref[0] = jnp.broadcast_to(head_squares(out), square_ref.shape[1:])


def project(x, weights, count, at, scale):
    tokens, width = x.shape
    block = (weights.shape[0], 1) + weights.shape[2:]
    return pl.pallas_call(
        functools.partial(project_kernel, scale),
        grid=(count,),
        in_specs=[
            pl.BlockSpec((tokens, width), lambda i: (0, 0)),
            pl.BlockSpec(block, lambda i: (0, at + i, 0, 0)),
        ],
        out_specs=[
            pl.BlockSpec((1, tokens, width), lambda i: (i, 0, 0)),
            pl.BlockSpec((1, 8, PAIR), lambda i: (i, 0, 0)),
        ],
        out_shape=[
            jax.ShapeDtypeStruct((count, tokens, width), bf16),
            jax.ShapeDtypeStruct((count, 8, PAIR), f32),
        ],
        compiler_params=params,
        cost_estimate=cost(2 * count * tokens * width * width, 4 * count * tokens * width),
        name="project",
    )(x, weights)


def low_half(rows):
    return lax.broadcasted_iota(jnp.int32, (rows, PAIR), 1) < HEAD_DIM


def choose(head, low):
    if head == 0:
        return lambda own, other: jnp.where(low, own, other)
    return lambda own, other: jnp.where(low, other, own)


def item_shift(bucket, tokens):
    return bucket + (tokens.bit_length() - 1 - 2)


def item_length(item, lengths_ref):
    length = jnp.zeros_like(item)
    for slot in range(SLOTS):
        length = jnp.where(item == slot, lengths_ref[0, slot], length)
    return length


def attend_kernel(
    causal, q_at, k_at, bucket_ref, lengths_ref, qsq_ref, ksq_ref, q_ref, k_ref, v_ref,
    out_ref, weight_ref, scale_ref, qmark, kmark,
):
    tokens = q_ref.shape[-2]
    low = low_half(tokens)
    pair = pl.program_id(0)

    @pl.when(pair == 0)
    def marks():
        shift = item_shift(bucket_ref[0], tokens)
        lane = lax.broadcasted_iota(jnp.int32, (tokens, PAIR), 1) & (HEAD_DIM - 1)
        row = lax.broadcasted_iota(jnp.int32, (tokens, PAIR), 0)
        item = row >> shift
        own = lane == item
        qmark[...] = jnp.where(own, 1.0, 0.0).astype(bf16)
        allowed = own & (row - (item << shift) < item_length(item, lengths_ref))
        kmark[...] = jnp.where((lane < SLOTS) & ~allowed, forbidden, 0.0).astype(bf16)

    q, k, v = q_ref[0], k_ref[0], v_ref[0]
    one = jnp.ones((tokens, PAIR), bf16)

    def operands(head):
        own = choose(head, low)
        return own(q, qmark[...]), own(k, kmark[...]), own(v, one)

    def finish(sums):
        even, odd = sums
        share = 1.0 / jnp.concatenate([even[HEAD_DIM:], odd[:HEAD_DIM]], axis=0)
        out = jnp.concatenate([even[:HEAD_DIM], odd[HEAD_DIM:]], axis=0) * share
        out_ref[...] = out.T.astype(bf16)
        scale_ref[...] = share.T

    bound = score_limit * score_limit
    small = (
        qsq_ref[q_at, 0, 2 * pair] * ksq_ref[k_at, 0, 2 * pair] <= bound
    ) & (qsq_ref[q_at, 0, 2 * pair + 1] * ksq_ref[k_at, 0, 2 * pair + 1] <= bound)

    @pl.when(small)
    def direct():
        sums = []
        for head in range(2):
            queries, keys, values = operands(head)
            if not causal:
                weight = jnp.exp2(contract(keys, queries, 1, 1)).astype(bf16)
                weight_ref[head] = weight
                sums.append(contract(values, weight, 0, 0))
                continue
            step = tokens // 2
            before = lax.broadcasted_iota(jnp.int32, (step, step), 0) <= lax.broadcasted_iota(
                jnp.int32, (step, step), 1
            )
            nothing = jnp.zeros((), bf16)
            top = jnp.exp2(contract(keys[:step], queries, 1, 1)).astype(bf16)
            top = jnp.concatenate(
                [jnp.where(before, top[:, :step], nothing), top[:, step:]], axis=1
            )
            weight_ref[head, :step] = top
            total = contract(values[:step], top, 0, 0)
            low_part = jnp.exp2(contract(keys[step:], queries[step:], 1, 1)).astype(bf16)
            low_part = jnp.where(before, low_part, nothing)
            weight_ref[head, step:, step:] = low_part
            rest = contract(values[step:], low_part, 0, 0)
            sums.append(jnp.concatenate([total[:, :step], total[:, step:] + rest], axis=1))
        finish(sums)

    @pl.when(jnp.logical_not(small))
    def shifted():
        sums = []
        for head in range(2):
            queries, keys, values = operands(head)
            scores = contract(keys, queries, 1, 1)
            if causal:
                before = lax.broadcasted_iota(
                    jnp.int32, scores.shape, 0
                ) <= lax.broadcasted_iota(jnp.int32, scores.shape, 1)
                scores = jnp.where(before, scores, forbidden)
            scores = scores - jnp.max(scores, axis=0, keepdims=True)
            weight = jnp.exp2(scores).astype(bf16)
            weight_ref[head] = weight
            sums.append(contract(values, weight, 0, 0))
        finish(sums)


def attend(bucket, lengths, q_pack, k_pack, v_pack, causal):
    (q, q_squares, q_at), (k, k_squares, k_at), (v, unused, v_at) = q_pack, k_pack, v_pack
    tokens, width = q.shape[1:]
    pairs = width // PAIR
    pair_spec = lambda at: pl.BlockSpec((1, tokens, PAIR), lambda j: (at, 0, j))
    flat_spec = pl.BlockSpec((tokens, PAIR), lambda j: (0, j))
    return pl.pallas_call(
        functools.partial(attend_kernel, causal, q_at, k_at),
        grid=(pairs,),
        in_specs=[smem(), smem(), smem(), smem(), pair_spec(q_at), pair_spec(k_at), pair_spec(v_at)],
        out_specs=[
            flat_spec,
            pl.BlockSpec((2, tokens, tokens), lambda j: (j, 0, 0)),
            flat_spec,
        ],
        out_shape=[
            jax.ShapeDtypeStruct((tokens, width), bf16),
            jax.ShapeDtypeStruct((2 * pairs, tokens, tokens), bf16),
            jax.ShapeDtypeStruct((tokens, width), f32),
        ],
        scratch_shapes=[pltpu.VMEM((tokens, PAIR), bf16), pltpu.VMEM((tokens, PAIR), bf16)],
        compiler_params=params,
        cost_estimate=cost(20e-6 * 1e15, 4 * pairs * tokens * tokens),
        name="attend",
    )(bucket, lengths, q_squares, k_squares, q, k, v)


def attend_back_kernel(
    causal, q_ref, k_ref, v_ref, grad_ref, out_ref, weight_ref, dq_ref, dk_ref, dv_ref
):
    tokens = q_ref.shape[-2]
    low = low_half(tokens)
    q, k, v, grad = q_ref[0], k_ref[0], v_ref[0], grad_ref[...]
    nothing = jnp.zeros((tokens, PAIR), bf16)
    minus = jnp.full((tokens, PAIR), -1.0, bf16)
    swap = (
        (lax.broadcasted_iota(jnp.int32, (PAIR, PAIR), 0) < HEAD_DIM)
        != (lax.broadcasted_iota(jnp.int32, (PAIR, PAIR), 1) < HEAD_DIM)
    ).astype(bf16)
    product = grad.astype(f32) * out_ref[...].astype(f32)
    high = product.astype(bf16)
    centre = contract(high, swap, 1, 0) + contract((product - high.astype(f32)).astype(bf16), swap, 1, 0)
    high = centre.astype(bf16)
    rest = (centre - high.astype(f32)).astype(bf16)
    lane = lax.broadcasted_iota(jnp.int32, (tokens, PAIR), 1) & (HEAD_DIM - 1)
    centre = jnp.where(lane == 0, high, jnp.where(lane == 1, rest, nothing))

    step = tokens // 2 if causal else tokens
    dq_turned = None
    for tile in range(tokens // step):
        at = tile * step
        rows = slice(at, at + step)
        dk = dv = None
        turned = []
        for head in range(2):
            own = choose(head, low)
            weight = weight_ref[head, rows, at:]
            dweight = contract(own(v, minus)[rows], own(grad, centre)[at:], 1, 1)
            dscore = weight * dweight.astype(bf16)
            dv_own = contract(weight, own(grad, nothing)[at:], 1, 0)
            dk_own = contract(dscore, own(q, nothing)[at:], 1, 0)
            dv = dv_own if head == 0 else dv + dv_own
            dk = dk_own if head == 0 else dk + dk_own
            turned.append(contract(k[rows], dscore, 0, 0)[head * HEAD_DIM : (head + 1) * HEAD_DIM])
        dv_ref[rows] = dv.astype(bf16)
        dk_ref[rows] = (dk * math.log(2.0)).astype(bf16)
        turned = jnp.concatenate(turned, axis=0)
        if tile == 0:
            dq_turned = turned
        else:
            dq_turned = jnp.concatenate([dq_turned[:, :at], dq_turned[:, at:] + turned], axis=1)
    dq_ref[...] = (dq_turned * HEAD_DIM ** (-0.5)).T.astype(bf16)


def attend_back(q_pack, k_pack, v_pack, grad, out, weight, causal):
    (q, unused, q_at), (k, unused, k_at), (v, unused, v_at) = q_pack, k_pack, v_pack
    tokens, width = q.shape[1:]
    pairs = width // PAIR
    pair_spec = lambda at: pl.BlockSpec((1, tokens, PAIR), lambda j: (at, 0, j))
    flat_spec = pl.BlockSpec((tokens, PAIR), lambda j: (0, j))
    return pl.pallas_call(
        functools.partial(attend_back_kernel, causal),
        grid=(pairs,),
        in_specs=[
            pair_spec(q_at),
            pair_spec(k_at),
            pair_spec(v_at),
            flat_spec,
            flat_spec,
            pl.BlockSpec((2, tokens, tokens), lambda j: (j, 0, 0)),
        ],
        out_specs=[flat_spec] * 3,
        out_shape=[jax.ShapeDtypeStruct((tokens, width), bf16)] * 3,
        compiler_params=params,
        cost_estimate=cost(35e-6 * 1e15, 4 * pairs * tokens * tokens),
        name="attend_back",
    )(q, k, v, grad, out, weight)


def first_kernel(x_ref, out_ref, gains_ref, wo_ref, wq_ref, first_ref, inverse_ref, q_ref, square_ref):
    z = x_ref[...].astype(f32) + contract(out_ref[...], whole(wo_ref), 1, 0)
    normal, inverse = normalise(z)
    first = normal * gains_ref[0:1]
    first_ref[...] = first
    inverse_ref[...] = jnp.broadcast_to(inverse, inverse_ref.shape)
    q = (contract(first.astype(bf16), whole(wq_ref), 1, 0) * query_scale).astype(bf16)
    q_ref[0] = q
    squares = jnp.broadcast_to(head_squares(q), square_ref.shape[1:])

    @pl.when(pl.program_id(0) == 0)
    def begin():
        square_ref[0] = squares

    @pl.when(pl.program_id(0) > 0)
    def more():
        square_ref[0] = jnp.maximum(square_ref[0], squares)


def after_self(x, out, gains, weights, output_at, query_at):
    tokens, width = x.shape
    rows = tokens // 4
    tile = pl.BlockSpec((rows, width), lambda i: (i, 0))
    return pl.pallas_call(
        first_kernel,
        grid=(tokens // rows,),
        in_specs=[
            tile,
            tile,
            pl.BlockSpec(gains.shape, lambda i: (0, 0)),
            weight_spec(weights, 1, output_at, 1),
            weight_spec(weights, 1, query_at, 1),
        ],
        out_specs=[
            tile,
            pl.BlockSpec((rows, PAIR), lambda i: (i, 0)),
            pl.BlockSpec((1, rows, width), lambda i: (0, i, 0)),
            pl.BlockSpec((1, 8, PAIR), lambda i: (0, 0, 0)),
        ],
        out_shape=[
            jax.ShapeDtypeStruct((tokens, width), f32),
            jax.ShapeDtypeStruct((tokens, PAIR), f32),
            jax.ShapeDtypeStruct((1, tokens, width), bf16),
            jax.ShapeDtypeStruct((1, 8, PAIR), f32),
        ],
        compiler_params=params,
        cost_estimate=cost(4 * tokens * width * width, 14 * tokens * width),
        name="after_self",
    )(x, out, gains, weights, weights)


def feed_kernel(
    bucket_ref, lengths_ref, first_ref, out_ref, share_ref, cotangent_ref, gains_ref, down_ref, up_ref,
    wo_ref, w1_ref, w2_ref,
    outputs_ref, grad_ref, grad_out_ref, down_grad_ref, up_grad_ref,
    down_low, up_low, slope_scratch,
):
    rows, width = first_ref.shape
    tokens = rows * pl.num_programs(0)
    step = pl.program_id(0)

    @pl.when(step == 0)
    def begin():
        down_low[...] = down_ref[...].astype(bf16)
        up_low[...] = up_ref[...].astype(bf16)
        down_grad_ref[...] = jnp.zeros_like(down_grad_ref)
        up_grad_ref[...] = jnp.zeros_like(up_grad_ref)

    chunks = w1_ref.shape[1]
    wo = whole(wo_ref)
    z = first_ref[...] + contract(out_ref[...], wo, 1, 0)
    second_normal, second_inverse = normalise(z)
    second = second_normal * gains_ref[1:2]
    second_low = second.astype(bf16)

    adapter_act, adapter_slope = gelu_and_slope(contract(second_low, down_low[...], 1, 0))
    adapter_act = adapter_act.astype(bf16)
    total = second + 4.0 * contract(adapter_act, up_low[...], 1, 0)
    for i in range(chunks):
        active, slope = gelu_and_slope(contract(second_low, part(w1_ref, i), 1, 0))
        slope_scratch[i] = slope.astype(bf16)
        total += contract(active.astype(bf16), quarter(w2_ref, i), 1, 0)

    third_normal, third_inverse = normalise(total)
    outputs_ref[...] = (third_normal * gains_ref[2:3]).astype(bf16)

    shift = item_shift(bucket_ref[0], 1024)
    row = lax.broadcasted_iota(jnp.int32, (rows, 1), 0) + step * rows
    item = row >> shift
    valid = row - (item << shift) < item_length(item, lengths_ref)
    upstream = jnp.where(valid, cotangent_ref[...].astype(f32), 0.0)
    grad_third = normalise_back(upstream * gains_ref[2:3], third_normal, third_inverse)

    grad_adapter_out = (4.0 * grad_third).astype(bf16)
    grad_feed = grad_third.astype(bf16)
    up_grad_ref[...] += contract(adapter_act, grad_adapter_out, 0, 0)
    grad_adapter_pre = (contract(grad_adapter_out, up_low[...], 1, 1) * adapter_slope).astype(bf16)
    down_grad_ref[...] += contract(second_low, grad_adapter_pre, 0, 0)
    grad_second = grad_third + contract(grad_adapter_pre, down_low[...], 1, 1)
    for i in range(chunks):
        grad_inner = contract(grad_feed, quarter(w2_ref, i), 1, 1)
        grad_inner = (grad_inner * slope_scratch[i].astype(f32)).astype(bf16)
        grad_second += contract(grad_inner, part(w1_ref, i), 1, 1)

    grad_pre = normalise_back(grad_second * gains_ref[1:2], second_normal, second_inverse)
    grad_ref[...] = grad_pre
    grad_out_ref[...] = (contract(grad_pre.astype(bf16), wo, 1, 1) * share_ref[...]).astype(bf16)


def feed(bucket, lengths, first, out, share, cotangent, gains, down, up, weights, output_at):
    tokens, width = first.shape
    rows = tokens // 4
    tile = pl.BlockSpec((rows, width), lambda i: (i, 0))
    fixed = lambda a: pl.BlockSpec(a.shape, lambda i: (0,) * a.ndim, pipeline_mode=pl.Buffered(1))
    return pl.pallas_call(
        feed_kernel,
        grid=(tokens // rows,),
        in_specs=[
            smem(),
            smem(),
            tile,
            tile,
            tile,
            tile,
            fixed(gains),
            fixed(down),
            fixed(up),
            weight_spec(weights, 1, output_at, 1),
            weight_spec(weights, 4, 0, 1),
            weight_spec(weights, 4, 1, 1),
        ],
        out_specs=[tile, tile, tile, fixed(down), fixed(up)],
        out_shape=[
            jax.ShapeDtypeStruct((tokens, width), bf16),
            jax.ShapeDtypeStruct((tokens, width), f32),
            jax.ShapeDtypeStruct((tokens, width), bf16),
            jax.ShapeDtypeStruct(down.shape, f32),
            jax.ShapeDtypeStruct(up.shape, f32),
        ],
        scratch_shapes=[
            pltpu.VMEM(down.shape, bf16),
            pltpu.VMEM(up.shape, bf16),
            pltpu.VMEM((4, rows, width), bf16),
        ],
        compiler_params=params,
        cost_estimate=cost(45e9, 40 * tokens * width),
        name="feed",
    )(bucket, lengths, first, out, share, cotangent, gains, down, up, weights, weights, weights)


def cross_back_kernel(
    dq_ref, dk_ref, dv_ref, grad_ref, first_ref, inverse_ref, share_ref, gains_ref,
    wq_ref, wk_ref, wv_ref, wo_ref, encoder_ref, pre_ref, grad_out_ref,
):
    grad_first = grad_ref[...] + contract(dq_ref[...], whole(wq_ref), 1, 1)
    gain = gains_ref[0:1]
    grad_pre = normalise_back(grad_first * gain, first_ref[...] / gain, inverse_ref[:, 0:1])
    pre_ref[...] = grad_pre
    grad_out_ref[...] = (contract(grad_pre.astype(bf16), whole(wo_ref), 1, 1) * share_ref[...]).astype(bf16)
    encoder_ref[...] = (
        contract(dk_ref[...], whole(wk_ref), 1, 1) + contract(dv_ref[...], whole(wv_ref), 1, 1)
    ).astype(bf16)


def after_cross_back(dq, dk, dv, grad, first, inverse, share, gains, weights, at):
    tokens, width = first.shape
    rows = tokens // 2
    tile = pl.BlockSpec((rows, width), lambda i: (i, 0))
    return pl.pallas_call(
        cross_back_kernel,
        grid=(tokens // rows,),
        in_specs=[tile] * 5
        + [pl.BlockSpec((rows, PAIR), lambda i: (i, 0)), tile, pl.BlockSpec(gains.shape, lambda i: (0, 0))]
        + [weight_spec(weights, 1, i, 1) for i in at],
        out_specs=[tile] * 3,
        out_shape=[
            jax.ShapeDtypeStruct((tokens, width), bf16),
            jax.ShapeDtypeStruct((tokens, width), f32),
            jax.ShapeDtypeStruct((tokens, width), bf16),
        ],
        compiler_params=params,
        cost_estimate=cost(8 * tokens * width * width, 24 * tokens * width),
        name="after_cross_back",
    )(dq, dk, dv, grad, first, inverse, share, gains, *([weights] * 4))


def input_kernel(dq_ref, dk_ref, dv_ref, pre_ref, wq_ref, wk_ref, wv_ref, out_ref):
    out_ref[...] = (
        pre_ref[...]
        + contract(dq_ref[...], whole(wq_ref), 1, 1)
        + contract(dk_ref[...], whole(wk_ref), 1, 1)
        + contract(dv_ref[...], whole(wv_ref), 1, 1)
    ).astype(bf16)


def input_gradient(dq, dk, dv, pre, weights, at):
    tokens, width = pre.shape
    rows = tokens // 4
    tile = pl.BlockSpec((rows, width), lambda i: (i, 0))
    return pl.pallas_call(
        input_kernel,
        grid=(tokens // rows,),
        in_specs=[tile] * 4 + [weight_spec(weights, 1, i, 1) for i in at],
        out_specs=tile,
        out_shape=jax.ShapeDtypeStruct((tokens, width), bf16),
        compiler_params=params,
        cost_estimate=cost(6 * tokens * width * width, 18 * tokens * width),
        name="input_gradient",
    )(dq, dk, dv, pre, *([weights] * 3))


def adamw(master, first_moment, second_moment, gradient):
    first_new = beta_first * first_moment + (1.0 - beta_first) * gradient
    second_new = beta_second * second_moment + (1.0 - beta_second) * gradient * gradient
    first_hat = first_new / (1.0 - beta_first**STEP)
    second_hat = second_new / (1.0 - beta_second**STEP)
    master_new = master - learn_rate * (
        first_hat / (jnp.sqrt(second_hat) + epsilon_adam) + weight_decay * master
    )
    return (first_new, second_new, master_new)


def gather(shards, feeds):
    axes = ("fsdp", "dp")
    parts, part_at = lax.axis_size("dp"), lax.axis_index("dp")

    def own(shard):
        rows = shard.shape[0] // parts
        return lax.dynamic_slice_in_dim(shard, part_at * rows, rows, 0)

    width = shards[0].shape[1]
    pieces = []
    if feeds:
        up, down = own(feeds[0]), own(feeds[1])
        rows = up.shape[0]
        pieces.append(jnp.transpose(up.reshape(rows, -1, width), (1, 0, 2)))
        pieces.append(down.reshape(-1, rows, width))
    pieces.append(jnp.stack([own(shard) for shard in shards]))
    stacked = jnp.concatenate(pieces, axis=0)
    count, rows = stacked.shape[:2]
    gathered = lax.all_gather(stacked, axes, axis=0)
    if rows % 16 == 0:
        return gathered
    square = jnp.transpose(gathered, (1, 0, 2, 3)).reshape(1, count, -1, width)
    if feeds:
        blocks = count - len(shards) - pieces[0].shape[0]
        start = pieces[0].shape[0]
        tall = gathered[:, start : start + blocks].reshape(1, blocks, -1, width)
        square = jnp.concatenate([square[:, :start], tall, square[:, start + blocks :]], axis=1)
    return square


def body(
    inputs, encoder, cotangent, buckets, lengths, self_query, self_key, self_value, self_output,
    cross_query, cross_key, cross_value, cross_output, fc_first, fc_second, norm_gains,
    down_master, up_master, down_first, down_second, up_first, up_second,
):
    early = gather((self_query, self_key, self_value), ())
    late = gather(
        (self_output, cross_query, cross_key, cross_value, cross_output), (fc_first, fc_second)
    )
    so, cq, ck, cv, co = range(8, 13)

    qkv, squares = project(inputs, early, 3, 0, query_scale)
    self_packs = [(qkv, squares, 0), (qkv, squares, 1), (qkv, None, 2)]
    self_out, self_weight, self_share = attend(buckets, lengths, *self_packs, True)

    kv, kv_squares = project(encoder, late, 2, ck, 1.0)
    first, first_inverse, query_cross, query_squares = after_self(
        inputs, self_out, norm_gains, late, so, cq
    )
    cross_packs = [(query_cross, query_squares, 0), (kv, kv_squares, 0), (kv, None, 1)]
    cross_out, cross_weight, cross_share = attend(buckets, lengths, *cross_packs, False)

    outputs, grad_cross_pre, grad_cross_out, down_local, up_local = feed(
        buckets, lengths, first, cross_out, cross_share, cotangent, norm_gains, down_master, up_master, late, co
    )
    down_grad, up_grad = lax.psum((down_local, up_local), ("fsdp", "dp"))

    dq, dk, dv = attend_back(*cross_packs, grad_cross_out, cross_out, cross_weight, False)
    encoder_grad, grad_self_pre, grad_self_out = after_cross_back(
        dq, dk, dv, grad_cross_pre, first, first_inverse, self_share, norm_gains, late, (cq, ck, cv, so)
    )
    dq, dk, dv = attend_back(*self_packs, grad_self_out, self_out, self_weight, True)
    input_grad = input_gradient(dq, dk, dv, grad_self_pre, early, (0, 1, 2))

    down_first_new, down_second_new, down_master_new = adamw(
        down_master, down_first, down_second, down_grad
    )
    up_first_new, up_second_new, up_master_new = adamw(up_master, up_first, up_second, up_grad)
    return (
        outputs,
        input_grad,
        encoder_grad,
        down_grad,
        up_grad,
        down_first_new,
        down_second_new,
        up_first_new,
        up_second_new,
        down_master_new,
        up_master_new,
        down_master_new.astype(bf16),
        up_master_new.astype(bf16),
    )


def solution(mesh):
    tokens, matrix = P(("fsdp", "dp"), None), P("fsdp", None)
    return jax.shard_map(
        body,
        mesh=mesh,
        in_specs=(tokens, tokens, tokens, P(("fsdp", "dp")), tokens) + (matrix,) * 10 + (P(),) * 7,
        out_specs=(tokens,) * 3 + (P(),) * 10,
        check_vma=False,
    )
```

```python
import functools
import math

import jax
import jax.numpy as jnp
from jax import lax
from jax.experimental import pallas as pl
from jax.experimental.pallas import tpu as pltpu
from jax.sharding import PartitionSpec as P

HEAD_DIM = 64
PAIR = 2 * HEAD_DIM
STEP = 10
SLOTS = 4

epsilon_norm = 1e-05
beta_first = 0.9
beta_second = 0.999
learn_rate = 0.05
weight_decay = 0.01
epsilon_adam = 1e-08

f32, bf16 = jnp.float32, jnp.bfloat16
query_scale = HEAD_DIM ** (-0.5) * math.log2(math.e)
forbidden = -(2.0**100)
score_limit = 64.0

params = pltpu.CompilerParams(vmem_limit_bytes=58 * 2**20)


def contract(left, right, left_dim, right_dim):
    return lax.dot_general(
        left, right, (((left_dim,), (right_dim,)), ((), ())), preferred_element_type=f32
    )


def start_loading(pieces, table_ref, wanted, store, sems):
    for slot, i in enumerate(wanted):
        for p, piece in enumerate(pieces):
            rows = piece.shape[1]
            at = pl.multiple_of(table_ref[0, p], 16)
            pltpu.make_async_copy(
                piece.at[i], store.at[slot, pl.ds(at, rows)], sems.at[slot]
            ).start()


def loaded(store, sems, slot):
    pltpu.make_async_copy(store.at[slot], store.at[slot], sems.at[slot]).wait()


def cost(microseconds):
    return pl.CostEstimate(flops=int(microseconds * 1.15e9), bytes_accessed=10**5, transcendentals=0)


def in_place():
    return pl.BlockSpec(memory_space=pl.ANY)


def stores(count, width):
    return [pltpu.VMEM((count, width, width), bf16), pltpu.SemaphoreType.DMA((count,))]


smem = functools.partial(pl.BlockSpec, memory_space=pltpu.SMEM)


def normalise(values):
    centre = values - jnp.mean(values, axis=-1, keepdims=True)
    inverse = lax.rsqrt(jnp.mean(centre * centre, axis=-1, keepdims=True) + epsilon_norm)
    return centre * inverse, inverse


def normalise_back(scaled, normal, inverse):
    return inverse * (
        scaled
        - jnp.mean(scaled, axis=-1, keepdims=True)
        - normal * jnp.mean(scaled * normal, axis=-1, keepdims=True)
    )


def gelu_and_slope(u):
    bell = jnp.exp2(u * u * (-0.5 * math.log2(math.e)))
    t = 1.0 / (1.0 + (0.3275911 * math.sqrt(0.5)) * jnp.abs(u))
    tail = t * (
        0.5 * 0.254829592
        + t
        * (
            0.5 * -0.284496736
            + t * (0.5 * 1.421413741 + t * (0.5 * -1.453152027 + t * (0.5 * 1.061405429)))
        )
    )
    tail = tail * bell
    below = jnp.where(u > 0, 1.0 - tail, tail)
    return u * below, below + u * bell * (1.0 / math.sqrt(2.0 * math.pi))


def head_squares(values):
    width = values.shape[1]
    member = (
        lax.broadcasted_iota(jnp.int32, (width, PAIR), 0) >> 6
        == lax.broadcasted_iota(jnp.int32, (width, PAIR), 1)
    ).astype(bf16)
    return jnp.max(contract(values * values, member, 1, 0), axis=0, keepdims=True)


def project_kernel(scale, squared, wanted, table_ref, x_ref, *refs):
    *pieces, out_ref, square_ref, store, sems = refs
    step = pl.program_id(0)

    @pl.when(step == 0)
    def begin():
        start_loading(pieces, table_ref, wanted, store, sems)

    loaded(store, sems, step)
    out = contract(x_ref[...], store[step], 1, 0)
    if scale != 1.0:
        out = out * jnp.where(step == 0, scale, 1.0)
    out = out.astype(bf16)
    out_ref[0] = out

    @pl.when(step < squared)
    def squares():
        square_ref[0] = jnp.broadcast_to(head_squares(out), square_ref.shape[1:])

    @pl.when(step >= squared)
    def no_squares():
        square_ref[0] = jnp.zeros(square_ref.shape[1:], f32)


def project(x, table, pieces, wanted, scale, squared):
    tokens, width = x.shape
    count = len(wanted)
    return pl.pallas_call(
        functools.partial(project_kernel, scale, squared, wanted),
        grid=(count,),
        in_specs=[smem(), pl.BlockSpec((tokens, width), lambda i: (0, 0))]
        + [in_place() for piece in pieces],
        out_specs=[
            pl.BlockSpec((1, tokens, width), lambda i: (i, 0, 0)),
            pl.BlockSpec((1, 8, PAIR), lambda i: (i, 0, 0)),
        ],
        out_shape=[
            jax.ShapeDtypeStruct((count, tokens, width), bf16),
            jax.ShapeDtypeStruct((count, 8, PAIR), f32),
        ],
        scratch_shapes=stores(count, width),
        compiler_params=params,
        cost_estimate=cost(0.1 * count),
        name="project",
    )(table, x, *pieces)


def low_half(rows):
    return lax.broadcasted_iota(jnp.int32, (rows, PAIR), 1) < HEAD_DIM


def choose(head, low):
    if head == 0:
        return lambda own, other: jnp.where(low, own, other)
    return lambda own, other: jnp.where(low, other, own)


def item_shift(bucket, tokens):
    return bucket + (tokens.bit_length() - 1 - 2)


def item_length(item, lengths_ref):
    length = jnp.zeros_like(item)
    for slot in range(SLOTS):
        length = jnp.where(item == slot, lengths_ref[0, slot], length)
    return length


def attend_kernel(
    causal, q_at, k_at, start, bucket_ref, lengths_ref, qsq_ref, ksq_ref, q_ref, k_ref, v_ref, *refs
):
    out_ref, weight_ref, scale_ref, done_ref, qmark, kmark = refs[-6:]
    done_ref[...] = jnp.zeros_like(done_ref)
    tokens = q_ref.shape[-2]
    low = low_half(tokens)
    pair = pl.program_id(0) + start

    @pl.when(pl.program_id(0) == 0)
    def marks():
        shift = item_shift(bucket_ref[0], tokens)
        lane = lax.broadcasted_iota(jnp.int32, (tokens, PAIR), 1) & (HEAD_DIM - 1)
        row = lax.broadcasted_iota(jnp.int32, (tokens, PAIR), 0)
        item = row >> shift
        own = lane == item
        qmark[...] = jnp.where(own, 1.0, 0.0).astype(bf16)
        allowed = own & (row - (item << shift) < item_length(item, lengths_ref))
        kmark[...] = jnp.where((lane < SLOTS) & ~allowed, forbidden, 0.0).astype(bf16)

    q, k, v = q_ref[0], k_ref[0], v_ref[0]
    one = jnp.ones((tokens, PAIR), bf16)

    def operands(head):
        own = choose(head, low)
        return own(q, qmark[...]), own(k, kmark[...]), own(v, one)

    def finish(sums):
        even, odd = sums
        share = 1.0 / jnp.concatenate([even[HEAD_DIM:], odd[:HEAD_DIM]], axis=0)
        out = jnp.concatenate([even[:HEAD_DIM], odd[HEAD_DIM:]], axis=0) * share
        out_ref[...] = out.T.astype(bf16)
        scale_ref[...] = share.T

    bound = score_limit * score_limit
    small = (
        qsq_ref[q_at, 0, 2 * pair] * ksq_ref[k_at, 0, 2 * pair] <= bound
    ) & (qsq_ref[q_at, 0, 2 * pair + 1] * ksq_ref[k_at, 0, 2 * pair + 1] <= bound)

    @pl.when(small)
    def direct():
        sums = []
        for head in range(2):
            queries, keys, values = operands(head)
            if not causal:
                weight = jnp.exp2(contract(keys, queries, 1, 1)).astype(bf16)
                weight_ref[head] = weight
                sums.append(contract(values, weight, 0, 0))
                continue
            step = tokens // 2
            before = lax.broadcasted_iota(jnp.int32, (step, step), 0) <= lax.broadcasted_iota(
                jnp.int32, (step, step), 1
            )
            nothing = jnp.zeros((), bf16)
            top = jnp.exp2(contract(keys[:step], queries, 1, 1)).astype(bf16)
            top = jnp.concatenate(
                [jnp.where(before, top[:, :step], nothing), top[:, step:]], axis=1
            )
            weight_ref[head, :step] = top
            total = contract(values[:step], top, 0, 0)
            low_part = jnp.exp2(contract(keys[step:], queries[step:], 1, 1)).astype(bf16)
            low_part = jnp.where(before, low_part, nothing)
            weight_ref[head, step:, step:] = low_part
            rest = contract(values[step:], low_part, 0, 0)
            sums.append(jnp.concatenate([total[:, :step], total[:, step:] + rest], axis=1))
        finish(sums)

    @pl.when(jnp.logical_not(small))
    def shifted():
        sums = []
        for head in range(2):
            queries, keys, values = operands(head)
            scores = contract(keys, queries, 1, 1)
            if causal:
                before = lax.broadcasted_iota(
                    jnp.int32, scores.shape, 0
                ) <= lax.broadcasted_iota(jnp.int32, scores.shape, 1)
                scores = jnp.where(before, scores, forbidden)
            scores = scores - jnp.max(scores, axis=0, keepdims=True)
            weight = jnp.exp2(scores).astype(bf16)
            weight_ref[head] = weight
            sums.append(contract(values, weight, 0, 0))
        finish(sums)


def attend(bucket, lengths, q_pack, k_pack, v_pack, causal, start, stop, so_far=(), sooner=()):
    (q, q_squares, q_at), (k, k_squares, k_at), (v, unused, v_at) = q_pack, k_pack, v_pack
    tokens, width = q.shape[1:]
    pairs = width // PAIR
    pair_spec = lambda at: pl.BlockSpec((1, tokens, PAIR), lambda j: (at, 0, start + j))
    flat_spec = pl.BlockSpec((tokens, PAIR), lambda j: (0, start + j))
    return pl.pallas_call(
        functools.partial(attend_kernel, causal, q_at, k_at, start),
        grid=(stop - start,),
        in_specs=[smem(), smem(), smem(), smem(), pair_spec(q_at), pair_spec(k_at), pair_spec(v_at)]
        + [in_place() for array in (*so_far, *sooner)],
        out_specs=[
            flat_spec,
            pl.BlockSpec((2, tokens, tokens), lambda j: (start + j, 0, 0)),
            flat_spec,
            pl.BlockSpec((8, PAIR), lambda j: (0, 0)),
        ],
        out_shape=[
            jax.ShapeDtypeStruct((tokens, width), bf16),
            jax.ShapeDtypeStruct((2 * pairs, tokens, tokens), bf16),
            jax.ShapeDtypeStruct((tokens, width), f32),
            jax.ShapeDtypeStruct((8, PAIR), f32),
        ],
        input_output_aliases={7 + i: i for i in range(len(so_far))},
        scratch_shapes=[pltpu.VMEM((tokens, PAIR), bf16), pltpu.VMEM((tokens, PAIR), bf16)],
        compiler_params=params,
        cost_estimate=cost(0.05 * (stop - start)),
        name="attend",
    )(bucket, lengths, q_squares, k_squares, q, k, v, *so_far, *sooner)


def attend_back_kernel(
    causal, q_ref, k_ref, v_ref, grad_ref, out_ref, weight_ref, dq_ref, dk_ref, dv_ref
):
    tokens = q_ref.shape[-2]
    low = low_half(tokens)
    q, k, v, grad = q_ref[0], k_ref[0], v_ref[0], grad_ref[...]
    nothing = jnp.zeros((tokens, PAIR), bf16)
    minus = jnp.full((tokens, PAIR), -1.0, bf16)
    swap = (
        (lax.broadcasted_iota(jnp.int32, (PAIR, PAIR), 0) < HEAD_DIM)
        != (lax.broadcasted_iota(jnp.int32, (PAIR, PAIR), 1) < HEAD_DIM)
    ).astype(bf16)
    product = grad.astype(f32) * out_ref[...].astype(f32)
    high = product.astype(bf16)
    centre = contract(high, swap, 1, 0) + contract((product - high.astype(f32)).astype(bf16), swap, 1, 0)
    high = centre.astype(bf16)
    rest = (centre - high.astype(f32)).astype(bf16)
    lane = lax.broadcasted_iota(jnp.int32, (tokens, PAIR), 1) & (HEAD_DIM - 1)
    centre = jnp.where(lane == 0, high, jnp.where(lane == 1, rest, nothing))

    step = tokens // 2 if causal else tokens
    dq_turned = None
    for tile in range(tokens // step):
        at = tile * step
        rows = slice(at, at + step)
        dk = dv = None
        turned = []
        for head in range(2):
            own = choose(head, low)
            weight = weight_ref[head, rows, at:]
            dweight = contract(own(v, minus)[rows], own(grad, centre)[at:], 1, 1)
            dscore = weight * dweight.astype(bf16)
            dv_own = contract(weight, own(grad, nothing)[at:], 1, 0)
            dk_own = contract(dscore, own(q, nothing)[at:], 1, 0)
            dv = dv_own if head == 0 else dv + dv_own
            dk = dk_own if head == 0 else dk + dk_own
            turned.append(contract(k[rows], dscore, 0, 0)[head * HEAD_DIM : (head + 1) * HEAD_DIM])
        dv_ref[rows] = dv.astype(bf16)
        dk_ref[rows] = (dk * math.log(2.0)).astype(bf16)
        turned = jnp.concatenate(turned, axis=0)
        if tile == 0:
            dq_turned = turned
        else:
            dq_turned = jnp.concatenate([dq_turned[:, :at], dq_turned[:, at:] + turned], axis=1)
    dq_ref[...] = (dq_turned * HEAD_DIM ** (-0.5)).T.astype(bf16)


def attend_back(q_pack, k_pack, v_pack, grad, out, weight, causal):
    (q, unused, q_at), (k, unused, k_at), (v, unused, v_at) = q_pack, k_pack, v_pack
    tokens, width = q.shape[1:]
    pairs = width // PAIR
    pair_spec = lambda at: pl.BlockSpec((1, tokens, PAIR), lambda j: (at, 0, j))
    flat_spec = pl.BlockSpec((tokens, PAIR), lambda j: (0, j))
    return pl.pallas_call(
        functools.partial(attend_back_kernel, causal),
        grid=(pairs,),
        in_specs=[
            pair_spec(q_at),
            pair_spec(k_at),
            pair_spec(v_at),
            flat_spec,
            flat_spec,
            pl.BlockSpec((2, tokens, tokens), lambda j: (j, 0, 0)),
        ],
        out_specs=[flat_spec] * 3,
        out_shape=[jax.ShapeDtypeStruct((tokens, width), bf16)] * 3,
        compiler_params=params,
        cost_estimate=cost(35),
        name="attend_back",
    )(q, k, v, grad, out, weight)


def first_kernel(wanted, count, table_ref, x_ref, out_ref, gains_ref, *refs):
    pieces = refs[:count]
    first_ref, inverse_ref, q_ref, square_ref, store, sems = refs[-6:]
    step = pl.program_id(0)

    @pl.when(step == 0)
    def load():
        start_loading(pieces, table_ref, wanted, store, sems)
        for slot in range(len(wanted)):
            loaded(store, sems, slot)

    z = x_ref[...].astype(f32) + contract(out_ref[...], store[0], 1, 0)
    normal, inverse = normalise(z)
    first = normal * gains_ref[0:1]
    first_ref[...] = first
    inverse_ref[...] = jnp.broadcast_to(inverse, inverse_ref.shape)
    q = (contract(first.astype(bf16), store[1], 1, 0) * query_scale).astype(bf16)
    q_ref[0] = q
    squares = jnp.broadcast_to(head_squares(q), square_ref.shape[1:])

    @pl.when(step == 0)
    def begin():
        square_ref[0] = squares

    @pl.when(step > 0)
    def more():
        square_ref[0] = jnp.maximum(square_ref[0], squares)


def after_self(x, out, gains, table, pieces, wanted, sooner):
    tokens, width = x.shape
    rows = tokens // 4
    tile = pl.BlockSpec((rows, width), lambda i: (i, 0))
    return pl.pallas_call(
        functools.partial(first_kernel, wanted, len(pieces)),
        grid=(tokens // rows,),
        in_specs=[smem(), tile, tile, pl.BlockSpec(gains.shape, lambda i: (0, 0))]
        + [in_place() for piece in (*pieces, *sooner)],
        out_specs=[
            tile,
            pl.BlockSpec((rows, PAIR), lambda i: (i, 0)),
            pl.BlockSpec((1, rows, width), lambda i: (0, i, 0)),
            pl.BlockSpec((1, 8, PAIR), lambda i: (0, 0, 0)),
        ],
        out_shape=[
            jax.ShapeDtypeStruct((tokens, width), f32),
            jax.ShapeDtypeStruct((tokens, PAIR), f32),
            jax.ShapeDtypeStruct((1, tokens, width), bf16),
            jax.ShapeDtypeStruct((1, 8, PAIR), f32),
        ],
        scratch_shapes=stores(len(wanted), width),
        compiler_params=params,
        cost_estimate=cost(0.2),
        name="after_self",
    )(table, x, out, gains, *pieces, *sooner)


def feed_kernel(
    output_at, counts, bucket_ref, lengths_ref, table_ref, first_ref, out_ref, share_ref,
    cotangent_ref, gains_ref, down_ref, up_ref, *refs,
):
    pieces, feed_pieces = refs[:counts], refs[counts : 2 * counts]
    (outputs_ref, grad_ref, grad_out_ref, down_grad_ref, up_grad_ref, down_low, up_low, slope_scratch,
     store, sems, feed_store, feed_sems) = refs[2 * counts :]
    rows, width = first_ref.shape
    tokens = rows * pl.num_programs(0)
    step = pl.program_id(0)
    chunks = slope_scratch.shape[0]

    @pl.when(step == 0)
    def begin():
        start_loading(pieces, table_ref, (output_at,), store, sems)
        for p, piece in enumerate(feed_pieces):
            rows_at = pl.ds(pl.multiple_of(table_ref[2, p], 16), piece.shape[1])
            for kind in range(2):
                pltpu.make_async_copy(
                    piece.at[pl.ds(kind * chunks, chunks)],
                    feed_store.at[kind, table_ref[1, p], :, rows_at],
                    feed_sems.at[kind],
                ).start()
        down_low[...] = down_ref[...].astype(bf16)
        up_low[...] = up_ref[...].astype(bf16)
        down_grad_ref[...] = jnp.zeros_like(down_grad_ref)
        up_grad_ref[...] = jnp.zeros_like(up_grad_ref)
        loaded(store, sems, 0)
        for kind in range(2):
            loaded(feed_store, feed_sems, kind)

    wo = store[0]

    def first_block(i):
        return feed_store[0, :, i].reshape(width, width)

    def second_block(i):
        devices = feed_store.shape[1]
        return feed_store[1, i * devices // chunks : (i + 1) * devices // chunks].reshape(width, width)

    z = first_ref[...] + contract(out_ref[...], wo, 1, 0)
    second_normal, second_inverse = normalise(z)
    second = second_normal * gains_ref[1:2]
    second_low = second.astype(bf16)

    adapter_act, adapter_slope = gelu_and_slope(contract(second_low, down_low[...], 1, 0))
    adapter_act = adapter_act.astype(bf16)
    total = second + 4.0 * contract(adapter_act, up_low[...], 1, 0)
    for i in range(chunks):
        active, slope = gelu_and_slope(contract(second_low, first_block(i), 1, 0))
        slope_scratch[i] = slope.astype(bf16)
        total += contract(active.astype(bf16), second_block(i), 1, 0)

    third_normal, third_inverse = normalise(total)
    outputs_ref[...] = (third_normal * gains_ref[2:3]).astype(bf16)

    shift = item_shift(bucket_ref[0], 1024)
    row = lax.broadcasted_iota(jnp.int32, (rows, 1), 0) + step * rows
    item = row >> shift
    valid = row - (item << shift) < item_length(item, lengths_ref)
    upstream = jnp.where(valid, cotangent_ref[...].astype(f32), 0.0)
    grad_third = normalise_back(upstream * gains_ref[2:3], third_normal, third_inverse)

    grad_adapter_out = (4.0 * grad_third).astype(bf16)
    grad_feed = grad_third.astype(bf16)
    up_grad_ref[...] += contract(adapter_act, grad_adapter_out, 0, 0)
    grad_adapter_pre = (contract(grad_adapter_out, up_low[...], 1, 1) * adapter_slope).astype(bf16)
    down_grad_ref[...] += contract(second_low, grad_adapter_pre, 0, 0)
    grad_second = grad_third + contract(grad_adapter_pre, down_low[...], 1, 1)
    for i in range(chunks):
        grad_inner = contract(grad_feed, second_block(i), 1, 1)
        grad_inner = (grad_inner * slope_scratch[i].astype(f32)).astype(bf16)
        grad_second += contract(grad_inner, first_block(i), 1, 1)

    grad_pre = normalise_back(grad_second * gains_ref[1:2], second_normal, second_inverse)
    grad_ref[...] = grad_pre
    grad_out_ref[...] = (contract(grad_pre.astype(bf16), wo, 1, 1) * share_ref[...]).astype(bf16)


def feed(
    bucket, lengths, table, first, out, share, cotangent, gains, down, up, pieces, output_at, feed_pieces
):
    tokens, width = first.shape
    rows = tokens // 4
    chunks, shard_rows = feed_pieces[0].shape[0] // 2, feed_pieces[0].shape[1]
    tile = pl.BlockSpec((rows, width), lambda i: (i, 0))
    fixed = lambda a: pl.BlockSpec(a.shape, lambda i: (0,) * a.ndim, pipeline_mode=pl.Buffered(1))
    return pl.pallas_call(
        functools.partial(feed_kernel, output_at, len(pieces)),
        grid=(tokens // rows,),
        in_specs=[
            smem(),
            smem(),
            smem(),
            tile,
            tile,
            tile,
            tile,
            fixed(gains),
            fixed(down),
            fixed(up),
        ]
        + [in_place() for piece in pieces + feed_pieces],
        out_specs=[tile, tile, tile, fixed(down), fixed(up)],
        out_shape=[
            jax.ShapeDtypeStruct((tokens, width), bf16),
            jax.ShapeDtypeStruct((tokens, width), f32),
            jax.ShapeDtypeStruct((tokens, width), bf16),
            jax.ShapeDtypeStruct(down.shape, f32),
            jax.ShapeDtypeStruct(up.shape, f32),
        ],
        scratch_shapes=[
            pltpu.VMEM(down.shape, bf16),
            pltpu.VMEM(up.shape, bf16),
            pltpu.VMEM((chunks, rows, width), bf16),
            *stores(1, width),
            pltpu.VMEM((2, width // shard_rows, chunks, shard_rows, width), bf16),
            pltpu.SemaphoreType.DMA((2,)),
        ],
        compiler_params=params,
        cost_estimate=cost(70),
        name="feed",
    )(bucket, lengths, table, first, out, share, cotangent, gains, down, up, *pieces, *feed_pieces)


def cross_back_kernel(
    wanted, table_ref, dq_ref, dk_ref, dv_ref, grad_ref, first_ref, inverse_ref, share_ref, gains_ref,
    *refs,
):
    *pieces, encoder_ref, pre_ref, grad_out_ref, store, sems = refs

    @pl.when(pl.program_id(0) == 0)
    def load():
        start_loading(pieces, table_ref, wanted, store, sems)
        for slot in range(len(wanted)):
            loaded(store, sems, slot)

    grad_first = grad_ref[...] + contract(dq_ref[...], store[0], 1, 1)
    gain = gains_ref[0:1]
    grad_pre = normalise_back(grad_first * gain, first_ref[...] / gain, inverse_ref[:, 0:1])
    pre_ref[...] = grad_pre
    grad_out_ref[...] = (contract(grad_pre.astype(bf16), store[1], 1, 1) * share_ref[...]).astype(bf16)
    encoder_ref[...] = (
        contract(dk_ref[...], store[2], 1, 1) + contract(dv_ref[...], store[3], 1, 1)
    ).astype(bf16)


def after_cross_back(dq, dk, dv, grad, first, inverse, share, gains, table, pieces, wanted):
    tokens, width = first.shape
    rows = tokens // 2
    tile = pl.BlockSpec((rows, width), lambda i: (i, 0))
    return pl.pallas_call(
        functools.partial(cross_back_kernel, wanted),
        grid=(tokens // rows,),
        in_specs=[smem()]
        + [tile] * 5
        + [pl.BlockSpec((rows, PAIR), lambda i: (i, 0)), tile, pl.BlockSpec(gains.shape, lambda i: (0, 0))]
        + [in_place() for piece in pieces],
        out_specs=[tile] * 3,
        out_shape=[
            jax.ShapeDtypeStruct((tokens, width), bf16),
            jax.ShapeDtypeStruct((tokens, width), f32),
            jax.ShapeDtypeStruct((tokens, width), bf16),
        ],
        scratch_shapes=stores(len(wanted), width),
        compiler_params=params,
        cost_estimate=cost(18),
        name="after_cross_back",
    )(table, dq, dk, dv, grad, first, inverse, share, gains, *pieces)


def input_kernel(wanted, table_ref, dq_ref, dk_ref, dv_ref, pre_ref, *refs):
    *pieces, out_ref, store, sems = refs

    @pl.when(pl.program_id(0) == 0)
    def load():
        start_loading(pieces, table_ref, wanted, store, sems)
        for slot in range(len(wanted)):
            loaded(store, sems, slot)

    out_ref[...] = (
        pre_ref[...]
        + contract(dq_ref[...], store[0], 1, 1)
        + contract(dk_ref[...], store[1], 1, 1)
        + contract(dv_ref[...], store[2], 1, 1)
    ).astype(bf16)


def input_gradient(dq, dk, dv, pre, table, pieces, wanted):
    tokens, width = pre.shape
    rows = tokens // 4
    tile = pl.BlockSpec((rows, width), lambda i: (i, 0))
    return pl.pallas_call(
        functools.partial(input_kernel, wanted),
        grid=(tokens // rows,),
        in_specs=[smem()] + [tile] * 4 + [in_place() for piece in pieces],
        out_specs=tile,
        out_shape=jax.ShapeDtypeStruct((tokens, width), bf16),
        scratch_shapes=stores(len(wanted), width),
        compiler_params=params,
        cost_estimate=cost(12),
        name="input_gradient",
    )(table, dq, dk, dv, pre, *pieces)


def adamw(master, first_moment, second_moment, gradient):
    first_new = beta_first * first_moment + (1.0 - beta_first) * gradient
    second_new = beta_second * second_moment + (1.0 - beta_second) * gradient * gradient
    first_hat = first_new / (1.0 - beta_first**STEP)
    second_hat = second_new / (1.0 - beta_second**STEP)
    master_new = master - learn_rate * (
        first_hat / (jnp.sqrt(second_hat) + epsilon_adam) + weight_decay * master
    )
    return (first_new, second_new, master_new)


def pack_kernel(*refs):
    *shards, out_ref = refs
    for i, shard in enumerate(shards):
        out_ref[i] = shard[...]


def pack(shards):
    return pl.pallas_call(
        pack_kernel,
        out_shape=jax.ShapeDtypeStruct((len(shards),) + shards[0].shape, bf16),
        compiler_params=params,
        cost_estimate=cost(2),
        name="pack",
    )(*shards)


def pack_feed_kernel(first_ref, second_ref, out_ref):
    blocks, rows, width = out_ref.shape
    blocks //= 2
    for i in range(blocks):
        out_ref[i] = first_ref[:, i * width : (i + 1) * width]
        out_ref[blocks + i] = second_ref[i * rows : (i + 1) * rows]


def pack_feed(first, second):
    rows, width = first.shape[0], second.shape[1]
    blocks = (first.size + second.size) // (rows * width)
    return pl.pallas_call(
        pack_feed_kernel,
        out_shape=jax.ShapeDtypeStruct((blocks, rows, width), bf16),
        compiler_params=params,
        cost_estimate=cost(3),
        name="pack_feed",
    )(first, second)


def after_kernel(*refs):
    done_ref = refs[-1]
    done_ref[0] = 0


def after(values, *sooner):
    if not sooner:
        return values
    return pl.pallas_call(
        after_kernel,
        in_specs=[in_place()] * (1 + len(sooner)),
        out_specs=[in_place(), smem()],
        out_shape=[jax.ShapeDtypeStruct(values.shape, values.dtype), jax.ShapeDtypeStruct((1,), jnp.int32)],
        input_output_aliases={0: 0},
        compiler_params=params,
        cost_estimate=cost(0.01),
        name="after",
    )(values, *sooner)[0]


AXES = ("fsdp", "dp")


def ring_order(size):
    return list(range(0, size, 2)) + list(range(size - 1, 0, -2))


class Links:
    def __init__(self, shard_rows):
        self.size, self.parts = lax.axis_size("fsdp"), lax.axis_size("dp")
        order = ring_order(self.size)
        after = {order[i]: order[(i + 1) % self.size] for i in range(self.size)}
        before = {later: sooner for sooner, later in after.items()}
        every = [(f, d) for f in range(self.size) for d in range(self.parts)]
        flat = lambda f, d: f * self.parts + d
        self.onward = [(flat(f, d), flat((before if d % 2 else after)[f], d)) for f, d in every]
        self.sibling = [(flat(f, d), flat(f, d ^ 1)) for f, d in every]
        self.core = lax.axis_index("dp") % 2
        self.hops = self.size // 2

        rows, table = shard_rows, []
        for f, d in every:
            place, core = order.index(f), d % 2
            toward = 1 - 2 * core
            shards, inside = [f], [0]
            for hop in range(1, self.hops + 1):
                for sign in (-1, 1):
                    shards.append(order[(place + sign * toward * hop) % self.size])
                    late = core if sign == -1 else 1 - core
                    inside.append(late * (rows // 2) if hop == self.hops else 0)
            first = [shard * rows + at for shard, at in zip(shards, inside)]
            table.append([first, shards, inside])
        self.table = lax.dynamic_index_in_dim(
            jnp.array(table, jnp.int32), lax.axis_index(AXES), 0, keepdims=False
        )

    def send(self, values, pairs):
        return lax.ppermute(values, AXES, pairs)

    def last(self, values):
        half = values.shape[1] // 2
        return lax.dynamic_slice_in_dim(values, self.core * half, half, 1)


class Gather:
    def __init__(self, links, own):
        self.links, self.moving, self.count, self.quarter, self.pieces = links, own, 0, 0, []

    def share(self, *sooner):
        self.moving = after(self.moving, *sooner)
        self.shared = self.moving
        self.pieces.append(self.moving)
        if self.count:
            self.pieces.append(self.links.send(self.moving, self.links.sibling))

    def hop(self, *sooner):
        links = self.links
        self.quarter += 1
        while self.count < self.quarter * links.hops // 4:
            self.share(*sooner)
            sooner = ()
            self.count += 1
            moving = links.last(self.moving) if self.count == links.hops else self.moving
            self.moving = links.send(moving, links.onward)
        if self.count == links.hops:
            self.share()


def body(
    inputs, encoder, cotangent, buckets, lengths, self_query, self_key, self_value, self_output,
    cross_query, cross_key, cross_value, cross_output, fc_first, fc_second, norm_gains,
    down_master, up_master, down_first, down_second, up_first, up_second,
):
    rows, width = self_query.shape
    links = Links(rows)
    table = links.table
    sq, sk, sv, ck, cv, so, cq, co = range(8)
    early = Gather(
        links,
        pack((self_query, self_key, self_value, cross_key, cross_value, self_output, cross_query, cross_output)),
    )
    early.hop()
    early.hop()
    early.hop()
    third = early.moving
    early.hop()
    late = Gather(links, pack_feed(fc_first, fc_second))
    late.hop(third)

    qkv, squares = project(inputs, table, early.pieces, (sq, sk, sv), query_scale, 2)
    kv, kv_squares = project(encoder, table, early.pieces, (ck, cv), 1.0, 1)
    self_packs = [(qkv, squares, 0), (qkv, squares, 1), (qkv, None, 2)]
    half = width // PAIR // 2
    late.hop(kv_squares)
    *self_half, done = attend(buckets, lengths, *self_packs, True, 0, half, (), (late.shared,))
    self_out, self_weight, self_share, done = attend(
        buckets, lengths, *self_packs, True, half, 2 * half, self_half
    )
    late.hop(done)
    first, first_inverse, query_cross, query_squares = after_self(
        inputs, self_out, norm_gains, table, early.pieces, (so, cq), (late.shared,)
    )
    cross_packs = [(query_cross, query_squares, 0), (kv, kv_squares, 0), (kv, None, 1)]
    *cross_half, done = attend(buckets, lengths, *cross_packs, False, 0, half)
    late.hop(done)
    cross_out, cross_weight, cross_share, done = attend(
        buckets, lengths, *cross_packs, False, half, 2 * half, cross_half, (late.shared,)
    )

    outputs, grad_cross_pre, grad_cross_out, down_local, up_local = feed(
        buckets, lengths, table, first, cross_out, cross_share, cotangent, norm_gains, down_master, up_master,
        early.pieces, co, late.pieces,
    )
    down_grad, up_grad = lax.psum((down_local, up_local), ("fsdp", "dp"))

    dq, dk, dv = attend_back(*cross_packs, grad_cross_out, cross_out, cross_weight, False)
    encoder_grad, grad_self_pre, grad_self_out = after_cross_back(
        dq, dk, dv, grad_cross_pre, first, first_inverse, self_share, norm_gains, table, early.pieces, (cq, so, ck, cv)
    )
    dq, dk, dv = attend_back(*self_packs, grad_self_out, self_out, self_weight, True)
    input_grad = input_gradient(dq, dk, dv, grad_self_pre, table, early.pieces, (sq, sk, sv))

    down_first_new, down_second_new, down_master_new = adamw(
        down_master, down_first, down_second, down_grad
    )
    up_first_new, up_second_new, up_master_new = adamw(up_master, up_first, up_second, up_grad)
    return (
        outputs,
        input_grad,
        encoder_grad,
        down_grad,
        up_grad,
        down_first_new,
        down_second_new,
        up_first_new,
        up_second_new,
        down_master_new,
        up_master_new,
        down_master_new.astype(bf16),
        up_master_new.astype(bf16),
    )


def solution(mesh):
    tokens, matrix = P(("fsdp", "dp"), None), P("fsdp", None)
    return jax.shard_map(
        body,
        mesh=mesh,
        in_specs=(tokens, tokens, tokens, P(("fsdp", "dp")), tokens) + (matrix,) * 10 + (P(),) * 7,
        out_specs=(tokens,) * 3 + (P(),) * 10,
        check_vma=False,
    )
```

```python
import functools
import math

import jax
import jax.numpy as jnp
from jax import lax
from jax.experimental import pallas as pl
from jax.experimental.pallas import tpu as pltpu
from jax.sharding import PartitionSpec as P

HEAD_DIM = 64
PAIR = 2 * HEAD_DIM
STEP = 10
SLOTS = 4

epsilon_norm = 1e-05
beta_first = 0.9
beta_second = 0.999
learn_rate = 0.05
weight_decay = 0.01
epsilon_adam = 1e-08

f32, bf16 = jnp.float32, jnp.bfloat16
query_scale = HEAD_DIM ** (-0.5) * math.log2(math.e)
forbidden = -(2.0**100)
score_limit = 64.0

params = pltpu.CompilerParams(vmem_limit_bytes=58 * 2**20)


def contract(left, right, left_dim, right_dim):
    return lax.dot_general(
        left, right, (((left_dim,), (right_dim,)), ((), ())), preferred_element_type=f32
    )


def start_loading(pieces, table_ref, wanted, store, sems):
    count = len(pieces) // 2
    for slot, (group, i) in enumerate(wanted):
        for p, piece in enumerate(pieces[group * count : (group + 1) * count]):
            rows = piece.shape[1]
            at = pl.multiple_of(table_ref[0, p], 16)
            pltpu.make_async_copy(
                piece.at[i], store.at[slot, pl.ds(at, rows)], sems.at[slot]
            ).start()


def loaded(store, sems, slot):
    pltpu.make_async_copy(store.at[slot], store.at[slot], sems.at[slot]).wait()


def loaded_once(store, sems, slot):
    @pl.when(pl.program_id(0) == 0)
    def wait():
        loaded(store, sems, slot)


def cost(microseconds):
    return pl.CostEstimate(flops=int(microseconds * 1.15e9), bytes_accessed=10**5, transcendentals=0)


def in_place():
    return pl.BlockSpec(memory_space=pl.ANY)


def stores(count, width):
    return [pltpu.VMEM((count, width, width), bf16), pltpu.SemaphoreType.DMA((count,))]


smem = functools.partial(pl.BlockSpec, memory_space=pltpu.SMEM)


def normalise(values):
    centre = values - jnp.mean(values, axis=-1, keepdims=True)
    inverse = lax.rsqrt(jnp.mean(centre * centre, axis=-1, keepdims=True) + epsilon_norm)
    return centre * inverse, inverse


def normalise_back(scaled, normal, inverse):
    return inverse * (
        scaled
        - jnp.mean(scaled, axis=-1, keepdims=True)
        - normal * jnp.mean(scaled * normal, axis=-1, keepdims=True)
    )


def gelu_and_slope(u):
    bell = jnp.exp2(u * u * (-0.5 * math.log2(math.e)))
    t = 1.0 / (1.0 + (0.3275911 * math.sqrt(0.5)) * jnp.abs(u))
    tail = t * (
        0.5 * 0.254829592
        + t
        * (
            0.5 * -0.284496736
            + t * (0.5 * 1.421413741 + t * (0.5 * -1.453152027 + t * (0.5 * 1.061405429)))
        )
    )
    tail = tail * bell
    below = jnp.where(u > 0, 1.0 - tail, tail)
    return u * below, below + u * bell * (1.0 / math.sqrt(2.0 * math.pi))


def head_squares(values):
    width = values.shape[1]
    member = (
        lax.broadcasted_iota(jnp.int32, (width, PAIR), 0) >> 6
        == lax.broadcasted_iota(jnp.int32, (width, PAIR), 1)
    ).astype(bf16)
    return jnp.max(contract(values * values, member, 1, 0), axis=0, keepdims=True)


def project_kernel(scale, squared, wanted, table_ref, x_ref, *refs):
    *pieces, out_ref, square_ref, store, sems = refs
    step = pl.program_id(0)

    @pl.when(step == 0)
    def begin():
        start_loading(pieces, table_ref, wanted, store, sems)

    loaded(store, sems, step)
    out = contract(x_ref[...], store[step], 1, 0)
    if scale != 1.0:
        out = out * jnp.where(step == 0, scale, 1.0)
    out = out.astype(bf16)
    out_ref[0] = out

    @pl.when(step < squared)
    def squares():
        square_ref[0] = jnp.broadcast_to(head_squares(out), square_ref.shape[1:])

    @pl.when(step >= squared)
    def no_squares():
        square_ref[0] = jnp.zeros(square_ref.shape[1:], f32)


def project(x, table, pieces, wanted, scale, squared):
    tokens, width = x.shape
    count = len(wanted)
    return pl.pallas_call(
        functools.partial(project_kernel, scale, squared, wanted),
        grid=(count,),
        in_specs=[smem(), pl.BlockSpec((tokens, width), lambda i: (0, 0))]
        + [in_place() for piece in pieces],
        out_specs=[
            pl.BlockSpec((1, tokens, width), lambda i: (i, 0, 0)),
            pl.BlockSpec((1, 8, PAIR), lambda i: (i, 0, 0)),
        ],
        out_shape=[
            jax.ShapeDtypeStruct((count, tokens, width), bf16),
            jax.ShapeDtypeStruct((count, 8, PAIR), f32),
        ],
        scratch_shapes=stores(count, width),
        compiler_params=params,
        cost_estimate=cost(0.1 * count),
        name="project",
    )(table, x, *pieces)


def low_half(rows):
    return lax.broadcasted_iota(jnp.int32, (rows, PAIR), 1) < HEAD_DIM


def choose(head, low):
    if head == 0:
        return lambda own, other: jnp.where(low, own, other)
    return lambda own, other: jnp.where(low, other, own)


def item_shift(bucket, tokens):
    return bucket + (tokens.bit_length() - 1 - 2)


def item_length(item, lengths_ref):
    length = jnp.zeros_like(item)
    for slot in range(SLOTS):
        length = jnp.where(item == slot, lengths_ref[0, slot], length)
    return length


def attend_kernel(
    causal, q_at, k_at, start, bucket_ref, lengths_ref, qsq_ref, ksq_ref, q_ref, k_ref, v_ref, *refs
):
    out_ref, weight_ref, scale_ref, done_ref, qmark, kmark = refs[-6:]
    done_ref[...] = jnp.zeros_like(done_ref)
    tokens = q_ref.shape[-2]
    low = low_half(tokens)
    pair = pl.program_id(0) + start

    @pl.when(pl.program_id(0) == 0)
    def marks():
        shift = item_shift(bucket_ref[0], tokens)
        lane = lax.broadcasted_iota(jnp.int32, (tokens, PAIR), 1) & (HEAD_DIM - 1)
        row = lax.broadcasted_iota(jnp.int32, (tokens, PAIR), 0)
        item = row >> shift
        own = lane == item
        qmark[...] = jnp.where(own, 1.0, 0.0).astype(bf16)
        allowed = own & (row - (item << shift) < item_length(item, lengths_ref))
        kmark[...] = jnp.where((lane < SLOTS) & ~allowed, forbidden, 0.0).astype(bf16)

    q, k, v = q_ref[0], k_ref[0], v_ref[0]
    one = jnp.ones((tokens, PAIR), bf16)

    def operands(head):
        own = choose(head, low)
        return own(q, qmark[...]), own(k, kmark[...]), own(v, one)

    def finish(sums):
        even, odd = sums
        share = 1.0 / jnp.concatenate([even[HEAD_DIM:], odd[:HEAD_DIM]], axis=0)
        out = jnp.concatenate([even[:HEAD_DIM], odd[HEAD_DIM:]], axis=0) * share
        out_ref[...] = out.T.astype(bf16)
        scale_ref[...] = share.T

    bound = score_limit * score_limit
    small = (
        qsq_ref[q_at, 0, 2 * pair] * ksq_ref[k_at, 0, 2 * pair] <= bound
    ) & (qsq_ref[q_at, 0, 2 * pair + 1] * ksq_ref[k_at, 0, 2 * pair + 1] <= bound)

    @pl.when(small)
    def direct():
        sums = []
        for head in range(2):
            queries, keys, values = operands(head)
            if not causal:
                weight = jnp.exp2(contract(keys, queries, 1, 1)).astype(bf16)
                weight_ref[head] = weight
                sums.append(contract(values, weight, 0, 0))
                continue
            step = tokens // 2
            before = lax.broadcasted_iota(jnp.int32, (step, step), 0) <= lax.broadcasted_iota(
                jnp.int32, (step, step), 1
            )
            nothing = jnp.zeros((), bf16)
            top = jnp.exp2(contract(keys[:step], queries, 1, 1)).astype(bf16)
            top = jnp.concatenate(
                [jnp.where(before, top[:, :step], nothing), top[:, step:]], axis=1
            )
            weight_ref[head, :step] = top
            total = contract(values[:step], top, 0, 0)
            low_part = jnp.exp2(contract(keys[step:], queries[step:], 1, 1)).astype(bf16)
            low_part = jnp.where(before, low_part, nothing)
            weight_ref[head, step:, step:] = low_part
            rest = contract(values[step:], low_part, 0, 0)
            sums.append(jnp.concatenate([total[:, :step], total[:, step:] + rest], axis=1))
        finish(sums)

    @pl.when(jnp.logical_not(small))
    def shifted():
        sums = []
        for head in range(2):
            queries, keys, values = operands(head)
            scores = contract(keys, queries, 1, 1)
            if causal:
                before = lax.broadcasted_iota(
                    jnp.int32, scores.shape, 0
                ) <= lax.broadcasted_iota(jnp.int32, scores.shape, 1)
                scores = jnp.where(before, scores, forbidden)
            scores = scores - jnp.max(scores, axis=0, keepdims=True)
            weight = jnp.exp2(scores).astype(bf16)
            weight_ref[head] = weight
            sums.append(contract(values, weight, 0, 0))
        finish(sums)


def attend(bucket, lengths, q_pack, k_pack, v_pack, causal, start, stop, so_far=(), sooner=()):
    (q, q_squares, q_at), (k, k_squares, k_at), (v, unused, v_at) = q_pack, k_pack, v_pack
    tokens, width = q.shape[1:]
    pairs = width // PAIR
    pair_spec = lambda at: pl.BlockSpec((1, tokens, PAIR), lambda j: (at, 0, start + j))
    flat_spec = pl.BlockSpec((tokens, PAIR), lambda j: (0, start + j))
    return pl.pallas_call(
        functools.partial(attend_kernel, causal, q_at, k_at, start),
        grid=(stop - start,),
        in_specs=[smem(), smem(), smem(), smem(), pair_spec(q_at), pair_spec(k_at), pair_spec(v_at)]
        + [in_place() for array in (*so_far, *sooner)],
        out_specs=[
            flat_spec,
            pl.BlockSpec((2, tokens, tokens), lambda j: (start + j, 0, 0)),
            flat_spec,
            pl.BlockSpec((8, PAIR), lambda j: (0, 0)),
        ],
        out_shape=[
            jax.ShapeDtypeStruct((tokens, width), bf16),
            jax.ShapeDtypeStruct((2 * pairs, tokens, tokens), bf16),
            jax.ShapeDtypeStruct((tokens, width), f32),
            jax.ShapeDtypeStruct((8, PAIR), f32),
        ],
        input_output_aliases={7 + i: i for i in range(len(so_far))},
        scratch_shapes=[pltpu.VMEM((tokens, PAIR), bf16), pltpu.VMEM((tokens, PAIR), bf16)],
        compiler_params=params,
        cost_estimate=cost(0.05 * (stop - start)),
        name="attend",
    )(bucket, lengths, q_squares, k_squares, q, k, v, *so_far, *sooner)


def attend_back_kernel(
    causal, q_ref, k_ref, v_ref, grad_ref, out_ref, weight_ref, dq_ref, dk_ref, dv_ref
):
    tokens = q_ref.shape[-2]
    low = low_half(tokens)
    q, k, v, grad = q_ref[0], k_ref[0], v_ref[0], grad_ref[...]
    nothing = jnp.zeros((tokens, PAIR), bf16)
    minus = jnp.full((tokens, PAIR), -1.0, bf16)
    swap = (
        (lax.broadcasted_iota(jnp.int32, (PAIR, PAIR), 0) < HEAD_DIM)
        != (lax.broadcasted_iota(jnp.int32, (PAIR, PAIR), 1) < HEAD_DIM)
    ).astype(bf16)
    product = grad.astype(f32) * out_ref[...].astype(f32)
    high = product.astype(bf16)
    centre = contract(high, swap, 1, 0) + contract((product - high.astype(f32)).astype(bf16), swap, 1, 0)
    high = centre.astype(bf16)
    rest = (centre - high.astype(f32)).astype(bf16)
    lane = lax.broadcasted_iota(jnp.int32, (tokens, PAIR), 1) & (HEAD_DIM - 1)
    centre = jnp.where(lane == 0, high, jnp.where(lane == 1, rest, nothing))

    step = tokens // 2 if causal else tokens
    dq_turned = None
    for tile in range(tokens // step):
        at = tile * step
        rows = slice(at, at + step)
        dk = dv = None
        turned = []
        for head in range(2):
            own = choose(head, low)
            weight = weight_ref[head, rows, at:]
            dweight = contract(own(v, minus)[rows], own(grad, centre)[at:], 1, 1)
            dscore = weight * dweight.astype(bf16)
            dv_own = contract(weight, own(grad, nothing)[at:], 1, 0)
            dk_own = contract(dscore, own(q, nothing)[at:], 1, 0)
            dv = dv_own if head == 0 else dv + dv_own
            dk = dk_own if head == 0 else dk + dk_own
            turned.append(contract(k[rows], dscore, 0, 0)[head * HEAD_DIM : (head + 1) * HEAD_DIM])
        dv_ref[rows] = dv.astype(bf16)
        dk_ref[rows] = (dk * math.log(2.0)).astype(bf16)
        turned = jnp.concatenate(turned, axis=0)
        if tile == 0:
            dq_turned = turned
        else:
            dq_turned = jnp.concatenate([dq_turned[:, :at], dq_turned[:, at:] + turned], axis=1)
    dq_ref[...] = (dq_turned * HEAD_DIM ** (-0.5)).T.astype(bf16)


def attend_back(q_pack, k_pack, v_pack, grad, out, weight, causal):
    (q, unused, q_at), (k, unused, k_at), (v, unused, v_at) = q_pack, k_pack, v_pack
    tokens, width = q.shape[1:]
    pairs = width // PAIR
    pair_spec = lambda at: pl.BlockSpec((1, tokens, PAIR), lambda j: (at, 0, j))
    flat_spec = pl.BlockSpec((tokens, PAIR), lambda j: (0, j))
    return pl.pallas_call(
        functools.partial(attend_back_kernel, causal),
        grid=(pairs,),
        in_specs=[
            pair_spec(q_at),
            pair_spec(k_at),
            pair_spec(v_at),
            flat_spec,
            flat_spec,
            pl.BlockSpec((2, tokens, tokens), lambda j: (j, 0, 0)),
        ],
        out_specs=[flat_spec] * 3,
        out_shape=[jax.ShapeDtypeStruct((tokens, width), bf16)] * 3,
        compiler_params=params,
        cost_estimate=cost(0.2),
        name="attend_back",
    )(q, k, v, grad, out, weight)


def first_kernel(wanted, count, table_ref, x_ref, out_ref, gains_ref, *refs):
    pieces = refs[:count]
    first_ref, inverse_ref, q_ref, square_ref, store, sems = refs[-6:]
    step = pl.program_id(0)

    @pl.when(step == 0)
    def load():
        start_loading(pieces, table_ref, wanted, store, sems)

    loaded_once(store, sems, 0)
    z = x_ref[...].astype(f32) + contract(out_ref[...], store[0], 1, 0)
    normal, inverse = normalise(z)
    first = normal * gains_ref[0:1]
    first_ref[...] = first
    inverse_ref[...] = jnp.broadcast_to(inverse, inverse_ref.shape)
    loaded_once(store, sems, 1)
    q = (contract(first.astype(bf16), store[1], 1, 0) * query_scale).astype(bf16)
    q_ref[0] = q
    squares = jnp.broadcast_to(head_squares(q), square_ref.shape[1:])

    @pl.when(step == 0)
    def begin():
        square_ref[0] = squares

    @pl.when(step > 0)
    def more():
        square_ref[0] = jnp.maximum(square_ref[0], squares)


def after_self(x, out, gains, table, pieces, wanted, sooner):
    tokens, width = x.shape
    rows = tokens // 4
    tile = pl.BlockSpec((rows, width), lambda i: (i, 0))
    return pl.pallas_call(
        functools.partial(first_kernel, wanted, len(pieces)),
        grid=(tokens // rows,),
        in_specs=[smem(), tile, tile, pl.BlockSpec(gains.shape, lambda i: (0, 0))]
        + [in_place() for piece in (*pieces, *sooner)],
        out_specs=[
            tile,
            pl.BlockSpec((rows, PAIR), lambda i: (i, 0)),
            pl.BlockSpec((1, rows, width), lambda i: (0, i, 0)),
            pl.BlockSpec((1, 8, PAIR), lambda i: (0, 0, 0)),
        ],
        out_shape=[
            jax.ShapeDtypeStruct((tokens, width), f32),
            jax.ShapeDtypeStruct((tokens, PAIR), f32),
            jax.ShapeDtypeStruct((1, tokens, width), bf16),
            jax.ShapeDtypeStruct((1, 8, PAIR), f32),
        ],
        scratch_shapes=stores(len(wanted), width),
        compiler_params=params,
        cost_estimate=cost(0.2),
        name="after_self",
    )(table, x, out, gains, *pieces, *sooner)


def load_feed(feed_pieces, table_ref, kinds, feed_store, feed_sems):
    blocks = feed_store.shape[2]
    for kind in kinds:
        for p, piece in enumerate(feed_pieces):
            rows_at = pl.ds(pl.multiple_of(table_ref[2, p], 16), piece.shape[1])
            pltpu.make_async_copy(
                piece.at[pl.ds(kind * blocks, blocks)],
                feed_store.at[kind, table_ref[1, p], :, rows_at],
                feed_sems.at[kind],
            ).start()


def first_block(feed_store, i):
    return feed_store[0, :, i].reshape(-1, feed_store.shape[-1])


def second_block(feed_store, i):
    devices, blocks = feed_store.shape[1:3]
    return feed_store[1, i * devices // blocks : (i + 1) * devices // blocks].reshape(
        -1, feed_store.shape[-1]
    )


def feed_kernel(
    wanted, count, bucket_ref, lengths_ref, table_ref, first_ref, out_ref, cotangent_ref, gains_ref, down_ref,
    up_ref, *refs,
):
    pieces, feed_pieces = refs[: 2 * count], refs[2 * count : 3 * count]
    (outputs_ref, third_ref, slope_ref, normal_ref, inverse_ref, adapter_ref, down_grad_ref, up_grad_ref,
     down_low, up_low, store, sems, feed_store, feed_sems) = refs[3 * count :]
    rows, width = first_ref.shape
    tokens = rows * pl.num_programs(0)
    step = pl.program_id(0)

    @pl.when(step == 0)
    def begin():
        start_loading(pieces, table_ref, wanted, store, sems)
        load_feed(feed_pieces, table_ref, (0, 1), feed_store, feed_sems)
        down_low[...] = down_ref[...].astype(bf16)
        up_low[...] = up_ref[...].astype(bf16)
        down_grad_ref[...] = jnp.zeros_like(down_grad_ref)
        up_grad_ref[...] = jnp.zeros_like(up_grad_ref)

    loaded_once(store, sems, 0)
    z = first_ref[...] + contract(out_ref[...], store[0], 1, 0)
    second_normal, second_inverse = normalise(z)
    normal_ref[...] = second_normal.astype(bf16)
    inverse_ref[...] = jnp.broadcast_to(second_inverse, inverse_ref.shape)
    second = second_normal * gains_ref[1:2]
    second_low = second.astype(bf16)

    adapter_act, adapter_slope = gelu_and_slope(contract(second_low, down_low[...], 1, 0))
    adapter_act = adapter_act.astype(bf16)
    total = second + 4.0 * contract(adapter_act, up_low[...], 1, 0)
    loaded_once(feed_store, feed_sems, 0)
    loaded_once(feed_store, feed_sems, 1)
    for i in range(feed_store.shape[2]):
        active, slope = gelu_and_slope(contract(second_low, first_block(feed_store, i), 1, 0))
        slope_ref[i] = slope.astype(bf16)
        total += contract(active.astype(bf16), second_block(feed_store, i), 1, 0)

    third_normal, third_inverse = normalise(total)
    outputs_ref[...] = (third_normal * gains_ref[2:3]).astype(bf16)

    shift = item_shift(bucket_ref[0], tokens)
    row = lax.broadcasted_iota(jnp.int32, (rows, 1), 0) + step * rows
    item = row >> shift
    valid = row - (item << shift) < item_length(item, lengths_ref)
    upstream = jnp.where(valid, cotangent_ref[...].astype(f32), 0.0)
    grad_third = normalise_back(upstream * gains_ref[2:3], third_normal, third_inverse)
    third_ref[...] = grad_third

    grad_adapter_out = (4.0 * grad_third).astype(bf16)
    up_grad_ref[...] += contract(adapter_act, grad_adapter_out, 0, 0)
    grad_adapter_pre = (contract(grad_adapter_out, up_low[...], 1, 1) * adapter_slope).astype(bf16)
    adapter_ref[...] = grad_adapter_pre
    down_grad_ref[...] += contract(second_low, grad_adapter_pre, 0, 0)


def feed(bucket, lengths, table, first, out, cotangent, gains, down, up, pieces, output_at, feed_pieces):
    tokens, width = first.shape
    rows = tokens // 4
    chunks, shard_rows = feed_pieces[0].shape[0] // 2, feed_pieces[0].shape[1]
    tile = pl.BlockSpec((rows, width), lambda i: (i, 0))
    fixed = lambda a: pl.BlockSpec(a.shape, lambda i: (0,) * a.ndim, pipeline_mode=pl.Buffered(1))
    return pl.pallas_call(
        functools.partial(feed_kernel, (output_at,), len(feed_pieces)),
        grid=(tokens // rows,),
        in_specs=[smem(), smem(), smem(), tile, tile, tile, fixed(gains), fixed(down), fixed(up)]
        + [in_place() for piece in pieces + feed_pieces],
        out_specs=[
            tile,
            tile,
            pl.BlockSpec((chunks, rows, width), lambda i: (0, i, 0)),
            tile,
            pl.BlockSpec((rows, PAIR), lambda i: (i, 0)),
            pl.BlockSpec((rows, down.shape[1]), lambda i: (i, 0)),
            fixed(down),
            fixed(up),
        ],
        out_shape=[
            jax.ShapeDtypeStruct((tokens, width), bf16),
            jax.ShapeDtypeStruct((tokens, width), f32),
            jax.ShapeDtypeStruct((chunks, tokens, width), bf16),
            jax.ShapeDtypeStruct((tokens, width), bf16),
            jax.ShapeDtypeStruct((tokens, PAIR), f32),
            jax.ShapeDtypeStruct((tokens, down.shape[1]), bf16),
            jax.ShapeDtypeStruct(down.shape, f32),
            jax.ShapeDtypeStruct(up.shape, f32),
        ],
        scratch_shapes=[
            pltpu.VMEM(down.shape, bf16),
            pltpu.VMEM(up.shape, bf16),
            *stores(1, width),
            pltpu.VMEM((2, width // shard_rows, chunks, shard_rows, width), bf16),
            pltpu.SemaphoreType.DMA((2,)),
        ],
        compiler_params=params,
        cost_estimate=cost(0.2),
        name="feed",
    )(bucket, lengths, table, first, out, cotangent, gains, down, up, *pieces, *feed_pieces)


def feed_back_kernel(
    wanted, count, table_ref, third_ref, slope_ref, normal_ref, inverse_ref, adapter_ref, share_ref, gains_ref,
    down_ref, *refs,
):
    pieces, feed_pieces = refs[: 2 * count], refs[2 * count : 3 * count]
    grad_ref, grad_out_ref, down_low, store, sems, feed_store, feed_sems = refs[3 * count :]

    @pl.when(pl.program_id(0) == 0)
    def begin():
        load_feed(feed_pieces, table_ref, (1, 0), feed_store, feed_sems)
        start_loading(pieces, table_ref, wanted, store, sems)
        down_low[...] = down_ref[...].astype(bf16)

    grad_third = third_ref[...]
    grad_feed = grad_third.astype(bf16)
    grad_second = grad_third + contract(adapter_ref[...], down_low[...], 1, 1)
    loaded_once(feed_store, feed_sems, 1)
    loaded_once(feed_store, feed_sems, 0)
    for i in range(feed_store.shape[2]):
        grad_inner = contract(grad_feed, second_block(feed_store, i), 1, 1)
        grad_inner = (grad_inner * slope_ref[i].astype(f32)).astype(bf16)
        grad_second += contract(grad_inner, first_block(feed_store, i), 1, 1)

    grad_pre = normalise_back(
        grad_second * gains_ref[1:2], normal_ref[...].astype(f32), inverse_ref[:, 0:1]
    )
    grad_ref[...] = grad_pre
    loaded_once(store, sems, 0)
    grad_out_ref[...] = (contract(grad_pre.astype(bf16), store[0], 1, 1) * share_ref[...]).astype(bf16)


def feed_back(table, third, slope, normal, inverse, adapter, share, gains, down, pieces, output_at, feed_pieces):
    tokens, width = third.shape
    rows = tokens // 4
    chunks, shard_rows = feed_pieces[0].shape[0] // 2, feed_pieces[0].shape[1]
    tile = pl.BlockSpec((rows, width), lambda i: (i, 0))
    fixed = lambda a: pl.BlockSpec(a.shape, lambda i: (0,) * a.ndim, pipeline_mode=pl.Buffered(1))
    return pl.pallas_call(
        functools.partial(feed_back_kernel, (output_at,), len(feed_pieces)),
        grid=(tokens // rows,),
        in_specs=[
            smem(),
            tile,
            pl.BlockSpec((chunks, rows, width), lambda i: (0, i, 0)),
            tile,
            pl.BlockSpec((rows, PAIR), lambda i: (i, 0)),
            pl.BlockSpec((rows, down.shape[1]), lambda i: (i, 0)),
            tile,
            fixed(gains),
            fixed(down),
        ]
        + [in_place() for piece in pieces + feed_pieces],
        out_specs=[tile, tile],
        out_shape=[
            jax.ShapeDtypeStruct((tokens, width), f32),
            jax.ShapeDtypeStruct((tokens, width), bf16),
        ],
        scratch_shapes=[
            pltpu.VMEM(down.shape, bf16),
            *stores(1, width),
            pltpu.VMEM((2, width // shard_rows, chunks, shard_rows, width), bf16),
            pltpu.SemaphoreType.DMA((2,)),
        ],
        compiler_params=params,
        cost_estimate=cost(0.2),
        name="feed_back",
    )(table, third, slope, normal, inverse, adapter, share, gains, down, *pieces, *feed_pieces)


def cross_back_kernel(
    wanted, table_ref, dq_ref, dk_ref, dv_ref, grad_ref, first_ref, inverse_ref, share_ref, gains_ref,
    *refs,
):
    *pieces, encoder_ref, pre_ref, grad_out_ref, store, sems = refs

    @pl.when(pl.program_id(0) == 0)
    def load():
        start_loading(pieces, table_ref, wanted, store, sems)

    loaded_once(store, sems, 0)
    grad_first = grad_ref[...] + contract(dq_ref[...], store[0], 1, 1)
    loaded_once(store, sems, 1)
    encoder = contract(dk_ref[...], store[1], 1, 1)
    loaded_once(store, sems, 2)
    encoder_ref[...] = (encoder + contract(dv_ref[...], store[2], 1, 1)).astype(bf16)
    gain = gains_ref[0:1]
    grad_pre = normalise_back(grad_first * gain, first_ref[...] / gain, inverse_ref[:, 0:1])
    pre_ref[...] = grad_pre
    loaded_once(store, sems, 3)
    grad_out_ref[...] = (contract(grad_pre.astype(bf16), store[3], 1, 1) * share_ref[...]).astype(bf16)


def after_cross_back(dq, dk, dv, grad, first, inverse, share, gains, table, pieces, wanted):
    tokens, width = first.shape
    rows = tokens // 4
    tile = pl.BlockSpec((rows, width), lambda i: (i, 0))
    return pl.pallas_call(
        functools.partial(cross_back_kernel, wanted),
        grid=(tokens // rows,),
        in_specs=[smem()]
        + [tile] * 5
        + [pl.BlockSpec((rows, PAIR), lambda i: (i, 0)), tile, pl.BlockSpec(gains.shape, lambda i: (0, 0))]
        + [in_place() for piece in pieces],
        out_specs=[tile] * 3,
        out_shape=[
            jax.ShapeDtypeStruct((tokens, width), bf16),
            jax.ShapeDtypeStruct((tokens, width), f32),
            jax.ShapeDtypeStruct((tokens, width), bf16),
        ],
        scratch_shapes=stores(len(wanted), width),
        compiler_params=params,
        cost_estimate=cost(0.2),
        name="after_cross_back",
    )(table, dq, dk, dv, grad, first, inverse, share, gains, *pieces)


def input_kernel(wanted, table_ref, dq_ref, dk_ref, dv_ref, pre_ref, *refs):
    *pieces, out_ref, store, sems = refs

    @pl.when(pl.program_id(0) == 0)
    def load():
        start_loading(pieces, table_ref, wanted, store, sems)

    total = pre_ref[...]
    for slot, ref in enumerate((dq_ref, dk_ref, dv_ref)):
        loaded_once(store, sems, slot)
        total += contract(ref[...], store[slot], 1, 1)
    out_ref[...] = total.astype(bf16)


def input_gradient(dq, dk, dv, pre, table, pieces, wanted):
    tokens, width = pre.shape
    rows = tokens // 4
    tile = pl.BlockSpec((rows, width), lambda i: (i, 0))
    return pl.pallas_call(
        functools.partial(input_kernel, wanted),
        grid=(tokens // rows,),
        in_specs=[smem()] + [tile] * 4 + [in_place() for piece in pieces],
        out_specs=tile,
        out_shape=jax.ShapeDtypeStruct((tokens, width), bf16),
        scratch_shapes=stores(len(wanted), width),
        compiler_params=params,
        cost_estimate=cost(0.2),
        name="input_gradient",
    )(table, dq, dk, dv, pre, *pieces)


def adamw(master, first_moment, second_moment, gradient):
    first_new = beta_first * first_moment + (1.0 - beta_first) * gradient
    second_new = beta_second * second_moment + (1.0 - beta_second) * gradient * gradient
    first_hat = first_new / (1.0 - beta_first**STEP)
    second_hat = second_new / (1.0 - beta_second**STEP)
    master_new = master - learn_rate * (
        first_hat / (jnp.sqrt(second_hat) + epsilon_adam) + weight_decay * master
    )
    return (first_new, second_new, master_new)


def pack_kernel(*refs):
    *shards, out_ref = refs
    for i, shard in enumerate(shards):
        out_ref[i] = shard[...]


def pack(shards):
    return pl.pallas_call(
        pack_kernel,
        out_shape=jax.ShapeDtypeStruct((len(shards),) + shards[0].shape, bf16),
        compiler_params=params,
        cost_estimate=cost(2),
        name="pack",
    )(*shards)


def pack_feed_kernel(first_ref, second_ref, out_ref):
    blocks, rows, width = out_ref.shape
    blocks //= 2
    for i in range(blocks):
        out_ref[i] = first_ref[:, i * width : (i + 1) * width]
        out_ref[blocks + i] = second_ref[i * rows : (i + 1) * rows]


def pack_feed(first, second):
    rows, width = first.shape[0], second.shape[1]
    blocks = (first.size + second.size) // (rows * width)
    return pl.pallas_call(
        pack_feed_kernel,
        out_shape=jax.ShapeDtypeStruct((blocks, rows, width), bf16),
        compiler_params=params,
        cost_estimate=cost(3),
        name="pack_feed",
    )(first, second)


def after_kernel(*refs):
    done_ref = refs[-1]
    done_ref[0] = 0


def after(values, *sooner):
    if not sooner:
        return values
    return pl.pallas_call(
        after_kernel,
        in_specs=[in_place()] * (1 + len(sooner)),
        out_specs=[in_place(), smem()],
        out_shape=[jax.ShapeDtypeStruct(values.shape, values.dtype), jax.ShapeDtypeStruct((1,), jnp.int32)],
        input_output_aliases={0: 0},
        compiler_params=params,
        cost_estimate=cost(0.01),
        name="after",
    )(values, *sooner)[0]


AXES = ("fsdp", "dp")


def ring_order(size):
    return list(range(0, size, 2)) + list(range(size - 1, 0, -2))


class Links:
    def __init__(self, shard_rows):
        self.size, self.parts = lax.axis_size("fsdp"), lax.axis_size("dp")
        order = ring_order(self.size)
        after = {order[i]: order[(i + 1) % self.size] for i in range(self.size)}
        before = {later: sooner for sooner, later in after.items()}
        every = [(f, d) for f in range(self.size) for d in range(self.parts)]
        flat = lambda f, d: f * self.parts + d
        self.onward = [(flat(f, d), flat((before if d % 2 else after)[f], d)) for f, d in every]
        self.sibling = [(flat(f, d), flat(f, d ^ 1)) for f, d in every]
        self.core = lax.axis_index("dp") % 2
        self.hops = self.size // 2

        rows, table = shard_rows, []
        for f, d in every:
            place, core = order.index(f), d % 2
            toward = 1 - 2 * core
            shards, inside = [f], [0]
            for hop in range(1, self.hops + 1):
                for sign in (-1, 1):
                    shards.append(order[(place + sign * toward * hop) % self.size])
                    late = core if sign == -1 else 1 - core
                    inside.append(late * (rows // 2) if hop == self.hops else 0)
            first = [shard * rows + at for shard, at in zip(shards, inside)]
            table.append([first, shards, inside])
        self.table = lax.dynamic_index_in_dim(
            jnp.array(table, jnp.int32), lax.axis_index(AXES), 0, keepdims=False
        )

    def send(self, values, pairs):
        return lax.ppermute(values, AXES, pairs)

    def last(self, values):
        half = values.shape[1] // 2
        return lax.dynamic_slice_in_dim(values, self.core * half, half, 1)


class Gather:
    def __init__(self, links, own):
        self.links, self.moving, self.count, self.quarter, self.pieces = links, own, 0, 0, []

    def share(self, *sooner):
        self.moving = after(self.moving, *sooner)
        self.shared = self.moving
        self.pieces.append(self.moving)
        if self.count:
            self.pieces.append(self.links.send(self.moving, self.links.sibling))

    def hop(self, *sooner):
        links = self.links
        self.quarter += 1
        while self.count < self.quarter * links.hops // 4:
            self.share(*sooner)
            sooner = ()
            self.count += 1
            moving = links.last(self.moving) if self.count == links.hops else self.moving
            self.moving = links.send(moving, links.onward)


def body(
    inputs, encoder, cotangent, buckets, lengths, self_query, self_key, self_value, self_output,
    cross_query, cross_key, cross_value, cross_output, fc_first, fc_second, norm_gains,
    down_master, up_master, down_first, down_second, up_first, up_second,
):
    rows, width = self_query.shape
    links = Links(rows)
    table = links.table
    sq, sk, sv, so = ((0, i) for i in range(4))
    ck, cv, cq, co = ((1, i) for i in range(4))
    one = Gather(links, pack((self_query, self_key, self_value, self_output)))
    two = Gather(links, pack((cross_key, cross_value, cross_query, cross_output)))
    for quarter in range(4):
        one.hop()
        two.hop()
    one.share()
    two.share()
    pieces = one.pieces + two.pieces
    late = Gather(links, pack_feed(fc_first, fc_second))
    late.hop(one.moving, two.moving)

    qkv, squares = project(inputs, table, pieces, (sq, sk, sv), query_scale, 2)
    kv, kv_squares = project(encoder, table, pieces, (ck, cv), 1.0, 1)
    self_packs = [(qkv, squares, 0), (qkv, squares, 1), (qkv, None, 2)]
    half = width // PAIR // 2
    late.hop(squares, kv_squares)
    *self_half, done = attend(buckets, lengths, *self_packs, True, 0, half, (), (late.shared,))
    self_out, self_weight, self_share, done = attend(
        buckets, lengths, *self_packs, True, half, 2 * half, self_half
    )
    late.hop(done)
    first, first_inverse, query_cross, query_squares = after_self(
        inputs, self_out, norm_gains, table, pieces, (so, cq), (late.shared,)
    )
    cross_packs = [(query_cross, query_squares, 0), (kv, kv_squares, 0), (kv, None, 1)]
    *cross_half, done = attend(buckets, lengths, *cross_packs, False, 0, half)
    late.hop(done)
    cross_out, cross_weight, cross_share, done = attend(
        buckets, lengths, *cross_packs, False, half, 2 * half, cross_half, (late.shared,)
    )
    late.share(done)

    outputs, grad_third, slope, second_normal, second_inverse, adapter, down_local, up_local = feed(
        buckets, lengths, table, first, cross_out, cotangent, norm_gains, down_master, up_master, pieces, co,
        late.pieces,
    )
    down_grad, up_grad = lax.psum((down_local, up_local), ("fsdp", "dp"))

    grad_cross_pre, grad_cross_out = feed_back(
        table, grad_third, slope, second_normal, second_inverse, adapter, cross_share, norm_gains, down_master,
        pieces, co, late.pieces,
    )
    dq, dk, dv = attend_back(*cross_packs, grad_cross_out, cross_out, cross_weight, False)
    encoder_grad, grad_self_pre, grad_self_out = after_cross_back(
        dq, dk, dv, grad_cross_pre, first, first_inverse, self_share, norm_gains, table, pieces, (cq, ck, cv, so)
    )
    dq, dk, dv = attend_back(*self_packs, grad_self_out, self_out, self_weight, True)
    input_grad = input_gradient(dq, dk, dv, grad_self_pre, table, pieces, (sq, sk, sv))

    down_first_new, down_second_new, down_master_new = adamw(
        down_master, down_first, down_second, down_grad
    )
    up_first_new, up_second_new, up_master_new = adamw(up_master, up_first, up_second, up_grad)
    return (
        outputs,
        input_grad,
        encoder_grad,
        down_grad,
        up_grad,
        down_first_new,
        down_second_new,
        up_first_new,
        up_second_new,
        down_master_new,
        up_master_new,
        down_master_new.astype(bf16),
        up_master_new.astype(bf16),
    )


def solution(mesh):
    tokens, matrix = P(("fsdp", "dp"), None), P("fsdp", None)
    return jax.shard_map(
        body,
        mesh=mesh,
        in_specs=(tokens, tokens, tokens, P(("fsdp", "dp")), tokens) + (matrix,) * 10 + (P(),) * 7,
        out_specs=(tokens,) * 3 + (P(),) * 10,
        check_vma=False,
    )
```

```python
import functools
import math

import jax
import jax.numpy as jnp
from jax import lax
from jax.experimental import pallas as pl
from jax.experimental.pallas import tpu as pltpu
from jax.sharding import PartitionSpec as P

HEAD_DIM = 64
PAIR = 2 * HEAD_DIM
STEP = 10
SLOTS = 4

epsilon_norm = 1e-05
beta_first = 0.9
beta_second = 0.999
learn_rate = 0.05
weight_decay = 0.01
epsilon_adam = 1e-08

f32, bf16 = jnp.float32, jnp.bfloat16
query_scale = HEAD_DIM ** (-0.5) * math.log2(math.e)
forbidden = -(2.0**100)
score_limit = 64.0

params = pltpu.CompilerParams(vmem_limit_bytes=63 * 2**20)


def contract(left, right, left_dim, right_dim):
    return lax.dot_general(
        left, right, (((left_dim,), (right_dim,)), ((), ())), preferred_element_type=f32
    )


def start_loading(pieces, table_ref, wanted, store, sems, start=0):
    count = len(pieces) // 3

    def copies(group, slot, i):
        for p, piece in enumerate(pieces[group * count : (group + 1) * count]):
            rows = piece.shape[1]
            at = pl.multiple_of(table_ref[0, p], 16)
            pltpu.make_async_copy(
                piece.at[i], store.at[slot, pl.ds(at, rows)], sems.at[slot]
            ).start()

    for slot, (kind, i) in list(enumerate(wanted))[start:]:
        if kind is None:
            copies(0, slot, i)
        else:
            pl.when(table_ref[3, 0] == kind)(functools.partial(copies, 1, slot, i))
            pl.when(table_ref[3, 0] != kind)(functools.partial(copies, 2, slot, i))


def loaded(store, sems, slot):
    pltpu.make_async_copy(store.at[slot], store.at[slot], sems.at[slot]).wait()


def loaded_once(store, sems, slot):
    @pl.when(pl.program_id(0) == 0)
    def wait():
        loaded(store, sems, slot)


def cost(microseconds):
    return pl.CostEstimate(flops=int(microseconds * 1.15e9), bytes_accessed=10**5, transcendentals=0)


def share_spec(share, rows):
    return pl.BlockSpec(share.shape[:2] + (rows,), lambda i: (0, 0, i))


def in_place():
    return pl.BlockSpec(memory_space=pl.ANY)


def stores(count, width):
    return [pltpu.VMEM((count, width, width), bf16), pltpu.SemaphoreType.DMA((count,))]


smem = functools.partial(pl.BlockSpec, memory_space=pltpu.SMEM)


def spread(share_ref, width):
    pairs, two, rows = share_ref.shape
    rest = share_ref[...].reshape(pairs * two, rows)
    member = (
        lax.broadcasted_iota(jnp.int32, (pairs * two, width), 0)
        == lax.broadcasted_iota(jnp.int32, (pairs * two, width), 1) >> 6
    ).astype(bf16)
    parts = []
    for i in range(3):
        parts.append(rest.astype(bf16))
        rest = rest - parts[-1].astype(f32)
    return contract(jnp.concatenate(parts, axis=0), jnp.concatenate([member] * 3, axis=0), 0, 0)


def normalise(values):
    centre = values - jnp.mean(values, axis=-1, keepdims=True)
    inverse = lax.rsqrt(jnp.mean(centre * centre, axis=-1, keepdims=True) + epsilon_norm)
    return centre * inverse, inverse


def normalise_back(scaled, normal, inverse):
    return inverse * (
        scaled
        - jnp.mean(scaled, axis=-1, keepdims=True)
        - normal * jnp.mean(scaled * normal, axis=-1, keepdims=True)
    )


def gelu_and_slope(u):
    bell = jnp.exp2(u * u * (-0.5 * math.log2(math.e)) - 0.5 * math.log2(2.0 * math.pi))
    below = 0.5 + 0.5 * lax.erf(u * math.sqrt(0.5))
    return u * below, below + u * bell


def head_squares(values):
    width = values.shape[1]
    member = (
        lax.broadcasted_iota(jnp.int32, (width, PAIR), 0) >> 6
        == lax.broadcasted_iota(jnp.int32, (width, PAIR), 1)
    ).astype(bf16)
    return jnp.max(contract(values * values, member, 1, 0), axis=0, keepdims=True)


def project_kernel(wanted, scale, squared, count, x_ref, table_ref, *refs):
    pieces = refs[:count]
    out_ref, square_ref, store, sems = refs[-4:]
    step = pl.program_id(0)

    @pl.when(step == 0)
    def begin():
        start_loading(pieces, table_ref, wanted[:1], store, sems)
        loaded(store, sems, 0)
        start_loading(pieces, table_ref, wanted, store, sems, 1)
        out = contract(x_ref[...], store[0], 1, 0)
        out_ref[0] = (out if scale == 1.0 else out * scale).astype(bf16)

    @pl.when(step > 0)
    def more():
        loaded(store, sems, step)
        out_ref[0] = contract(x_ref[...], store[step], 1, 0).astype(bf16)

    @pl.when(step < squared)
    def squares():
        square_ref[0] = jnp.broadcast_to(head_squares(out_ref[0]), square_ref.shape[1:])

    @pl.when(step >= squared)
    def no_squares():
        square_ref[0] = jnp.zeros(square_ref.shape[1:], f32)


def project(x, table, pieces, wanted, scale, squared, sooner=()):
    tokens, width = x.shape
    count = len(wanted)
    return pl.pallas_call(
        functools.partial(project_kernel, wanted, scale, squared, len(pieces)),
        grid=(count,),
        in_specs=[pl.BlockSpec((tokens, width), lambda i: (0, 0)), smem()]
        + [in_place() for piece in (*pieces, *sooner)],
        out_specs=[
            pl.BlockSpec((1, tokens, width), lambda i: (i, 0, 0)),
            pl.BlockSpec((1, 8, PAIR), lambda i: (i, 0, 0)),
        ],
        out_shape=[
            jax.ShapeDtypeStruct((count, tokens, width), bf16),
            jax.ShapeDtypeStruct((count, 8, PAIR), f32),
        ],
        scratch_shapes=stores(count, width),
        compiler_params=params,
        cost_estimate=cost(4 * count),
        name="project",
    )(x, table, *pieces, *sooner)


def low_half(rows):
    return lax.broadcasted_iota(jnp.int32, (rows, PAIR), 1) < HEAD_DIM


def choose(head, low):
    if head == 0:
        return lambda own, other: jnp.where(low, own, other)
    return lambda own, other: jnp.where(low, other, own)


def item_shift(bucket, tokens):
    return bucket + (tokens.bit_length() - 1 - 2)


def item_length(item, lengths_ref):
    length = jnp.zeros_like(item)
    for slot in range(SLOTS):
        length = jnp.where(item == slot, lengths_ref[0, slot], length)
    return length


def attend_kernel(
    causal, q_at, k_at, start, bucket_ref, lengths_ref, qsq_ref, ksq_ref, q_ref, k_ref, v_ref, *refs
):
    out_ref, weight_ref, share_ref, done_ref, qmark, kmark = refs[-6:]
    done_ref[...] = jnp.zeros_like(done_ref)
    tokens = q_ref.shape[-2]
    low = low_half(tokens)
    pair = pl.program_id(0) + start

    @pl.when(pl.program_id(0) == 0)
    def marks():
        shift = item_shift(bucket_ref[0], tokens)
        lane = lax.broadcasted_iota(jnp.int32, (tokens, PAIR), 1) & (HEAD_DIM - 1)
        row = lax.broadcasted_iota(jnp.int32, (tokens, PAIR), 0)
        item = row >> shift
        own = lane == item
        qmark[...] = jnp.where(own, 1.0, 0.0).astype(bf16)
        allowed = own & (row - (item << shift) < item_length(item, lengths_ref))
        kmark[...] = jnp.where((lane < SLOTS) & ~allowed, forbidden, 0.0).astype(bf16)

    q, k, v = q_ref[0], k_ref[0], v_ref[0]
    one = jnp.ones((tokens, PAIR), bf16)

    def operands(head):
        own = choose(head, low)
        return own(q, qmark[...]), own(k, kmark[...]), own(v, one)

    def finish(sums):
        even, odd = sums
        even_share, odd_share = 1.0 / even[HEAD_DIM : HEAD_DIM + 8], 1.0 / odd[:8]
        out = jnp.concatenate(
            [even[:HEAD_DIM] * even_share[:1], odd[HEAD_DIM:] * odd_share[:1]], axis=0
        )
        out_ref[...] = out.astype(bf16).T
        share_ref[0, 0:1] = even_share[:1]
        share_ref[0, 1:2] = odd_share[:1]

    bound = score_limit * score_limit
    small = (
        qsq_ref[q_at, 0, 2 * pair] * ksq_ref[k_at, 0, 2 * pair] <= bound
    ) & (qsq_ref[q_at, 0, 2 * pair + 1] * ksq_ref[k_at, 0, 2 * pair + 1] <= bound)

    @pl.when(small)
    def direct():
        sums = []
        for head in range(2):
            queries, keys, values = operands(head)
            if not causal:
                weight = jnp.exp2(contract(keys, queries, 1, 1)).astype(bf16)
                weight_ref[head] = weight
                sums.append(contract(values, weight, 0, 0))
                continue
            step = tokens // 2
            before = lax.broadcasted_iota(jnp.int32, (step, step), 0) <= lax.broadcasted_iota(
                jnp.int32, (step, step), 1
            )
            nothing = jnp.zeros((), bf16)
            top = jnp.exp2(contract(keys[:step], queries, 1, 1)).astype(bf16)
            top = jnp.concatenate(
                [jnp.where(before, top[:, :step], nothing), top[:, step:]], axis=1
            )
            weight_ref[head, :step] = top
            total = contract(values[:step], top, 0, 0)
            low_part = jnp.exp2(contract(keys[step:], queries[step:], 1, 1)).astype(bf16)
            low_part = jnp.where(before, low_part, nothing)
            weight_ref[head, step:, step:] = low_part
            rest = contract(values[step:], low_part, 0, 0)
            sums.append(jnp.concatenate([total[:, :step], total[:, step:] + rest], axis=1))
        finish(sums)

    @pl.when(jnp.logical_not(small))
    def shifted():
        sums = []
        for head in range(2):
            queries, keys, values = operands(head)
            scores = contract(keys, queries, 1, 1)
            if causal:
                before = lax.broadcasted_iota(
                    jnp.int32, scores.shape, 0
                ) <= lax.broadcasted_iota(jnp.int32, scores.shape, 1)
                scores = jnp.where(before, scores, forbidden)
            scores = scores - jnp.max(scores, axis=0, keepdims=True)
            weight = jnp.exp2(scores).astype(bf16)
            weight_ref[head] = weight
            sums.append(contract(values, weight, 0, 0))
        finish(sums)


def attend(bucket, lengths, q_pack, k_pack, v_pack, causal, start, stop, so_far=(), sooner=()):
    (q, q_squares, q_at), (k, k_squares, k_at), (v, unused, v_at) = q_pack, k_pack, v_pack
    tokens, width = q.shape[1:]
    pairs = width // PAIR
    pair_spec = lambda at: pl.BlockSpec((1, tokens, PAIR), lambda j: (at, 0, start + j))
    flat_spec = pl.BlockSpec((tokens, PAIR), lambda j: (0, start + j))
    return pl.pallas_call(
        functools.partial(attend_kernel, causal, q_at, k_at, start),
        grid=(stop - start,),
        in_specs=[smem(), smem(), smem(), smem(), pair_spec(q_at), pair_spec(k_at), pair_spec(v_at)]
        + [in_place() for array in (*so_far, *sooner)],
        out_specs=[
            flat_spec,
            pl.BlockSpec((2, tokens, tokens), lambda j: (start + j, 0, 0)),
            pl.BlockSpec((1, 2, tokens), lambda j: (start + j, 0, 0)),
            pl.BlockSpec((8, PAIR), lambda j: (0, 0)),
        ],
        out_shape=[
            jax.ShapeDtypeStruct((tokens, width), bf16),
            jax.ShapeDtypeStruct((2 * pairs, tokens, tokens), bf16),
            jax.ShapeDtypeStruct((pairs, 2, tokens), f32),
            jax.ShapeDtypeStruct((8, PAIR), f32),
        ],
        input_output_aliases={7 + i: i for i in range(len(so_far))},
        scratch_shapes=[pltpu.VMEM((tokens, PAIR), bf16), pltpu.VMEM((tokens, PAIR), bf16)],
        compiler_params=params,
        cost_estimate=cost(0.05 * (stop - start)),
        name="attend",
    )(bucket, lengths, q_squares, k_squares, q, k, v, *so_far, *sooner)


def attend_back_kernel(
    causal, q_ref, k_ref, v_ref, grad_ref, out_ref, weight_ref, dq_ref, dk_ref, dv_ref
):
    tokens = q_ref.shape[-2]
    low = low_half(tokens)
    q, k, v, grad = q_ref[0], k_ref[0], v_ref[0], grad_ref[...]
    nothing = jnp.zeros((tokens, PAIR), bf16)
    minus = jnp.full((tokens, PAIR), -1.0, bf16)
    swap = (
        (lax.broadcasted_iota(jnp.int32, (PAIR, PAIR), 0) < HEAD_DIM)
        != (lax.broadcasted_iota(jnp.int32, (PAIR, PAIR), 1) < HEAD_DIM)
    ).astype(bf16)
    product = grad.astype(f32) * out_ref[...].astype(f32)
    high = product.astype(bf16)
    centre = contract(high, swap, 1, 0) + contract((product - high.astype(f32)).astype(bf16), swap, 1, 0)
    high = centre.astype(bf16)
    rest = (centre - high.astype(f32)).astype(bf16)
    lane = lax.broadcasted_iota(jnp.int32, (tokens, PAIR), 1) & (HEAD_DIM - 1)
    centre = jnp.where(lane == 0, high, jnp.where(lane == 1, rest, nothing))

    step = tokens // 2 if causal else tokens
    dq_turned = None
    for tile in range(tokens // step):
        at = tile * step
        rows = slice(at, at + step)
        dk = dv = None
        turned = []
        for head in range(2):
            own = choose(head, low)
            weight = weight_ref[head, rows, at:]
            dweight = contract(own(v, minus)[rows], own(grad, centre)[at:], 1, 1)
            dscore = weight * dweight.astype(bf16)
            dv_own = contract(weight, own(grad, nothing)[at:], 1, 0)
            dk_own = contract(dscore, own(q, nothing)[at:], 1, 0)
            dv = dv_own if head == 0 else dv + dv_own
            dk = dk_own if head == 0 else dk + dk_own
            turned.append(contract(k[rows], dscore, 0, 0)[head * HEAD_DIM : (head + 1) * HEAD_DIM])
        dv_ref[rows] = dv.astype(bf16)
        dk_ref[rows] = (dk * math.log(2.0)).astype(bf16)
        turned = jnp.concatenate(turned, axis=0)
        if tile == 0:
            dq_turned = turned
        else:
            dq_turned = jnp.concatenate([dq_turned[:, :at], dq_turned[:, at:] + turned], axis=1)
    dq_ref[...] = (dq_turned * HEAD_DIM ** (-0.5)).T.astype(bf16)


def attend_back(q_pack, k_pack, v_pack, grad, out, weight, causal):
    (q, unused, q_at), (k, unused, k_at), (v, unused, v_at) = q_pack, k_pack, v_pack
    tokens, width = q.shape[1:]
    pairs = width // PAIR
    pair_spec = lambda at: pl.BlockSpec((1, tokens, PAIR), lambda j: (at, 0, j))
    flat_spec = pl.BlockSpec((tokens, PAIR), lambda j: (0, j))
    return pl.pallas_call(
        functools.partial(attend_back_kernel, causal),
        grid=(pairs,),
        in_specs=[
            pair_spec(q_at),
            pair_spec(k_at),
            pair_spec(v_at),
            flat_spec,
            flat_spec,
            pl.BlockSpec((2, tokens, tokens), lambda j: (j, 0, 0)),
        ],
        out_specs=[flat_spec] * 3,
        out_shape=[jax.ShapeDtypeStruct((tokens, width), bf16)] * 3,
        compiler_params=params,
        cost_estimate=cost(0.2),
        name="attend_back",
    )(q, k, v, grad, out, weight)


def first_kernel(wanted, count, table_ref, x_ref, out_ref, gains_ref, *refs):
    pieces = refs[:count]
    first_ref, inverse_ref, q_ref, square_ref, store, sems = refs[-6:]
    step = pl.program_id(0)

    @pl.when(step == 0)
    def load():
        start_loading(pieces, table_ref, wanted, store, sems)

    loaded_once(store, sems, 0)
    z = x_ref[...].astype(f32) + contract(out_ref[...], store[0], 1, 0)
    normal, inverse = normalise(z)
    first = normal * gains_ref[0:1]
    first_ref[...] = first
    inverse_ref[...] = jnp.broadcast_to(inverse, inverse_ref.shape)
    loaded_once(store, sems, 1)
    q = (contract(first.astype(bf16), store[1], 1, 0) * query_scale).astype(bf16)
    q_ref[0] = q
    squares = jnp.broadcast_to(head_squares(q), square_ref.shape[1:])

    @pl.when(step == 0)
    def begin():
        square_ref[0] = squares

    @pl.when(step > 0)
    def more():
        square_ref[0] = jnp.maximum(square_ref[0], squares)


def after_self(x, out, gains, table, pieces, wanted, sooner):
    tokens, width = x.shape
    rows = tokens // 4
    tile = pl.BlockSpec((rows, width), lambda i: (i, 0))
    return pl.pallas_call(
        functools.partial(first_kernel, wanted, len(pieces)),
        grid=(tokens // rows,),
        in_specs=[smem(), tile, tile, pl.BlockSpec(gains.shape, lambda i: (0, 0))]
        + [in_place() for piece in (*pieces, *sooner)],
        out_specs=[
            tile,
            pl.BlockSpec((rows, PAIR), lambda i: (i, 0)),
            pl.BlockSpec((1, rows, width), lambda i: (0, i, 0)),
            pl.BlockSpec((1, 8, PAIR), lambda i: (0, 0, 0)),
        ],
        out_shape=[
            jax.ShapeDtypeStruct((tokens, width), f32),
            jax.ShapeDtypeStruct((tokens, PAIR), f32),
            jax.ShapeDtypeStruct((1, tokens, width), bf16),
            jax.ShapeDtypeStruct((1, 8, PAIR), f32),
        ],
        scratch_shapes=stores(len(wanted), width),
        compiler_params=params,
        cost_estimate=cost(0.2),
        name="after_self",
    )(table, x, out, gains, *pieces, *sooner)


def load_feed(feed_pieces, table_ref, kinds, feed_store, feed_sems):
    blocks = feed_store.shape[2]
    for kind in kinds:
        for p, piece in enumerate(feed_pieces):
            rows_at = pl.ds(pl.multiple_of(table_ref[2, p], 16), piece.shape[1])
            pltpu.make_async_copy(
                piece.at[pl.ds(kind * blocks, blocks)],
                feed_store.at[kind, table_ref[1, p], :, rows_at],
                feed_sems.at[kind],
            ).start()


def first_block(feed_store, i):
    return feed_store[0, :, i].reshape(-1, feed_store.shape[-1])


def second_block(feed_store, i):
    devices, blocks = feed_store.shape[1:3]
    return feed_store[1, i * devices // blocks : (i + 1) * devices // blocks].reshape(
        -1, feed_store.shape[-1]
    )


def feed_kernel(
    wanted, count, bucket_ref, lengths_ref, table_ref, first_ref, out_ref, cotangent_ref, gains_ref, down_ref,
    up_ref, *refs,
):
    pieces, feed_pieces = refs[: 3 * count], refs[3 * count : 4 * count]
    (outputs_ref, third_ref, slope_ref, normal_ref, inverse_ref, adapter_ref, down_grad_ref, up_grad_ref,
     down_low, up_low, store, sems, feed_store, feed_sems) = refs[4 * count :]
    rows, width = first_ref.shape
    tokens = rows * pl.num_programs(0)
    step = pl.program_id(0)

    @pl.when(step == 0)
    def begin():
        start_loading(pieces, table_ref, wanted, store, sems)
        load_feed(feed_pieces, table_ref, (0, 1), feed_store, feed_sems)
        down_low[...] = down_ref[...].astype(bf16)
        up_low[...] = up_ref[...].astype(bf16)
        down_grad_ref[...] = jnp.zeros_like(down_grad_ref)
        up_grad_ref[...] = jnp.zeros_like(up_grad_ref)

    loaded_once(store, sems, 0)
    z = first_ref[...] + contract(out_ref[...], store[0], 1, 0)
    second_normal, second_inverse = normalise(z)
    normal_ref[...] = second_normal.astype(bf16)
    inverse_ref[...] = jnp.broadcast_to(second_inverse, inverse_ref.shape)
    second = second_normal * gains_ref[1:2]
    second_low = second.astype(bf16)

    adapter_act, adapter_slope = gelu_and_slope(contract(second_low, down_low[...], 1, 0))
    adapter_act = adapter_act.astype(bf16)
    total = second + 4.0 * contract(adapter_act, up_low[...], 1, 0)
    loaded_once(feed_store, feed_sems, 0)
    loaded_once(feed_store, feed_sems, 1)
    for i in range(feed_store.shape[2]):
        active, slope = gelu_and_slope(contract(second_low, first_block(feed_store, i), 1, 0))
        slope_ref[i] = slope.astype(bf16)
        total += contract(active.astype(bf16), second_block(feed_store, i), 1, 0)

    third_normal, third_inverse = normalise(total)
    outputs_ref[...] = (third_normal * gains_ref[2:3]).astype(bf16)

    shift = item_shift(bucket_ref[0], tokens)
    row = lax.broadcasted_iota(jnp.int32, (rows, 1), 0) + step * rows
    item = row >> shift
    valid = row - (item << shift) < item_length(item, lengths_ref)
    upstream = jnp.where(valid, cotangent_ref[...].astype(f32), 0.0)
    grad_third = normalise_back(upstream * gains_ref[2:3], third_normal, third_inverse)
    third_ref[...] = grad_third

    grad_adapter_out = (4.0 * grad_third).astype(bf16)
    up_grad_ref[...] += contract(adapter_act, grad_adapter_out, 0, 0)
    grad_adapter_pre = (contract(grad_adapter_out, up_low[...], 1, 1) * adapter_slope).astype(bf16)
    adapter_ref[...] = grad_adapter_pre
    down_grad_ref[...] += contract(second_low, grad_adapter_pre, 0, 0)


def feed(bucket, lengths, table, first, out, cotangent, gains, down, up, pieces, output_at, feed_pieces):
    tokens, width = first.shape
    rows = tokens // 4
    chunks, shard_rows = feed_pieces[0].shape[0] // 2, feed_pieces[0].shape[1]
    tile = pl.BlockSpec((rows, width), lambda i: (i, 0))
    fixed = lambda a: pl.BlockSpec(a.shape, lambda i: (0,) * a.ndim, pipeline_mode=pl.Buffered(1))
    return pl.pallas_call(
        functools.partial(feed_kernel, (output_at,), len(feed_pieces)),
        grid=(tokens // rows,),
        in_specs=[smem(), smem(), smem(), tile, tile, tile, fixed(gains), fixed(down), fixed(up)]
        + [in_place() for piece in pieces + feed_pieces],
        out_specs=[
            tile,
            tile,
            pl.BlockSpec((chunks, rows, width), lambda i: (0, i, 0)),
            tile,
            pl.BlockSpec((rows, PAIR), lambda i: (i, 0)),
            pl.BlockSpec((rows, down.shape[1]), lambda i: (i, 0)),
            fixed(down),
            fixed(up),
        ],
        out_shape=[
            jax.ShapeDtypeStruct((tokens, width), bf16),
            jax.ShapeDtypeStruct((tokens, width), f32),
            jax.ShapeDtypeStruct((chunks, tokens, width), bf16),
            jax.ShapeDtypeStruct((tokens, width), bf16),
            jax.ShapeDtypeStruct((tokens, PAIR), f32),
            jax.ShapeDtypeStruct((tokens, down.shape[1]), bf16),
            jax.ShapeDtypeStruct(down.shape, f32),
            jax.ShapeDtypeStruct(up.shape, f32),
        ],
        scratch_shapes=[
            pltpu.VMEM(down.shape, bf16),
            pltpu.VMEM(up.shape, bf16),
            *stores(1, width),
            pltpu.VMEM((2, width // shard_rows, chunks, shard_rows, width), bf16),
            pltpu.SemaphoreType.DMA((2,)),
        ],
        compiler_params=params,
        cost_estimate=cost(0.2),
        name="feed",
    )(bucket, lengths, table, first, out, cotangent, gains, down, up, *pieces, *feed_pieces)


def feed_back_kernel(
    wanted, count, table_ref, third_ref, slope_ref, normal_ref, inverse_ref, adapter_ref, share_ref, gains_ref,
    down_ref, *refs,
):
    pieces, feed_pieces = refs[: 3 * count], refs[3 * count : 4 * count]
    grad_ref, grad_out_ref, down_low, store, sems, feed_store, feed_sems = refs[4 * count :]

    @pl.when(pl.program_id(0) == 0)
    def begin():
        load_feed(feed_pieces, table_ref, (1, 0), feed_store, feed_sems)
        start_loading(pieces, table_ref, wanted, store, sems)
        down_low[...] = down_ref[...].astype(bf16)

    grad_third = third_ref[...]
    grad_feed = grad_third.astype(bf16)
    grad_second = grad_third + contract(adapter_ref[...], down_low[...], 1, 1)
    loaded_once(feed_store, feed_sems, 1)
    loaded_once(feed_store, feed_sems, 0)
    for i in range(feed_store.shape[2]):
        grad_inner = contract(grad_feed, second_block(feed_store, i), 1, 1)
        grad_inner = (grad_inner * slope_ref[i].astype(f32)).astype(bf16)
        grad_second += contract(grad_inner, first_block(feed_store, i), 1, 1)

    grad_pre = normalise_back(
        grad_second * gains_ref[1:2], normal_ref[...].astype(f32), inverse_ref[:, 0:1]
    )
    grad_ref[...] = grad_pre
    loaded_once(store, sems, 0)
    grad_out_ref[...] = (
        contract(grad_pre.astype(bf16), store[0], 1, 1) * spread(share_ref, grad_pre.shape[1])
    ).astype(bf16)


def feed_back(table, third, slope, normal, inverse, adapter, share, gains, down, pieces, output_at, feed_pieces):
    tokens, width = third.shape
    rows = tokens // 4
    chunks, shard_rows = feed_pieces[0].shape[0] // 2, feed_pieces[0].shape[1]
    tile = pl.BlockSpec((rows, width), lambda i: (i, 0))
    fixed = lambda a: pl.BlockSpec(a.shape, lambda i: (0,) * a.ndim, pipeline_mode=pl.Buffered(1))
    return pl.pallas_call(
        functools.partial(feed_back_kernel, (output_at,), len(feed_pieces)),
        grid=(tokens // rows,),
        in_specs=[
            smem(),
            tile,
            pl.BlockSpec((chunks, rows, width), lambda i: (0, i, 0)),
            tile,
            pl.BlockSpec((rows, PAIR), lambda i: (i, 0)),
            pl.BlockSpec((rows, down.shape[1]), lambda i: (i, 0)),
            share_spec(share, rows),
            fixed(gains),
            fixed(down),
        ]
        + [in_place() for piece in pieces + feed_pieces],
        out_specs=[tile, tile],
        out_shape=[
            jax.ShapeDtypeStruct((tokens, width), f32),
            jax.ShapeDtypeStruct((tokens, width), bf16),
        ],
        scratch_shapes=[
            pltpu.VMEM(down.shape, bf16),
            *stores(1, width),
            pltpu.VMEM((2, width // shard_rows, chunks, shard_rows, width), bf16),
            pltpu.SemaphoreType.DMA((2,)),
        ],
        compiler_params=params,
        cost_estimate=cost(0.2),
        name="feed_back",
    )(table, third, slope, normal, inverse, adapter, share, gains, down, *pieces, *feed_pieces)


def cross_back_kernel(
    wanted, table_ref, dq_ref, dk_ref, dv_ref, grad_ref, first_ref, inverse_ref, share_ref, gains_ref,
    *refs,
):
    *pieces, encoder_ref, pre_ref, grad_out_ref, store, sems = refs

    @pl.when(pl.program_id(0) == 0)
    def load():
        start_loading(pieces, table_ref, wanted, store, sems)

    loaded_once(store, sems, 0)
    grad_first = grad_ref[...] + contract(dq_ref[...], store[0], 1, 1)
    loaded_once(store, sems, 1)
    encoder = contract(dk_ref[...], store[1], 1, 1)
    loaded_once(store, sems, 2)
    encoder_ref[...] = (encoder + contract(dv_ref[...], store[2], 1, 1)).astype(bf16)
    gain = gains_ref[0:1]
    grad_pre = normalise_back(grad_first * gain, first_ref[...] / gain, inverse_ref[:, 0:1])
    pre_ref[...] = grad_pre
    loaded_once(store, sems, 3)
    grad_out_ref[...] = (
        contract(grad_pre.astype(bf16), store[3], 1, 1) * spread(share_ref, grad_pre.shape[1])
    ).astype(bf16)


def after_cross_back(dq, dk, dv, grad, first, inverse, share, gains, table, pieces, wanted):
    tokens, width = first.shape
    rows = tokens // 4
    tile = pl.BlockSpec((rows, width), lambda i: (i, 0))
    return pl.pallas_call(
        functools.partial(cross_back_kernel, wanted),
        grid=(tokens // rows,),
        in_specs=[smem()]
        + [tile] * 5
        + [pl.BlockSpec((rows, PAIR), lambda i: (i, 0)), share_spec(share, rows), pl.BlockSpec(gains.shape, lambda i: (0, 0))]
        + [in_place() for piece in pieces],
        out_specs=[tile] * 3,
        out_shape=[
            jax.ShapeDtypeStruct((tokens, width), bf16),
            jax.ShapeDtypeStruct((tokens, width), f32),
            jax.ShapeDtypeStruct((tokens, width), bf16),
        ],
        scratch_shapes=stores(len(wanted), width),
        compiler_params=params,
        cost_estimate=cost(0.2),
        name="after_cross_back",
    )(table, dq, dk, dv, grad, first, inverse, share, gains, *pieces)


def input_kernel(wanted, table_ref, dq_ref, dk_ref, dv_ref, pre_ref, *refs):
    *pieces, out_ref, store, sems = refs

    @pl.when(pl.program_id(0) == 0)
    def load():
        start_loading(pieces, table_ref, wanted, store, sems)

    total = pre_ref[...]
    for slot, ref in enumerate((dq_ref, dk_ref, dv_ref)):
        loaded_once(store, sems, slot)
        total += contract(ref[...], store[slot], 1, 1)
    out_ref[...] = total.astype(bf16)


def input_gradient(dq, dk, dv, pre, table, pieces, wanted):
    tokens, width = pre.shape
    rows = tokens // 4
    tile = pl.BlockSpec((rows, width), lambda i: (i, 0))
    return pl.pallas_call(
        functools.partial(input_kernel, wanted),
        grid=(tokens // rows,),
        in_specs=[smem()] + [tile] * 4 + [in_place() for piece in pieces],
        out_specs=tile,
        out_shape=jax.ShapeDtypeStruct((tokens, width), bf16),
        scratch_shapes=stores(len(wanted), width),
        compiler_params=params,
        cost_estimate=cost(0.2),
        name="input_gradient",
    )(table, dq, dk, dv, pre, *pieces)


def adamw(master, first_moment, second_moment, gradient):
    first_new = beta_first * first_moment + (1.0 - beta_first) * gradient
    second_new = beta_second * second_moment + (1.0 - beta_second) * gradient * gradient
    first_hat = first_new / (1.0 - beta_first**STEP)
    second_hat = second_new / (1.0 - beta_second**STEP)
    master_new = master - learn_rate * (
        first_hat / (jnp.sqrt(second_hat) + epsilon_adam) + weight_decay * master
    )
    return (first_new, second_new, master_new)


def pack_kernel(*refs):
    *shards, out_ref = refs
    for i, shard in enumerate(shards):
        out_ref[i] = shard[...]


def pack(shards):
    return pl.pallas_call(
        pack_kernel,
        out_shape=jax.ShapeDtypeStruct((len(shards),) + shards[0].shape, bf16),
        compiler_params=params,
        cost_estimate=cost(2),
        name="pack",
    )(*shards)


def pack_pair_kernel(table_ref, *refs):
    *shards, own_ref, other_ref = refs
    half = len(shards) // 2

    def both(first_ref, second_ref):
        for i in range(half):
            first_ref[i] = shards[i][...]
            second_ref[i] = shards[half + i][...]

    pl.when(table_ref[3, 0] == 0)(functools.partial(both, own_ref, other_ref))
    pl.when(table_ref[3, 0] != 0)(functools.partial(both, other_ref, own_ref))


def pack_pair(table, shards):
    shape = jax.ShapeDtypeStruct((len(shards) // 2,) + shards[0].shape, bf16)
    vmem = pl.BlockSpec(memory_space=pltpu.VMEM)
    return pl.pallas_call(
        pack_pair_kernel,
        in_specs=[smem()] + [vmem] * len(shards),
        out_specs=[vmem, vmem],
        out_shape=[shape, shape],
        compiler_params=params,
        cost_estimate=cost(2),
        name="pack_pair",
    )(table, *shards)


def pack_feed_kernel(first_ref, second_ref, out_ref):
    blocks, rows, width = out_ref.shape
    blocks //= 2
    for i in range(blocks):
        out_ref[i] = first_ref[:, i * width : (i + 1) * width]
        out_ref[blocks + i] = second_ref[i * rows : (i + 1) * rows]


def pack_feed(first, second):
    rows, width = first.shape[0], second.shape[1]
    blocks = (first.size + second.size) // (rows * width)
    return pl.pallas_call(
        pack_feed_kernel,
        out_shape=jax.ShapeDtypeStruct((blocks, rows, width), bf16),
        compiler_params=params,
        cost_estimate=cost(3),
        name="pack_feed",
    )(first, second)


def after_kernel(*refs):
    done_ref = refs[-1]
    done_ref[0] = 0


def after(values, *sooner):
    if not sooner:
        return values
    return pl.pallas_call(
        after_kernel,
        in_specs=[in_place()] * (1 + len(sooner)),
        out_specs=[in_place(), smem()],
        out_shape=[jax.ShapeDtypeStruct(values.shape, values.dtype), jax.ShapeDtypeStruct((1,), jnp.int32)],
        input_output_aliases={0: 0},
        compiler_params=params,
        cost_estimate=cost(0.01),
        name="after",
    )(values, *sooner)[0]


AXES = ("fsdp", "dp")


def ring_order(size):
    return list(range(0, size, 2)) + list(range(size - 1, 0, -2))


class Links:
    def __init__(self, shard_rows):
        self.size, self.parts = lax.axis_size("fsdp"), lax.axis_size("dp")
        order = ring_order(self.size)
        after = {order[i]: order[(i + 1) % self.size] for i in range(self.size)}
        before = {later: sooner for sooner, later in after.items()}
        every = [(f, d) for f in range(self.size) for d in range(self.parts)]
        flat = lambda f, d: f * self.parts + d
        self.onward = [(flat(f, d), flat((before if d % 2 else after)[f], d)) for f, d in every]
        self.sibling = [(flat(f, d), flat(f, d ^ 1)) for f, d in every]
        self.across = [(flat(f, d), flat(f, d ^ 2)) for f, d in every]
        self.core = lax.axis_index("dp") % 2
        self.hops = self.size // 2

        rows, table = shard_rows, []
        for f, d in every:
            place, core, plane = order.index(f), d % 2, d // 2 % 2
            toward = 1 - 2 * core
            shards, inside = [f], [0]
            for hop in range(1, self.hops + 1):
                for sign in (-1, 1):
                    shards.append(order[(place + sign * toward * hop) % self.size])
                    late = core if sign == -1 else 1 - core
                    inside.append(late * (rows // 2) if hop == self.hops else 0)
            first = [shard * rows + at for shard, at in zip(shards, inside)]
            table.append([first, shards, inside, [plane] * len(first)])
        self.table = lax.dynamic_index_in_dim(
            jnp.array(table, jnp.int32), lax.axis_index(AXES), 0, keepdims=False
        )

    def send(self, values, pairs):
        return lax.ppermute(values, AXES, pairs)

    def last(self, values):
        half = values.shape[1] // 2
        return lax.dynamic_slice_in_dim(values, self.core * half, half, 1)


class Gather:
    def __init__(self, links, own, other=None):
        self.links, self.moving, self.count, self.quarter, self.pieces = links, own, 0, 0, []
        self.rest = [] if other is None else [other]

    def share(self, *sooner):
        self.moving = after(self.moving, *sooner)
        self.shared = self.moving
        self.pieces.append(self.moving)
        if self.count:
            self.pieces.append(self.links.send(self.moving, self.links.sibling))
            if self.rest:
                self.crossed = self.links.send(self.moving, self.links.across)
                if self.count < self.links.hops:
                    self.hand_over()

    def hand_over(self, *sooner):
        crossed = after(self.crossed, *sooner)
        self.rest += [crossed, self.links.send(crossed, self.links.sibling)]

    def hop(self, *sooner, chained=False):
        links = self.links
        self.quarter += 1
        while self.count < self.quarter * links.hops // 4:
            if chained and len(self.pieces) > 1:
                sooner = (*sooner, self.pieces[-1], *self.rest[2:][-1:])
            self.share(*sooner)
            sooner = ()
            self.count += 1
            moving = links.last(self.moving) if self.count == links.hops else self.moving
            self.moving = links.send(moving, links.onward)


def body(
    inputs, encoder, cotangent, buckets, lengths, self_query, self_key, self_value, self_output,
    cross_query, cross_key, cross_value, cross_output, fc_first, fc_second, norm_gains,
    down_master, up_master, down_first, down_second, up_first, up_second,
):
    rows, width = self_query.shape
    links = Links(rows)
    table = links.table
    sq, sk, sv, so = ((None, i) for i in range(4))
    ck, cv, cq, co = (0, 0), (0, 1), (1, 0), (1, 1)
    one = Gather(links, pack((self_query, self_key, self_value, self_output)))
    two = Gather(links, *pack_pair(table, (cross_key, cross_value, cross_query, cross_output)))
    two_own = two.moving
    one.hop(chained=True)
    two.hop(chained=True)
    one.hop(two_own, chained=True)
    two.hop(chained=True)
    for quarter in range(2):
        one.hop(chained=True)
        two.hop(chained=True)
    one.share()
    two.share()
    late = Gather(links, pack_feed(fc_first, fc_second))
    late.hop(one.moving, two.moving)

    qkv, squares = project(inputs, table, one.pieces * 3, (sq, sk, sv), query_scale, 2, (late.shared,))
    two.hand_over(squares)
    pieces = one.pieces + two.pieces + two.rest
    kv, kv_squares = project(encoder, table, two.pieces + two.pieces + two.rest, (ck, cv), 1.0, 1, (squares,))
    self_packs = [(qkv, squares, 0), (qkv, squares, 1), (qkv, None, 2)]
    half = width // PAIR // 2
    late.hop(squares, kv_squares)
    *self_half, done = attend(buckets, lengths, *self_packs, True, 0, half, (), (late.shared,))
    self_out, self_weight, self_share, done = attend(
        buckets, lengths, *self_packs, True, half, 2 * half, self_half
    )
    late.hop(done)
    first, first_inverse, query_cross, query_squares = after_self(
        inputs, self_out, norm_gains, table, pieces, (so, cq), (late.shared,)
    )
    cross_packs = [(query_cross, query_squares, 0), (kv, kv_squares, 0), (kv, None, 1)]
    *cross_half, done = attend(buckets, lengths, *cross_packs, False, 0, half)
    late.hop(done)
    cross_out, cross_weight, cross_share, done = attend(
        buckets, lengths, *cross_packs, False, half, 2 * half, cross_half, (late.shared,)
    )
    late.share(done)

    outputs, grad_third, slope, second_normal, second_inverse, adapter, down_local, up_local = feed(
        buckets, lengths, table, first, cross_out, cotangent, norm_gains, down_master, up_master, pieces, co,
        late.pieces,
    )
    down_grad, up_grad = lax.psum((down_local, up_local), ("fsdp", "dp"))

    grad_cross_pre, grad_cross_out = feed_back(
        table, grad_third, slope, second_normal, second_inverse, adapter, cross_share, norm_gains, down_master,
        pieces, co, late.pieces,
    )
    dq, dk, dv = attend_back(*cross_packs, grad_cross_out, cross_out, cross_weight, False)
    encoder_grad, grad_self_pre, grad_self_out = after_cross_back(
        dq, dk, dv, grad_cross_pre, first, first_inverse, self_share, norm_gains, table, pieces, (cq, ck, cv, so)
    )
    dq, dk, dv = attend_back(*self_packs, grad_self_out, self_out, self_weight, True)
    input_grad = input_gradient(dq, dk, dv, grad_self_pre, table, pieces, (sq, sk, sv))

    down_first_new, down_second_new, down_master_new = adamw(
        down_master, down_first, down_second, down_grad
    )
    up_first_new, up_second_new, up_master_new = adamw(up_master, up_first, up_second, up_grad)
    return (
        outputs,
        input_grad,
        encoder_grad,
        down_grad,
        up_grad,
        down_first_new,
        down_second_new,
        up_first_new,
        up_second_new,
        down_master_new,
        up_master_new,
        down_master_new.astype(bf16),
        up_master_new.astype(bf16),
    )


def solution(mesh):
    tokens, matrix = P(("fsdp", "dp"), None), P("fsdp", None)
    return jax.shard_map(
        body,
        mesh=mesh,
        in_specs=(tokens, tokens, tokens, P(("fsdp", "dp")), tokens) + (matrix,) * 10 + (P(),) * 7,
        out_specs=(tokens,) * 3 + (P(),) * 10,
        check_vma=False,
    )
```

```python
import functools
import math

import jax
import jax.numpy as jnp
from jax import lax
from jax.experimental import pallas as pl
from jax.experimental.pallas import tpu as pltpu
from jax.sharding import PartitionSpec as P

HEAD_DIM = 64
PAIR = 2 * HEAD_DIM
STEP = 10
SLOTS = 4

epsilon_norm = 1e-05
beta_first = 0.9
beta_second = 0.999
learn_rate = 0.05
weight_decay = 0.01
epsilon_adam = 1e-08

f32, bf16 = jnp.float32, jnp.bfloat16
query_scale = HEAD_DIM ** (-0.5) * math.log2(math.e)
forbidden = -(2.0**100)
least_sum, most_sum = 2.0**-40, 2.0**60

params = pltpu.CompilerParams(vmem_limit_bytes=63 * 2**20)


def contract(left, right, left_dim, right_dim):
    return lax.dot_general(
        left, right, (((left_dim,), (right_dim,)), ((), ())), preferred_element_type=f32
    )


def start_loading(pieces, table_ref, wanted, store, sems, start=0):
    count = len(pieces) // 3

    def copies(group, slot, i):
        for p, piece in enumerate(pieces[group * count : (group + 1) * count]):
            rows = piece.shape[1]
            at = pl.multiple_of(table_ref[0, p], 16)
            pltpu.make_async_copy(
                piece.at[i], store.at[slot, pl.ds(at, rows)], sems.at[slot]
            ).start()

    for slot, (kind, i) in list(enumerate(wanted))[start:]:
        if kind is None:
            copies(0, slot, i)
        else:
            pl.when(table_ref[3, 0] == kind)(functools.partial(copies, 1, slot, i))
            pl.when(table_ref[3, 0] != kind)(functools.partial(copies, 2, slot, i))


def loaded(store, sems, slot):
    pltpu.make_async_copy(store.at[slot], store.at[slot], sems.at[slot]).wait()


def loaded_once(store, sems, slot):
    @pl.when(pl.program_id(0) == 0)
    def wait():
        loaded(store, sems, slot)


def cost(microseconds):
    return pl.CostEstimate(flops=int(microseconds * 1.15e9), bytes_accessed=10**5, transcendentals=0)


def share_spec(share, rows):
    return pl.BlockSpec(share.shape[:2] + (rows,), lambda i: (0, 0, i))


def in_place():
    return pl.BlockSpec(memory_space=pl.ANY)


def stores(count, width):
    return [pltpu.VMEM((count, width, width), bf16), pltpu.SemaphoreType.DMA((count,))]


smem = functools.partial(pl.BlockSpec, memory_space=pltpu.SMEM)


def spread(share_ref, width):
    pairs, two, rows = share_ref.shape
    rest = share_ref[...].reshape(pairs * two, rows)
    member = (
        lax.broadcasted_iota(jnp.int32, (pairs * two, width), 0)
        == lax.broadcasted_iota(jnp.int32, (pairs * two, width), 1) >> 6
    ).astype(bf16)
    parts = []
    for i in range(3):
        parts.append(rest.astype(bf16))
        rest = rest - parts[-1].astype(f32)
    return contract(jnp.concatenate(parts, axis=0), jnp.concatenate([member] * 3, axis=0), 0, 0)


def normalise(values):
    centre = values - jnp.mean(values, axis=-1, keepdims=True)
    inverse = lax.rsqrt(jnp.mean(centre * centre, axis=-1, keepdims=True) + epsilon_norm)
    return centre * inverse, inverse


def normalise_back(scaled, normal, inverse):
    return inverse * (
        scaled
        - jnp.mean(scaled, axis=-1, keepdims=True)
        - normal * jnp.mean(scaled * normal, axis=-1, keepdims=True)
    )


def gelu_and_slope(u):
    bell = jnp.exp2(u * u * (-0.5 * math.log2(math.e)) - 0.5 * math.log2(2.0 * math.pi))
    below = 0.5 + 0.5 * lax.erf(u * math.sqrt(0.5))
    return u * below, below + u * bell


def project_kernel(wanted, scale, count, x_ref, table_ref, *refs):
    pieces = refs[:count]
    out_ref, store, sems = refs[-3:]
    step = pl.program_id(0)

    @pl.when(step == 0)
    def begin():
        start_loading(pieces, table_ref, wanted[:1], store, sems)
        loaded(store, sems, 0)
        start_loading(pieces, table_ref, wanted, store, sems, 1)
        out = contract(x_ref[...], store[0], 1, 0)
        out_ref[0] = (out if scale == 1.0 else out * scale).astype(bf16)

    @pl.when(step > 0)
    def more():
        loaded(store, sems, step)
        out_ref[0] = contract(x_ref[...], store[step], 1, 0).astype(bf16)


def project(x, table, pieces, wanted, scale, sooner=()):
    tokens, width = x.shape
    count = len(wanted)
    return pl.pallas_call(
        functools.partial(project_kernel, wanted, scale, len(pieces)),
        grid=(count,),
        in_specs=[pl.BlockSpec((tokens, width), lambda i: (0, 0)), smem()]
        + [in_place() for piece in (*pieces, *sooner)],
        out_specs=pl.BlockSpec((1, tokens, width), lambda i: (i, 0, 0)),
        out_shape=jax.ShapeDtypeStruct((count, tokens, width), bf16),
        scratch_shapes=stores(count, width),
        compiler_params=params,
        cost_estimate=cost(4 * count),
        name="project",
    )(x, table, *pieces, *sooner)


def low_half(rows):
    return lax.broadcasted_iota(jnp.int32, (rows, PAIR), 1) < HEAD_DIM


def choose(head, low):
    if head == 0:
        return lambda own, other: jnp.where(low, own, other)
    return lambda own, other: jnp.where(low, other, own)


def item_shift(bucket, tokens):
    return bucket + (tokens.bit_length() - 1 - 2)


def item_length(item, lengths_ref):
    length = jnp.zeros_like(item)
    for slot in range(SLOTS):
        length = jnp.where(item == slot, lengths_ref[0, slot], length)
    return length


def attend_kernel(
    causal, bucket_ref, lengths_ref, q_ref, k_ref, v_ref, *refs
):
    out_ref, weight_ref, share_ref, done_ref, qmark, kmark = refs[-6:]
    done_ref[...] = jnp.zeros_like(done_ref)
    tokens = q_ref.shape[-2]
    low = low_half(tokens)

    @pl.when(pl.program_id(0) == 0)
    def marks():
        shift = item_shift(bucket_ref[0], tokens)
        lane = lax.broadcasted_iota(jnp.int32, (tokens, PAIR), 1) & (HEAD_DIM - 1)
        row = lax.broadcasted_iota(jnp.int32, (tokens, PAIR), 0)
        item = row >> shift
        own = lane == item
        qmark[...] = jnp.where(own, 1.0, 0.0).astype(bf16)
        allowed = own & (row - (item << shift) < item_length(item, lengths_ref))
        kmark[...] = jnp.where((lane < SLOTS) & ~allowed, forbidden, 0.0).astype(bf16)

    q, k, v = q_ref[0], k_ref[0], v_ref[0]
    one = jnp.ones((tokens, PAIR), bf16)

    def operands(head):
        own = choose(head, low)
        return own(q, qmark[...]), own(k, kmark[...]), own(v, one)

    def finish(sums):
        even, odd = sums
        even_share, odd_share = 1.0 / even[HEAD_DIM : HEAD_DIM + 8], 1.0 / odd[:8]
        out = jnp.concatenate(
            [even[:HEAD_DIM] * even_share[:1], odd[HEAD_DIM:] * odd_share[:1]], axis=0
        )
        out_ref[...] = out.astype(bf16).T
        share_ref[0, 0:1] = even_share[:1]
        share_ref[0, 1:2] = odd_share[:1]
        return even[HEAD_DIM : HEAD_DIM + 1], odd[:1]

    def direct():
        sums = []
        for head in range(2):
            queries, keys, values = operands(head)
            if not causal:
                weight = jnp.exp2(contract(keys, queries, 1, 1)).astype(bf16)
                weight_ref[head] = weight
                sums.append(contract(values, weight, 0, 0))
                continue
            step = tokens // 2
            before = lax.broadcasted_iota(jnp.int32, (step, step), 0) <= lax.broadcasted_iota(
                jnp.int32, (step, step), 1
            )
            nothing = jnp.zeros((), bf16)
            top = jnp.exp2(contract(keys[:step], queries, 1, 1)).astype(bf16)
            top = jnp.concatenate(
                [jnp.where(before, top[:, :step], nothing), top[:, step:]], axis=1
            )
            weight_ref[head, :step] = top
            total = contract(values[:step], top, 0, 0)
            low_part = jnp.exp2(contract(keys[step:], queries[step:], 1, 1)).astype(bf16)
            low_part = jnp.where(before, low_part, nothing)
            weight_ref[head, step:, step:] = low_part
            rest = contract(values[step:], low_part, 0, 0)
            sums.append(jnp.concatenate([total[:, :step], total[:, step:] + rest], axis=1))
        return finish(sums)

    totals = jnp.concatenate(direct(), axis=0)
    sound = (jnp.min(totals) >= least_sum) & (jnp.max(totals) <= most_sum)

    @pl.when(jnp.logical_not(sound))
    def shifted():
        sums = []
        for head in range(2):
            queries, keys, values = operands(head)
            scores = contract(keys, queries, 1, 1)
            if causal:
                before = lax.broadcasted_iota(
                    jnp.int32, scores.shape, 0
                ) <= lax.broadcasted_iota(jnp.int32, scores.shape, 1)
                scores = jnp.where(before, scores, forbidden)
            scores = scores - jnp.max(scores, axis=0, keepdims=True)
            weight = jnp.exp2(scores).astype(bf16)
            weight_ref[head] = weight
            sums.append(contract(values, weight, 0, 0))
        finish(sums)


def attend(bucket, lengths, q_pack, k_pack, v_pack, causal, start, stop, so_far=(), sooner=()):
    (q, q_at), (k, k_at), (v, v_at) = q_pack, k_pack, v_pack
    tokens, width = q.shape[1:]
    pairs = width // PAIR
    pair_spec = lambda at: pl.BlockSpec((1, tokens, PAIR), lambda j: (at, 0, start + j))
    flat_spec = pl.BlockSpec((tokens, PAIR), lambda j: (0, start + j))
    return pl.pallas_call(
        functools.partial(attend_kernel, causal),
        grid=(stop - start,),
        in_specs=[smem(), smem(), pair_spec(q_at), pair_spec(k_at), pair_spec(v_at)]
        + [in_place() for array in (*so_far, *sooner)],
        out_specs=[
            flat_spec,
            pl.BlockSpec((2, tokens, tokens), lambda j: (start + j, 0, 0)),
            pl.BlockSpec((1, 2, tokens), lambda j: (start + j, 0, 0)),
            pl.BlockSpec((8, PAIR), lambda j: (0, 0)),
        ],
        out_shape=[
            jax.ShapeDtypeStruct((tokens, width), bf16),
            jax.ShapeDtypeStruct((2 * pairs, tokens, tokens), bf16),
            jax.ShapeDtypeStruct((pairs, 2, tokens), f32),
            jax.ShapeDtypeStruct((8, PAIR), f32),
        ],
        input_output_aliases={5 + i: i for i in range(len(so_far))},
        scratch_shapes=[pltpu.VMEM((tokens, PAIR), bf16), pltpu.VMEM((tokens, PAIR), bf16)],
        compiler_params=params,
        cost_estimate=cost(0.05 * (stop - start)),
        name="attend",
    )(bucket, lengths, q, k, v, *so_far, *sooner)


def attend_back_kernel(
    causal, q_ref, k_ref, v_ref, grad_ref, out_ref, weight_ref, dq_ref, dk_ref, dv_ref
):
    tokens = q_ref.shape[-2]
    low = low_half(tokens)
    q, k, v, grad = q_ref[0], k_ref[0], v_ref[0], grad_ref[...]
    nothing = jnp.zeros((tokens, PAIR), bf16)
    minus = jnp.full((tokens, PAIR), -1.0, bf16)
    swap = (
        (lax.broadcasted_iota(jnp.int32, (PAIR, PAIR), 0) < HEAD_DIM)
        != (lax.broadcasted_iota(jnp.int32, (PAIR, PAIR), 1) < HEAD_DIM)
    ).astype(bf16)
    product = grad.astype(f32) * out_ref[...].astype(f32)
    high = product.astype(bf16)
    centre = contract(high, swap, 1, 0) + contract((product - high.astype(f32)).astype(bf16), swap, 1, 0)
    high = centre.astype(bf16)
    rest = (centre - high.astype(f32)).astype(bf16)
    lane = lax.broadcasted_iota(jnp.int32, (tokens, PAIR), 1) & (HEAD_DIM - 1)
    centre = jnp.where(lane == 0, high, jnp.where(lane == 1, rest, nothing))

    step = tokens // 2 if causal else tokens
    dq_turned = None
    for tile in range(tokens // step):
        at = tile * step
        rows = slice(at, at + step)
        dk = dv = None
        turned = []
        for head in range(2):
            own = choose(head, low)
            weight = weight_ref[head, rows, at:]
            dweight = contract(own(v, minus)[rows], own(grad, centre)[at:], 1, 1)
            dscore = weight * dweight.astype(bf16)
            dv_own = contract(weight, own(grad, nothing)[at:], 1, 0)
            dk_own = contract(dscore, own(q, nothing)[at:], 1, 0)
            dv = dv_own if head == 0 else dv + dv_own
            dk = dk_own if head == 0 else dk + dk_own
            turned.append(contract(k[rows], dscore, 0, 0)[head * HEAD_DIM : (head + 1) * HEAD_DIM])
        dv_ref[rows] = dv.astype(bf16)
        dk_ref[rows] = (dk * math.log(2.0)).astype(bf16)
        turned = jnp.concatenate(turned, axis=0)
        if tile == 0:
            dq_turned = turned
        else:
            dq_turned = jnp.concatenate([dq_turned[:, :at], dq_turned[:, at:] + turned], axis=1)
    dq_ref[...] = (dq_turned * HEAD_DIM ** (-0.5)).T.astype(bf16)


def attend_back(q_pack, k_pack, v_pack, grad, out, weight, causal):
    (q, q_at), (k, k_at), (v, v_at) = q_pack, k_pack, v_pack
    tokens, width = q.shape[1:]
    pairs = width // PAIR
    pair_spec = lambda at: pl.BlockSpec((1, tokens, PAIR), lambda j: (at, 0, j))
    flat_spec = pl.BlockSpec((tokens, PAIR), lambda j: (0, j))
    return pl.pallas_call(
        functools.partial(attend_back_kernel, causal),
        grid=(pairs,),
        in_specs=[
            pair_spec(q_at),
            pair_spec(k_at),
            pair_spec(v_at),
            flat_spec,
            flat_spec,
            pl.BlockSpec((2, tokens, tokens), lambda j: (j, 0, 0)),
        ],
        out_specs=[flat_spec] * 3,
        out_shape=[jax.ShapeDtypeStruct((tokens, width), bf16)] * 3,
        compiler_params=params,
        cost_estimate=cost(0.2),
        name="attend_back",
    )(q, k, v, grad, out, weight)


def first_kernel(wanted, count, table_ref, x_ref, out_ref, gains_ref, *refs):
    pieces = refs[:count]
    first_ref, inverse_ref, q_ref, store, sems = refs[-5:]
    step = pl.program_id(0)

    @pl.when(step == 0)
    def load():
        start_loading(pieces, table_ref, wanted, store, sems)

    loaded_once(store, sems, 0)
    z = x_ref[...].astype(f32) + contract(out_ref[...], store[0], 1, 0)
    normal, inverse = normalise(z)
    first = normal * gains_ref[0:1]
    first_ref[...] = first
    inverse_ref[...] = jnp.broadcast_to(inverse, inverse_ref.shape)
    loaded_once(store, sems, 1)
    q = (contract(first.astype(bf16), store[1], 1, 0) * query_scale).astype(bf16)
    q_ref[0] = q


def after_self(x, out, gains, table, pieces, wanted, sooner):
    tokens, width = x.shape
    rows = tokens // 4
    tile = pl.BlockSpec((rows, width), lambda i: (i, 0))
    return pl.pallas_call(
        functools.partial(first_kernel, wanted, len(pieces)),
        grid=(tokens // rows,),
        in_specs=[smem(), tile, tile, pl.BlockSpec(gains.shape, lambda i: (0, 0))]
        + [in_place() for piece in (*pieces, *sooner)],
        out_specs=[
            tile,
            pl.BlockSpec((rows, PAIR), lambda i: (i, 0)),
            pl.BlockSpec((1, rows, width), lambda i: (0, i, 0)),
        ],
        out_shape=[
            jax.ShapeDtypeStruct((tokens, width), f32),
            jax.ShapeDtypeStruct((tokens, PAIR), f32),
            jax.ShapeDtypeStruct((1, tokens, width), bf16),
        ],
        scratch_shapes=stores(len(wanted), width),
        compiler_params=params,
        cost_estimate=cost(0.2),
        name="after_self",
    )(table, x, out, gains, *pieces, *sooner)


def load_feed(feed_pieces, table_ref, kinds, feed_store, feed_sems):
    blocks = feed_store.shape[2]
    for kind in kinds:
        for p, piece in enumerate(feed_pieces):
            rows_at = pl.ds(pl.multiple_of(table_ref[2, p], 16), piece.shape[1])
            pltpu.make_async_copy(
                piece.at[pl.ds(kind * blocks, blocks)],
                feed_store.at[kind, table_ref[1, p], :, rows_at],
                feed_sems.at[kind],
            ).start()


def first_block(feed_store, i):
    return feed_store[0, :, i].reshape(-1, feed_store.shape[-1])


def second_block(feed_store, i):
    devices, blocks = feed_store.shape[1:3]
    return feed_store[1, i * devices // blocks : (i + 1) * devices // blocks].reshape(
        -1, feed_store.shape[-1]
    )


def feed_kernel(
    wanted, count, bucket_ref, lengths_ref, table_ref, first_ref, out_ref, cotangent_ref, gains_ref, down_ref,
    up_ref, *refs,
):
    pieces, feed_pieces = refs[: 3 * count], refs[3 * count : 4 * count]
    (outputs_ref, third_ref, slope_ref, normal_ref, inverse_ref, adapter_ref, down_grad_ref, up_grad_ref,
     down_low, up_low, store, sems, feed_store, feed_sems) = refs[4 * count :]
    rows, width = first_ref.shape
    tokens = rows * pl.num_programs(0)
    step = pl.program_id(0)

    @pl.when(step == 0)
    def begin():
        start_loading(pieces, table_ref, wanted, store, sems)
        load_feed(feed_pieces, table_ref, (0, 1), feed_store, feed_sems)
        down_low[...] = down_ref[...].astype(bf16)
        up_low[...] = up_ref[...].astype(bf16)
        down_grad_ref[...] = jnp.zeros_like(down_grad_ref)
        up_grad_ref[...] = jnp.zeros_like(up_grad_ref)

    loaded_once(store, sems, 0)
    z = first_ref[...] + contract(out_ref[...], store[0], 1, 0)
    second_normal, second_inverse = normalise(z)
    normal_ref[...] = second_normal.astype(bf16)
    inverse_ref[...] = jnp.broadcast_to(second_inverse, inverse_ref.shape)
    second = second_normal * gains_ref[1:2]
    second_low = second.astype(bf16)

    adapter_act, adapter_slope = gelu_and_slope(contract(second_low, down_low[...], 1, 0))
    adapter_act = adapter_act.astype(bf16)
    total = second + 4.0 * contract(adapter_act, up_low[...], 1, 0)
    loaded_once(feed_store, feed_sems, 0)
    loaded_once(feed_store, feed_sems, 1)
    for i in range(feed_store.shape[2]):
        active, slope = gelu_and_slope(contract(second_low, first_block(feed_store, i), 1, 0))
        slope_ref[i] = slope.astype(bf16)
        total += contract(active.astype(bf16), second_block(feed_store, i), 1, 0)

    third_normal, third_inverse = normalise(total)
    outputs_ref[...] = (third_normal * gains_ref[2:3]).astype(bf16)

    shift = item_shift(bucket_ref[0], tokens)
    row = lax.broadcasted_iota(jnp.int32, (rows, 1), 0) + step * rows
    item = row >> shift
    valid = row - (item << shift) < item_length(item, lengths_ref)
    upstream = jnp.where(valid, cotangent_ref[...].astype(f32), 0.0)
    grad_third = normalise_back(upstream * gains_ref[2:3], third_normal, third_inverse)
    third_ref[...] = grad_third

    grad_adapter_out = (4.0 * grad_third).astype(bf16)
    up_grad_ref[...] += contract(adapter_act, grad_adapter_out, 0, 0)
    grad_adapter_pre = (contract(grad_adapter_out, up_low[...], 1, 1) * adapter_slope).astype(bf16)
    adapter_ref[...] = grad_adapter_pre
    down_grad_ref[...] += contract(second_low, grad_adapter_pre, 0, 0)


def feed(bucket, lengths, table, first, out, cotangent, gains, down, up, pieces, output_at, feed_pieces):
    tokens, width = first.shape
    rows = tokens // 4
    chunks, shard_rows = feed_pieces[0].shape[0] // 2, feed_pieces[0].shape[1]
    tile = pl.BlockSpec((rows, width), lambda i: (i, 0))
    fixed = lambda a: pl.BlockSpec(a.shape, lambda i: (0,) * a.ndim, pipeline_mode=pl.Buffered(1))
    return pl.pallas_call(
        functools.partial(feed_kernel, (output_at,), len(feed_pieces)),
        grid=(tokens // rows,),
        in_specs=[smem(), smem(), smem(), tile, tile, tile, fixed(gains), fixed(down), fixed(up)]
        + [in_place() for piece in pieces + feed_pieces],
        out_specs=[
            tile,
            tile,
            pl.BlockSpec((chunks, rows, width), lambda i: (0, i, 0)),
            tile,
            pl.BlockSpec((rows, PAIR), lambda i: (i, 0)),
            pl.BlockSpec((rows, down.shape[1]), lambda i: (i, 0)),
            fixed(down),
            fixed(up),
        ],
        out_shape=[
            jax.ShapeDtypeStruct((tokens, width), bf16),
            jax.ShapeDtypeStruct((tokens, width), f32),
            jax.ShapeDtypeStruct((chunks, tokens, width), bf16),
            jax.ShapeDtypeStruct((tokens, width), bf16),
            jax.ShapeDtypeStruct((tokens, PAIR), f32),
            jax.ShapeDtypeStruct((tokens, down.shape[1]), bf16),
            jax.ShapeDtypeStruct(down.shape, f32),
            jax.ShapeDtypeStruct(up.shape, f32),
        ],
        scratch_shapes=[
            pltpu.VMEM(down.shape, bf16),
            pltpu.VMEM(up.shape, bf16),
            *stores(1, width),
            pltpu.VMEM((2, width // shard_rows, chunks, shard_rows, width), bf16),
            pltpu.SemaphoreType.DMA((2,)),
        ],
        compiler_params=params,
        cost_estimate=cost(0.2),
        name="feed",
    )(bucket, lengths, table, first, out, cotangent, gains, down, up, *pieces, *feed_pieces)


def feed_back_kernel(
    wanted, count, table_ref, third_ref, slope_ref, normal_ref, inverse_ref, adapter_ref, share_ref, gains_ref,
    down_ref, *refs,
):
    pieces, feed_pieces = refs[: 3 * count], refs[3 * count : 4 * count]
    grad_ref, grad_out_ref, down_low, store, sems, feed_store, feed_sems = refs[4 * count :]

    @pl.when(pl.program_id(0) == 0)
    def begin():
        load_feed(feed_pieces, table_ref, (1, 0), feed_store, feed_sems)
        start_loading(pieces, table_ref, wanted, store, sems)
        down_low[...] = down_ref[...].astype(bf16)

    grad_third = third_ref[...]
    grad_feed = grad_third.astype(bf16)
    grad_second = grad_third + contract(adapter_ref[...], down_low[...], 1, 1)
    loaded_once(feed_store, feed_sems, 1)
    loaded_once(feed_store, feed_sems, 0)
    for i in range(feed_store.shape[2]):
        grad_inner = contract(grad_feed, second_block(feed_store, i), 1, 1)
        grad_inner = (grad_inner * slope_ref[i].astype(f32)).astype(bf16)
        grad_second += contract(grad_inner, first_block(feed_store, i), 1, 1)

    grad_pre = normalise_back(
        grad_second * gains_ref[1:2], normal_ref[...].astype(f32), inverse_ref[:, 0:1]
    )
    grad_ref[...] = grad_pre
    loaded_once(store, sems, 0)
    grad_out_ref[...] = (
        contract(grad_pre.astype(bf16), store[0], 1, 1) * spread(share_ref, grad_pre.shape[1])
    ).astype(bf16)


def feed_back(table, third, slope, normal, inverse, adapter, share, gains, down, pieces, output_at, feed_pieces):
    tokens, width = third.shape
    rows = tokens // 4
    chunks, shard_rows = feed_pieces[0].shape[0] // 2, feed_pieces[0].shape[1]
    tile = pl.BlockSpec((rows, width), lambda i: (i, 0))
    fixed = lambda a: pl.BlockSpec(a.shape, lambda i: (0,) * a.ndim, pipeline_mode=pl.Buffered(1))
    return pl.pallas_call(
        functools.partial(feed_back_kernel, (output_at,), len(feed_pieces)),
        grid=(tokens // rows,),
        in_specs=[
            smem(),
            tile,
            pl.BlockSpec((chunks, rows, width), lambda i: (0, i, 0)),
            tile,
            pl.BlockSpec((rows, PAIR), lambda i: (i, 0)),
            pl.BlockSpec((rows, down.shape[1]), lambda i: (i, 0)),
            share_spec(share, rows),
            fixed(gains),
            fixed(down),
        ]
        + [in_place() for piece in pieces + feed_pieces],
        out_specs=[tile, tile],
        out_shape=[
            jax.ShapeDtypeStruct((tokens, width), f32),
            jax.ShapeDtypeStruct((tokens, width), bf16),
        ],
        scratch_shapes=[
            pltpu.VMEM(down.shape, bf16),
            *stores(1, width),
            pltpu.VMEM((2, width // shard_rows, chunks, shard_rows, width), bf16),
            pltpu.SemaphoreType.DMA((2,)),
        ],
        compiler_params=params,
        cost_estimate=cost(0.2),
        name="feed_back",
    )(table, third, slope, normal, inverse, adapter, share, gains, down, *pieces, *feed_pieces)


def cross_back_kernel(
    wanted, table_ref, dq_ref, dk_ref, dv_ref, grad_ref, first_ref, inverse_ref, share_ref, gains_ref,
    *refs,
):
    *pieces, encoder_ref, pre_ref, grad_out_ref, store, sems = refs

    @pl.when(pl.program_id(0) == 0)
    def load():
        start_loading(pieces, table_ref, wanted, store, sems)

    loaded_once(store, sems, 0)
    grad_first = grad_ref[...] + contract(dq_ref[...], store[0], 1, 1)
    loaded_once(store, sems, 1)
    encoder = contract(dk_ref[...], store[1], 1, 1)
    loaded_once(store, sems, 2)
    encoder_ref[...] = (encoder + contract(dv_ref[...], store[2], 1, 1)).astype(bf16)
    gain = gains_ref[0:1]
    grad_pre = normalise_back(grad_first * gain, first_ref[...] / gain, inverse_ref[:, 0:1])
    pre_ref[...] = grad_pre
    loaded_once(store, sems, 3)
    grad_out_ref[...] = (
        contract(grad_pre.astype(bf16), store[3], 1, 1) * spread(share_ref, grad_pre.shape[1])
    ).astype(bf16)


def after_cross_back(dq, dk, dv, grad, first, inverse, share, gains, table, pieces, wanted):
    tokens, width = first.shape
    rows = tokens // 4
    tile = pl.BlockSpec((rows, width), lambda i: (i, 0))
    return pl.pallas_call(
        functools.partial(cross_back_kernel, wanted),
        grid=(tokens // rows,),
        in_specs=[smem()]
        + [tile] * 5
        + [pl.BlockSpec((rows, PAIR), lambda i: (i, 0)), share_spec(share, rows), pl.BlockSpec(gains.shape, lambda i: (0, 0))]
        + [in_place() for piece in pieces],
        out_specs=[tile] * 3,
        out_shape=[
            jax.ShapeDtypeStruct((tokens, width), bf16),
            jax.ShapeDtypeStruct((tokens, width), f32),
            jax.ShapeDtypeStruct((tokens, width), bf16),
        ],
        scratch_shapes=stores(len(wanted), width),
        compiler_params=params,
        cost_estimate=cost(0.2),
        name="after_cross_back",
    )(table, dq, dk, dv, grad, first, inverse, share, gains, *pieces)


def input_kernel(wanted, table_ref, dq_ref, dk_ref, dv_ref, pre_ref, *refs):
    *pieces, out_ref, store, sems = refs

    @pl.when(pl.program_id(0) == 0)
    def load():
        start_loading(pieces, table_ref, wanted, store, sems)

    total = pre_ref[...]
    for slot, ref in enumerate((dq_ref, dk_ref, dv_ref)):
        loaded_once(store, sems, slot)
        total += contract(ref[...], store[slot], 1, 1)
    out_ref[...] = total.astype(bf16)


def input_gradient(dq, dk, dv, pre, table, pieces, wanted):
    tokens, width = pre.shape
    rows = tokens // 4
    tile = pl.BlockSpec((rows, width), lambda i: (i, 0))
    return pl.pallas_call(
        functools.partial(input_kernel, wanted),
        grid=(tokens // rows,),
        in_specs=[smem()] + [tile] * 4 + [in_place() for piece in pieces],
        out_specs=tile,
        out_shape=jax.ShapeDtypeStruct((tokens, width), bf16),
        scratch_shapes=stores(len(wanted), width),
        compiler_params=params,
        cost_estimate=cost(0.2),
        name="input_gradient",
    )(table, dq, dk, dv, pre, *pieces)


def adamw_kernel(*refs):
    for ins, outs in ((refs[0:4], refs[8:13]), (refs[4:8], refs[13:18])):
        master, first_moment, second_moment, gradient = (ref[...] for ref in ins)
        first_new = beta_first * first_moment + (1.0 - beta_first) * gradient
        second_new = beta_second * second_moment + (1.0 - beta_second) * gradient * gradient
        first_hat = first_new / (1.0 - beta_first**STEP)
        second_hat = second_new / (1.0 - beta_second**STEP)
        master_new = master - learn_rate * (
            first_hat / (jnp.sqrt(second_hat) + epsilon_adam) + weight_decay * master
        )
        for ref, value in zip(outs, (gradient, first_new, second_new, master_new, master_new.astype(bf16))):
            ref[...] = value


def adamw(down, up):
    steps = 2

    def spec(array):
        return pl.BlockSpec((array.shape[0] // steps, array.shape[1]), lambda i: (i, 0))

    ins = (*down, *up)
    shapes = [
        jax.ShapeDtypeStruct(arrays[0].shape, kind)
        for arrays in (down, up)
        for kind in (f32, f32, f32, f32, bf16)
    ]
    return pl.pallas_call(
        adamw_kernel,
        grid=(steps,),
        in_specs=[spec(array) for array in ins],
        out_specs=[spec(shape) for shape in shapes],
        out_shape=shapes,
        compiler_params=params,
        cost_estimate=cost(10),
        name="adamw",
    )(*ins)


def pack_kernel(*refs):
    *shards, out_ref = refs
    for i, shard in enumerate(shards):
        out_ref[i] = shard[...]


def pack(shards):
    return pl.pallas_call(
        pack_kernel,
        out_shape=jax.ShapeDtypeStruct((len(shards),) + shards[0].shape, bf16),
        compiler_params=params,
        cost_estimate=cost(2),
        name="pack",
    )(*shards)


def pack_pair_kernel(table_ref, *refs):
    *shards, own_ref, other_ref = refs
    half = len(shards) // 2

    def both(first_ref, second_ref):
        for i in range(half):
            first_ref[i] = shards[i][...]
            second_ref[i] = shards[half + i][...]

    pl.when(table_ref[3, 0] == 0)(functools.partial(both, own_ref, other_ref))
    pl.when(table_ref[3, 0] != 0)(functools.partial(both, other_ref, own_ref))


def pack_pair(table, shards):
    shape = jax.ShapeDtypeStruct((len(shards) // 2,) + shards[0].shape, bf16)
    vmem = pl.BlockSpec(memory_space=pltpu.VMEM)
    return pl.pallas_call(
        pack_pair_kernel,
        in_specs=[smem()] + [vmem] * len(shards),
        out_specs=[vmem, vmem],
        out_shape=[shape, shape],
        compiler_params=params,
        cost_estimate=cost(2),
        name="pack_pair",
    )(table, *shards)


def pack_feed_kernel(first_ref, second_ref, out_ref):
    blocks, rows, width = out_ref.shape
    blocks //= 2
    for i in range(blocks):
        out_ref[i] = first_ref[:, i * width : (i + 1) * width]
        out_ref[blocks + i] = second_ref[i * rows : (i + 1) * rows]


def pack_feed(first, second):
    rows, width = first.shape[0], second.shape[1]
    blocks = (first.size + second.size) // (rows * width)
    return pl.pallas_call(
        pack_feed_kernel,
        out_shape=jax.ShapeDtypeStruct((blocks, rows, width), bf16),
        compiler_params=params,
        cost_estimate=cost(3),
        name="pack_feed",
    )(first, second)


def after_kernel(*refs):
    done_ref = refs[-1]
    done_ref[0] = 0


def after(values, *sooner):
    if not sooner:
        return values
    return pl.pallas_call(
        after_kernel,
        in_specs=[in_place()] * (1 + len(sooner)),
        out_specs=[in_place(), smem()],
        out_shape=[jax.ShapeDtypeStruct(values.shape, values.dtype), jax.ShapeDtypeStruct((1,), jnp.int32)],
        input_output_aliases={0: 0},
        compiler_params=params,
        cost_estimate=cost(0.01),
        name="after",
    )(values, *sooner)[0]


AXES = ("fsdp", "dp")


def ring_order(size):
    return list(range(0, size, 2)) + list(range(size - 1, 0, -2))


class Links:
    def __init__(self, shard_rows):
        self.size, self.parts = lax.axis_size("fsdp"), lax.axis_size("dp")
        order = ring_order(self.size)
        after = {order[i]: order[(i + 1) % self.size] for i in range(self.size)}
        before = {later: sooner for sooner, later in after.items()}
        every = [(f, d) for f in range(self.size) for d in range(self.parts)]
        flat = lambda f, d: f * self.parts + d
        self.onward = [(flat(f, d), flat((before if d % 2 else after)[f], d)) for f, d in every]
        self.sibling = [(flat(f, d), flat(f, d ^ 1)) for f, d in every]
        self.across = [(flat(f, d), flat(f, d ^ 2)) for f, d in every]
        self.core = lax.axis_index("dp") % 2
        self.hops = self.size // 2

        rows, table = shard_rows, []
        for f, d in every:
            place, core, plane = order.index(f), d % 2, d // 2 % 2
            toward = 1 - 2 * core
            shards, inside = [f], [0]
            for hop in range(1, self.hops + 1):
                for sign in (-1, 1):
                    shards.append(order[(place + sign * toward * hop) % self.size])
                    late = core if sign == -1 else 1 - core
                    inside.append(late * (rows // 2) if hop == self.hops else 0)
            first = [shard * rows + at for shard, at in zip(shards, inside)]
            table.append([first, shards, inside, [plane] * len(first)])
        self.table = lax.dynamic_index_in_dim(
            jnp.array(table, jnp.int32), lax.axis_index(AXES), 0, keepdims=False
        )

    def send(self, values, pairs):
        return lax.ppermute(values, AXES, pairs)

    def last(self, values):
        half = values.shape[1] // 2
        return lax.dynamic_slice_in_dim(values, self.core * half, half, 1)


class Gather:
    def __init__(self, links, own, other=None):
        self.links, self.moving, self.count, self.quarter, self.pieces = links, own, 0, 0, []
        self.rest = [] if other is None else [other]

    def share(self, *sooner):
        self.moving = after(self.moving, *sooner)
        self.shared = self.moving
        self.pieces.append(self.moving)
        if self.count:
            self.pieces.append(self.links.send(self.moving, self.links.sibling))
            if self.rest:
                self.crossed = self.links.send(self.moving, self.links.across)
                if self.count < self.links.hops:
                    self.hand_over()

    def hand_over(self, *sooner):
        crossed = after(self.crossed, *sooner)
        self.rest += [crossed, self.links.send(crossed, self.links.sibling)]

    def hop(self, *sooner, chained=False):
        links = self.links
        self.quarter += 1
        while self.count < self.quarter * links.hops // 4:
            if chained and len(self.pieces) > 1:
                sooner = (*sooner, self.pieces[-1], *self.rest[2:][-1:])
            self.share(*sooner)
            sooner = ()
            self.count += 1
            moving = links.last(self.moving) if self.count == links.hops else self.moving
            self.moving = links.send(moving, links.onward)


def body(
    inputs, encoder, cotangent, buckets, lengths, self_query, self_key, self_value, self_output,
    cross_query, cross_key, cross_value, cross_output, fc_first, fc_second, norm_gains,
    down_master, up_master, down_first, down_second, up_first, up_second,
):
    rows, width = self_query.shape
    links = Links(rows)
    table = links.table
    sq, sk, sv, so = ((None, i) for i in range(4))
    ck, cv, cq, co = (0, 0), (0, 1), (1, 0), (1, 1)
    one = Gather(links, pack((self_query, self_key, self_value, self_output)))
    two = Gather(links, *pack_pair(table, (cross_key, cross_value, cross_query, cross_output)))
    late = Gather(links, pack_feed(fc_first, fc_second))
    two_own, late_own = two.moving, late.moving
    one.hop(chained=True)
    two.hop(chained=True)
    one.hop(two_own, late_own, chained=True)
    two.hop(chained=True)
    one.hop(chained=True)
    two.hop(chained=True)
    one.hop(chained=True)
    two.hop(chained=True)
    fourth = one.moving
    one.share()
    two.share()
    late.hop(fourth)

    qkv = project(inputs, table, one.pieces * 3, (sq, sk, sv), query_scale, (late.shared,))
    two.hand_over(qkv)
    pieces = one.pieces + two.pieces + two.rest
    kv = project(encoder, table, two.pieces + two.pieces + two.rest, (ck, cv), 1.0, (qkv,))
    self_packs = [(qkv, 0), (qkv, 1), (qkv, 2)]
    half = width // PAIR // 2
    late.hop(qkv, kv)
    *self_half, done = attend(buckets, lengths, *self_packs, True, 0, half, (), (late.shared,))
    self_out, self_weight, self_share, done = attend(
        buckets, lengths, *self_packs, True, half, 2 * half, self_half
    )
    late.hop(done)
    first, first_inverse, query_cross = after_self(
        inputs, self_out, norm_gains, table, pieces, (so, cq), (late.shared,)
    )
    cross_packs = [(query_cross, 0), (kv, 0), (kv, 1)]
    *cross_half, done = attend(buckets, lengths, *cross_packs, False, 0, half)
    late.hop(done)
    cross_out, cross_weight, cross_share, done = attend(
        buckets, lengths, *cross_packs, False, half, 2 * half, cross_half, (late.shared,)
    )
    late.share(done)

    outputs, grad_third, slope, second_normal, second_inverse, adapter, down_local, up_local = feed(
        buckets, lengths, table, first, cross_out, cotangent, norm_gains, down_master, up_master, pieces, co,
        late.pieces,
    )
    down_grad, up_grad = lax.psum((down_local, up_local), ("fsdp", "dp"))

    grad_cross_pre, grad_cross_out = feed_back(
        table, grad_third, slope, second_normal, second_inverse, adapter, cross_share, norm_gains, down_master,
        pieces, co, late.pieces,
    )
    dq, dk, dv = attend_back(*cross_packs, grad_cross_out, cross_out, cross_weight, False)
    encoder_grad, grad_self_pre, grad_self_out = after_cross_back(
        dq, dk, dv, grad_cross_pre, first, first_inverse, self_share, norm_gains, table, pieces, (cq, ck, cv, so)
    )
    dq, dk, dv = attend_back(*self_packs, grad_self_out, self_out, self_weight, True)
    input_grad = input_gradient(dq, dk, dv, grad_self_pre, table, pieces, (sq, sk, sv))

    (
        down_grad, down_first_new, down_second_new, down_master_new, down_weight,
        up_grad, up_first_new, up_second_new, up_master_new, up_weight,
    ) = adamw(
        (down_master, down_first, down_second, down_grad), (up_master, up_first, up_second, up_grad)
    )
    return (
        outputs,
        input_grad,
        encoder_grad,
        down_grad,
        up_grad,
        down_first_new,
        down_second_new,
        up_first_new,
        up_second_new,
        down_master_new,
        up_master_new,
        down_weight,
        up_weight,
    )


def solution(mesh):
    tokens, matrix = P(("fsdp", "dp"), None), P("fsdp", None)
    return jax.shard_map(
        body,
        mesh=mesh,
        in_specs=(tokens, tokens, tokens, P(("fsdp", "dp")), tokens) + (matrix,) * 10 + (P(),) * 7,
        out_specs=(tokens,) * 3 + (P(),) * 10,
        check_vma=False,
    )
```

```python
import functools
import math

import jax
import jax.numpy as jnp
from jax import lax
from jax.experimental import pallas as pl
from jax.experimental.pallas import tpu as pltpu
from jax.sharding import PartitionSpec as P

HEAD_DIM = 64
PAIR = 2 * HEAD_DIM
STEP = 10
SLOTS = 4

epsilon_norm = 1e-05
beta_first = 0.9
beta_second = 0.999
learn_rate = 0.05
weight_decay = 0.01
epsilon_adam = 1e-08

f32, bf16 = jnp.float32, jnp.bfloat16
query_scale = HEAD_DIM ** (-0.5)
log2_e = math.log2(math.e)
forbidden = -(2.0**100)
least_sum, most_sum = 2.0**-40, 2.0**60

params = pltpu.CompilerParams(vmem_limit_bytes=63 * 2**20)


def contract(left, right, left_dim, right_dim):
    return lax.dot_general(
        left, right, (((left_dim,), (right_dim,)), ((), ())), preferred_element_type=f32
    )


def start_loading(pieces, table_ref, wanted, store, sems, start=0):
    count = len(pieces) // 3

    def copies(group, slot, i):
        for p, piece in enumerate(pieces[group * count : (group + 1) * count]):
            rows = piece.shape[1]
            at = pl.multiple_of(table_ref[0, p], 16)
            pltpu.make_async_copy(
                piece.at[i], store.at[slot, pl.ds(at, rows)], sems.at[slot]
            ).start()

    for slot, (kind, i) in list(enumerate(wanted))[start:]:
        if kind is None:
            copies(0, slot, i)
        else:
            pl.when(table_ref[3, 0] == kind)(functools.partial(copies, 1, slot, i))
            pl.when(table_ref[3, 0] != kind)(functools.partial(copies, 2, slot, i))


def loaded(store, sems, slot):
    pltpu.make_async_copy(store.at[slot], store.at[slot], sems.at[slot]).wait()


def loaded_once(store, sems, slot):
    @pl.when(pl.program_id(0) == 0)
    def wait():
        loaded(store, sems, slot)


def cost(microseconds):
    return pl.CostEstimate(flops=int(microseconds * 1.15e9), bytes_accessed=10**5, transcendentals=0)


def share_spec(share, rows):
    return pl.BlockSpec(share.shape[:2] + (rows,), lambda i: (0, 0, i))


def in_place():
    return pl.BlockSpec(memory_space=pl.ANY)


def stores(count, width):
    return [pltpu.VMEM((count, width, width), bf16), pltpu.SemaphoreType.DMA((count,))]


smem = functools.partial(pl.BlockSpec, memory_space=pltpu.SMEM)


def spread(share_ref, width):
    pairs, two, rows = share_ref.shape
    rest = share_ref[...].reshape(pairs * two, rows)
    member = (
        lax.broadcasted_iota(jnp.int32, (pairs * two, width), 0)
        == lax.broadcasted_iota(jnp.int32, (pairs * two, width), 1) >> 6
    ).astype(bf16)
    parts = []
    for i in range(3):
        parts.append(rest.astype(bf16))
        rest = rest - parts[-1].astype(f32)
    return contract(jnp.concatenate(parts, axis=0), jnp.concatenate([member] * 3, axis=0), 0, 0)


def normalise(values):
    centre = values - jnp.mean(values, axis=-1, keepdims=True)
    inverse = lax.rsqrt(jnp.mean(centre * centre, axis=-1, keepdims=True) + epsilon_norm)
    return centre * inverse, inverse


def normalise_back(scaled, normal, inverse):
    return inverse * (
        scaled
        - jnp.mean(scaled, axis=-1, keepdims=True)
        - normal * jnp.mean(scaled * normal, axis=-1, keepdims=True)
    )


def gelu_and_slope(u):
    bell = jnp.exp2(u * u * (-0.5 * math.log2(math.e)) - 0.5 * math.log2(2.0 * math.pi))
    below = 0.5 + 0.5 * lax.erf(u * math.sqrt(0.5))
    return u * below, below + u * bell


def project_kernel(wanted, scale, count, x_ref, table_ref, *refs):
    pieces = refs[:count]
    out_ref, store, sems = refs[-3:]
    step = pl.program_id(0)

    @pl.when(step == 0)
    def begin():
        start_loading(pieces, table_ref, wanted[:1], store, sems)
        loaded(store, sems, 0)
        start_loading(pieces, table_ref, wanted, store, sems, 1)
        out = contract(x_ref[...], store[0], 1, 0)
        out_ref[0] = (out if scale == 1.0 else out * scale).astype(bf16)

    @pl.when(step > 0)
    def more():
        loaded(store, sems, step)
        out_ref[0] = contract(x_ref[...], store[step], 1, 0).astype(bf16)


def project(x, table, pieces, wanted, scale, sooner=()):
    tokens, width = x.shape
    count = len(wanted)
    return pl.pallas_call(
        functools.partial(project_kernel, wanted, scale, len(pieces)),
        grid=(count,),
        in_specs=[pl.BlockSpec((tokens, width), lambda i: (0, 0)), smem()]
        + [in_place() for piece in (*pieces, *sooner)],
        out_specs=pl.BlockSpec((1, tokens, width), lambda i: (i, 0, 0)),
        out_shape=jax.ShapeDtypeStruct((count, tokens, width), bf16),
        scratch_shapes=stores(count, width),
        compiler_params=params,
        cost_estimate=cost(4 * count),
        name="project",
    )(x, table, *pieces, *sooner)


def low_half(rows):
    return lax.broadcasted_iota(jnp.int32, (rows, PAIR), 1) < HEAD_DIM


def choose(head, low):
    if head == 0:
        return lambda own, other: jnp.where(low, own, other)
    return lambda own, other: jnp.where(low, other, own)


def item_shift(bucket, tokens):
    return bucket + (tokens.bit_length() - 1 - 2)


def item_length(item, lengths_ref):
    length = jnp.zeros_like(item)
    for slot in range(SLOTS):
        length = jnp.where(item == slot, lengths_ref[0, slot], length)
    return length


def attend_kernel(
    causal, bucket_ref, lengths_ref, q_ref, k_ref, v_ref, *refs
):
    out_ref, rest_ref, weight_ref, share_ref, done_ref, qmark, kmark = refs[-7:]
    done_ref[...] = jnp.zeros_like(done_ref)
    tokens = q_ref.shape[-2]
    low = low_half(tokens)

    @pl.when(pl.program_id(0) == 0)
    def marks():
        shift = item_shift(bucket_ref[0], tokens)
        lane = lax.broadcasted_iota(jnp.int32, (tokens, PAIR), 1) & (HEAD_DIM - 1)
        row = lax.broadcasted_iota(jnp.int32, (tokens, PAIR), 0)
        item = row >> shift
        own = lane == item
        qmark[...] = jnp.where(own, 1.0, 0.0).astype(bf16)
        allowed = own & (row - (item << shift) < item_length(item, lengths_ref))
        kmark[...] = jnp.where((lane < SLOTS) & ~allowed, forbidden, 0.0).astype(bf16)

    q, k, v = q_ref[0], k_ref[0], v_ref[0]
    one = jnp.ones((tokens, PAIR), bf16)

    def operands(head):
        own = choose(head, low)
        return own(q, qmark[...]), own(k, kmark[...]), own(v, one)

    def finish(sums):
        even, odd = sums
        even_share, odd_share = 1.0 / even[HEAD_DIM : HEAD_DIM + 8], 1.0 / odd[:8]
        out = jnp.concatenate(
            [even[:HEAD_DIM] * even_share[:1], odd[HEAD_DIM:] * odd_share[:1]], axis=0
        )
        high = out.astype(bf16)
        out_ref[...] = high.T
        rest_ref[...] = (out - high.astype(f32)).astype(bf16).T
        share_ref[0, 0:1] = even_share[:1]
        share_ref[0, 1:2] = odd_share[:1]
        return even[HEAD_DIM : HEAD_DIM + 1], odd[:1]

    def direct():
        sums = []
        for head in range(2):
            queries, keys, values = operands(head)
            if not causal:
                weight = jnp.exp2(contract(keys, queries, 1, 1) * log2_e).astype(bf16)
                weight_ref[head] = weight
                sums.append(contract(values, weight, 0, 0))
                continue
            step = tokens // 2
            before = lax.broadcasted_iota(jnp.int32, (step, step), 0) <= lax.broadcasted_iota(
                jnp.int32, (step, step), 1
            )
            nothing = jnp.zeros((), bf16)
            top = jnp.exp2(contract(keys[:step], queries, 1, 1) * log2_e).astype(bf16)
            top = jnp.concatenate(
                [jnp.where(before, top[:, :step], nothing), top[:, step:]], axis=1
            )
            weight_ref[head, :step] = top
            total = contract(values[:step], top, 0, 0)
            low_part = jnp.exp2(contract(keys[step:], queries[step:], 1, 1) * log2_e).astype(bf16)
            low_part = jnp.where(before, low_part, nothing)
            weight_ref[head, step:, step:] = low_part
            rest = contract(values[step:], low_part, 0, 0)
            sums.append(jnp.concatenate([total[:, :step], total[:, step:] + rest], axis=1))
        return finish(sums)

    totals = jnp.concatenate(direct(), axis=0)
    sound = (jnp.min(totals) >= least_sum) & (jnp.max(totals) <= most_sum)

    @pl.when(jnp.logical_not(sound))
    def shifted():
        sums = []
        for head in range(2):
            queries, keys, values = operands(head)
            scores = contract(keys, queries, 1, 1)
            if causal:
                before = lax.broadcasted_iota(
                    jnp.int32, scores.shape, 0
                ) <= lax.broadcasted_iota(jnp.int32, scores.shape, 1)
                scores = jnp.where(before, scores, forbidden)
            scores = scores - jnp.max(scores, axis=0, keepdims=True)
            weight = jnp.exp2(scores * log2_e).astype(bf16)
            weight_ref[head] = weight
            sums.append(contract(values, weight, 0, 0))
        finish(sums)


def attend(bucket, lengths, q_pack, k_pack, v_pack, causal, start, stop, so_far=(), sooner=()):
    (q, q_at), (k, k_at), (v, v_at) = q_pack, k_pack, v_pack
    tokens, width = q.shape[1:]
    pairs = width // PAIR
    pair_spec = lambda at: pl.BlockSpec((1, tokens, PAIR), lambda j: (at, 0, start + j))
    flat_spec = pl.BlockSpec((tokens, PAIR), lambda j: (0, start + j))
    return pl.pallas_call(
        functools.partial(attend_kernel, causal),
        grid=(stop - start,),
        in_specs=[smem(), smem(), pair_spec(q_at), pair_spec(k_at), pair_spec(v_at)]
        + [in_place() for array in (*so_far, *sooner)],
        out_specs=[
            flat_spec,
            flat_spec,
            pl.BlockSpec((2, tokens, tokens), lambda j: (start + j, 0, 0)),
            pl.BlockSpec((1, 2, tokens), lambda j: (start + j, 0, 0)),
            pl.BlockSpec((8, PAIR), lambda j: (0, 0)),
        ],
        out_shape=[
            jax.ShapeDtypeStruct((tokens, width), bf16),
            jax.ShapeDtypeStruct((tokens, width), bf16),
            jax.ShapeDtypeStruct((2 * pairs, tokens, tokens), bf16),
            jax.ShapeDtypeStruct((pairs, 2, tokens), f32),
            jax.ShapeDtypeStruct((8, PAIR), f32),
        ],
        input_output_aliases={5 + i: i for i in range(len(so_far))},
        scratch_shapes=[pltpu.VMEM((tokens, PAIR), bf16), pltpu.VMEM((tokens, PAIR), bf16)],
        compiler_params=params,
        cost_estimate=cost(0.05 * (stop - start)),
        name="attend",
    )(bucket, lengths, q, k, v, *so_far, *sooner)


def attend_back_kernel(
    causal, q_ref, k_ref, v_ref, grad_ref, out_ref, rest_ref, weight_ref, dq_ref, dk_ref, dv_ref
):
    tokens = q_ref.shape[-2]
    low = low_half(tokens)
    q, k, v, grad = q_ref[0], k_ref[0], v_ref[0], grad_ref[...]
    nothing = jnp.zeros((tokens, PAIR), bf16)
    minus = jnp.full((tokens, PAIR), -1.0, bf16)
    swap = (
        (lax.broadcasted_iota(jnp.int32, (PAIR, PAIR), 0) < HEAD_DIM)
        != (lax.broadcasted_iota(jnp.int32, (PAIR, PAIR), 1) < HEAD_DIM)
    ).astype(bf16)
    product = grad.astype(f32) * (out_ref[...].astype(f32) + rest_ref[...].astype(f32))
    high = product.astype(bf16)
    centre = contract(high, swap, 1, 0) + contract((product - high.astype(f32)).astype(bf16), swap, 1, 0)
    high = centre.astype(bf16)
    rest = (centre - high.astype(f32)).astype(bf16)
    lane = lax.broadcasted_iota(jnp.int32, (tokens, PAIR), 1) & (HEAD_DIM - 1)
    centre = jnp.where(lane == 0, high, jnp.where(lane == 1, rest, nothing))

    step = tokens // 2 if causal else tokens
    dq_turned = None
    for tile in range(tokens // step):
        at = tile * step
        rows = slice(at, at + step)
        dk = dv = None
        turned = []
        for head in range(2):
            own = choose(head, low)
            weight = weight_ref[head, rows, at:]
            dweight = contract(own(v, minus)[rows], own(grad, centre)[at:], 1, 1)
            dscore = weight * dweight.astype(bf16)
            dv_own = contract(weight, own(grad, nothing)[at:], 1, 0)
            dk_own = contract(dscore, own(q, nothing)[at:], 1, 0)
            dv = dv_own if head == 0 else dv + dv_own
            dk = dk_own if head == 0 else dk + dk_own
            turned.append(contract(k[rows], dscore, 0, 0)[head * HEAD_DIM : (head + 1) * HEAD_DIM])
        dv_ref[rows] = dv.astype(bf16)
        dk_ref[rows] = dk.astype(bf16)
        turned = jnp.concatenate(turned, axis=0)
        if tile == 0:
            dq_turned = turned
        else:
            dq_turned = jnp.concatenate([dq_turned[:, :at], dq_turned[:, at:] + turned], axis=1)
    dq_ref[...] = (dq_turned * HEAD_DIM ** (-0.5)).T.astype(bf16)


def attend_back(q_pack, k_pack, v_pack, grad, out, rest, weight, causal):
    (q, q_at), (k, k_at), (v, v_at) = q_pack, k_pack, v_pack
    tokens, width = q.shape[1:]
    pairs = width // PAIR
    pair_spec = lambda at: pl.BlockSpec((1, tokens, PAIR), lambda j: (at, 0, j))
    flat_spec = pl.BlockSpec((tokens, PAIR), lambda j: (0, j))
    return pl.pallas_call(
        functools.partial(attend_back_kernel, causal),
        grid=(pairs,),
        in_specs=[
            pair_spec(q_at),
            pair_spec(k_at),
            pair_spec(v_at),
            flat_spec,
            flat_spec,
            flat_spec,
            pl.BlockSpec((2, tokens, tokens), lambda j: (j, 0, 0)),
        ],
        out_specs=[flat_spec] * 3,
        out_shape=[jax.ShapeDtypeStruct((tokens, width), bf16)] * 3,
        compiler_params=params,
        cost_estimate=cost(0.2),
        name="attend_back",
    )(q, k, v, grad, out, rest, weight)


def first_kernel(wanted, count, table_ref, x_ref, out_ref, gains_ref, *refs):
    pieces = refs[:count]
    first_ref, inverse_ref, q_ref, store, sems = refs[-5:]
    step = pl.program_id(0)

    @pl.when(step == 0)
    def load():
        start_loading(pieces, table_ref, wanted, store, sems)

    loaded_once(store, sems, 0)
    z = x_ref[...].astype(f32) + contract(out_ref[...], store[0], 1, 0)
    normal, inverse = normalise(z)
    first = normal * gains_ref[0:1]
    first_ref[...] = first
    inverse_ref[...] = jnp.broadcast_to(inverse, inverse_ref.shape)
    loaded_once(store, sems, 1)
    q = (contract(first.astype(bf16), store[1], 1, 0) * query_scale).astype(bf16)
    q_ref[0] = q


def after_self(x, out, gains, table, pieces, wanted, sooner):
    tokens, width = x.shape
    rows = tokens // 4
    tile = pl.BlockSpec((rows, width), lambda i: (i, 0))
    return pl.pallas_call(
        functools.partial(first_kernel, wanted, len(pieces)),
        grid=(tokens // rows,),
        in_specs=[smem(), tile, tile, pl.BlockSpec(gains.shape, lambda i: (0, 0))]
        + [in_place() for piece in (*pieces, *sooner)],
        out_specs=[
            tile,
            pl.BlockSpec((rows, PAIR), lambda i: (i, 0)),
            pl.BlockSpec((1, rows, width), lambda i: (0, i, 0)),
        ],
        out_shape=[
            jax.ShapeDtypeStruct((tokens, width), f32),
            jax.ShapeDtypeStruct((tokens, PAIR), f32),
            jax.ShapeDtypeStruct((1, tokens, width), bf16),
        ],
        scratch_shapes=stores(len(wanted), width),
        compiler_params=params,
        cost_estimate=cost(0.2),
        name="after_self",
    )(table, x, out, gains, *pieces, *sooner)


def load_feed(feed_pieces, table_ref, kinds, feed_store, feed_sems):
    blocks = feed_store.shape[2]
    for kind in kinds:
        for p, piece in enumerate(feed_pieces):
            rows_at = pl.ds(pl.multiple_of(table_ref[2, p], 16), piece.shape[1])
            pltpu.make_async_copy(
                piece.at[pl.ds(kind * blocks, blocks)],
                feed_store.at[kind, table_ref[1, p], :, rows_at],
                feed_sems.at[kind],
            ).start()


def first_block(feed_store, i):
    return feed_store[0, :, i].reshape(-1, feed_store.shape[-1])


def second_block(feed_store, i):
    devices, blocks = feed_store.shape[1:3]
    return feed_store[1, i * devices // blocks : (i + 1) * devices // blocks].reshape(
        -1, feed_store.shape[-1]
    )


def feed_kernel(
    wanted, count, bucket_ref, lengths_ref, table_ref, first_ref, out_ref, cotangent_ref, gains_ref, down_ref,
    up_ref, *refs,
):
    pieces, feed_pieces = refs[: 3 * count], refs[3 * count : 4 * count]
    (outputs_ref, third_ref, slope_ref, normal_ref, inverse_ref, adapter_ref, down_grad_ref, up_grad_ref,
     down_low, up_low, store, sems, feed_store, feed_sems) = refs[4 * count :]
    rows, width = first_ref.shape
    tokens = rows * pl.num_programs(0)
    step = pl.program_id(0)

    @pl.when(step == 0)
    def begin():
        start_loading(pieces, table_ref, wanted, store, sems)
        load_feed(feed_pieces, table_ref, (0, 1), feed_store, feed_sems)
        down_low[...] = down_ref[...].astype(bf16)
        up_low[...] = up_ref[...].astype(bf16)
        down_grad_ref[...] = jnp.zeros_like(down_grad_ref)
        up_grad_ref[...] = jnp.zeros_like(up_grad_ref)

    loaded_once(store, sems, 0)
    z = first_ref[...] + contract(out_ref[...], store[0], 1, 0)
    second_normal, second_inverse = normalise(z)
    normal_ref[...] = second_normal.astype(bf16)
    inverse_ref[...] = jnp.broadcast_to(second_inverse, inverse_ref.shape)
    second = second_normal * gains_ref[1:2]
    second_low = second.astype(bf16)

    adapter_act, adapter_slope = gelu_and_slope(contract(second_low, down_low[...], 1, 0))
    adapter_act = adapter_act.astype(bf16)
    total = second + 4.0 * contract(adapter_act, up_low[...], 1, 0)
    loaded_once(feed_store, feed_sems, 0)
    loaded_once(feed_store, feed_sems, 1)
    for i in range(feed_store.shape[2]):
        active, slope = gelu_and_slope(contract(second_low, first_block(feed_store, i), 1, 0))
        slope_ref[i] = slope.astype(bf16)
        total += contract(active.astype(bf16), second_block(feed_store, i), 1, 0)

    third_normal, third_inverse = normalise(total)
    outputs_ref[...] = (third_normal * gains_ref[2:3]).astype(bf16)

    shift = item_shift(bucket_ref[0], tokens)
    row = lax.broadcasted_iota(jnp.int32, (rows, 1), 0) + step * rows
    item = row >> shift
    valid = row - (item << shift) < item_length(item, lengths_ref)
    upstream = jnp.where(valid, cotangent_ref[...].astype(f32), 0.0)
    grad_third = normalise_back(upstream * gains_ref[2:3], third_normal, third_inverse)
    third_ref[...] = grad_third

    grad_adapter_out = (4.0 * grad_third).astype(bf16)
    up_grad_ref[...] += contract(adapter_act, grad_adapter_out, 0, 0)
    grad_adapter_pre = (contract(grad_adapter_out, up_low[...], 1, 1) * adapter_slope).astype(bf16)
    adapter_ref[...] = grad_adapter_pre
    down_grad_ref[...] += contract(second_low, grad_adapter_pre, 0, 0)


def feed(bucket, lengths, table, first, out, cotangent, gains, down, up, pieces, output_at, feed_pieces):
    tokens, width = first.shape
    rows = tokens // 4
    chunks, shard_rows = feed_pieces[0].shape[0] // 2, feed_pieces[0].shape[1]
    tile = pl.BlockSpec((rows, width), lambda i: (i, 0))
    fixed = lambda a: pl.BlockSpec(a.shape, lambda i: (0,) * a.ndim, pipeline_mode=pl.Buffered(1))
    return pl.pallas_call(
        functools.partial(feed_kernel, (output_at,), len(feed_pieces)),
        grid=(tokens // rows,),
        in_specs=[smem(), smem(), smem(), tile, tile, tile, fixed(gains), fixed(down), fixed(up)]
        + [in_place() for piece in pieces + feed_pieces],
        out_specs=[
            tile,
            tile,
            pl.BlockSpec((chunks, rows, width), lambda i: (0, i, 0)),
            tile,
            pl.BlockSpec((rows, PAIR), lambda i: (i, 0)),
            pl.BlockSpec((rows, down.shape[1]), lambda i: (i, 0)),
            fixed(down),
            fixed(up),
        ],
        out_shape=[
            jax.ShapeDtypeStruct((tokens, width), bf16),
            jax.ShapeDtypeStruct((tokens, width), f32),
            jax.ShapeDtypeStruct((chunks, tokens, width), bf16),
            jax.ShapeDtypeStruct((tokens, width), bf16),
            jax.ShapeDtypeStruct((tokens, PAIR), f32),
            jax.ShapeDtypeStruct((tokens, down.shape[1]), bf16),
            jax.ShapeDtypeStruct(down.shape, f32),
            jax.ShapeDtypeStruct(up.shape, f32),
        ],
        scratch_shapes=[
            pltpu.VMEM(down.shape, bf16),
            pltpu.VMEM(up.shape, bf16),
            *stores(1, width),
            pltpu.VMEM((2, width // shard_rows, chunks, shard_rows, width), bf16),
            pltpu.SemaphoreType.DMA((2,)),
        ],
        compiler_params=params,
        cost_estimate=cost(0.2),
        name="feed",
    )(bucket, lengths, table, first, out, cotangent, gains, down, up, *pieces, *feed_pieces)


def feed_back_kernel(
    wanted, count, table_ref, third_ref, slope_ref, normal_ref, inverse_ref, adapter_ref, share_ref, gains_ref,
    down_ref, *refs,
):
    pieces, feed_pieces = refs[: 3 * count], refs[3 * count : 4 * count]
    grad_ref, grad_out_ref, down_low, store, sems, feed_store, feed_sems = refs[4 * count :]

    @pl.when(pl.program_id(0) == 0)
    def begin():
        load_feed(feed_pieces, table_ref, (1, 0), feed_store, feed_sems)
        start_loading(pieces, table_ref, wanted, store, sems)
        down_low[...] = down_ref[...].astype(bf16)

    grad_third = third_ref[...]
    grad_feed = grad_third.astype(bf16)
    grad_second = grad_third + contract(adapter_ref[...], down_low[...], 1, 1)
    loaded_once(feed_store, feed_sems, 1)
    loaded_once(feed_store, feed_sems, 0)
    for i in range(feed_store.shape[2]):
        grad_inner = contract(grad_feed, second_block(feed_store, i), 1, 1)
        grad_inner = (grad_inner * slope_ref[i].astype(f32)).astype(bf16)
        grad_second += contract(grad_inner, first_block(feed_store, i), 1, 1)

    grad_pre = normalise_back(
        grad_second * gains_ref[1:2], normal_ref[...].astype(f32), inverse_ref[:, 0:1]
    )
    grad_ref[...] = grad_pre
    loaded_once(store, sems, 0)
    grad_out_ref[...] = (
        contract(grad_pre.astype(bf16), store[0], 1, 1) * spread(share_ref, grad_pre.shape[1])
    ).astype(bf16)


def feed_back(table, third, slope, normal, inverse, adapter, share, gains, down, pieces, output_at, feed_pieces):
    tokens, width = third.shape
    rows = tokens // 4
    chunks, shard_rows = feed_pieces[0].shape[0] // 2, feed_pieces[0].shape[1]
    tile = pl.BlockSpec((rows, width), lambda i: (i, 0))
    fixed = lambda a: pl.BlockSpec(a.shape, lambda i: (0,) * a.ndim, pipeline_mode=pl.Buffered(1))
    return pl.pallas_call(
        functools.partial(feed_back_kernel, (output_at,), len(feed_pieces)),
        grid=(tokens // rows,),
        in_specs=[
            smem(),
            tile,
            pl.BlockSpec((chunks, rows, width), lambda i: (0, i, 0)),
            tile,
            pl.BlockSpec((rows, PAIR), lambda i: (i, 0)),
            pl.BlockSpec((rows, down.shape[1]), lambda i: (i, 0)),
            share_spec(share, rows),
            fixed(gains),
            fixed(down),
        ]
        + [in_place() for piece in pieces + feed_pieces],
        out_specs=[tile, tile],
        out_shape=[
            jax.ShapeDtypeStruct((tokens, width), f32),
            jax.ShapeDtypeStruct((tokens, width), bf16),
        ],
        scratch_shapes=[
            pltpu.VMEM(down.shape, bf16),
            *stores(1, width),
            pltpu.VMEM((2, width // shard_rows, chunks, shard_rows, width), bf16),
            pltpu.SemaphoreType.DMA((2,)),
        ],
        compiler_params=params,
        cost_estimate=cost(0.2),
        name="feed_back",
    )(table, third, slope, normal, inverse, adapter, share, gains, down, *pieces, *feed_pieces)


def cross_back_kernel(
    wanted, table_ref, dq_ref, dk_ref, dv_ref, grad_ref, first_ref, inverse_ref, share_ref, gains_ref,
    *refs,
):
    *pieces, encoder_ref, pre_ref, grad_out_ref, store, sems = refs

    @pl.when(pl.program_id(0) == 0)
    def load():
        start_loading(pieces, table_ref, wanted, store, sems)

    loaded_once(store, sems, 0)
    grad_first = grad_ref[...] + contract(dq_ref[...], store[0], 1, 1)
    loaded_once(store, sems, 1)
    encoder = contract(dk_ref[...], store[1], 1, 1)
    loaded_once(store, sems, 2)
    encoder_ref[...] = (encoder + contract(dv_ref[...], store[2], 1, 1)).astype(bf16)
    gain = gains_ref[0:1]
    grad_pre = normalise_back(grad_first * gain, first_ref[...] / gain, inverse_ref[:, 0:1])
    pre_ref[...] = grad_pre
    loaded_once(store, sems, 3)
    grad_out_ref[...] = (
        contract(grad_pre.astype(bf16), store[3], 1, 1) * spread(share_ref, grad_pre.shape[1])
    ).astype(bf16)


def after_cross_back(dq, dk, dv, grad, first, inverse, share, gains, table, pieces, wanted):
    tokens, width = first.shape
    rows = tokens // 4
    tile = pl.BlockSpec((rows, width), lambda i: (i, 0))
    return pl.pallas_call(
        functools.partial(cross_back_kernel, wanted),
        grid=(tokens // rows,),
        in_specs=[smem()]
        + [tile] * 5
        + [pl.BlockSpec((rows, PAIR), lambda i: (i, 0)), share_spec(share, rows), pl.BlockSpec(gains.shape, lambda i: (0, 0))]
        + [in_place() for piece in pieces],
        out_specs=[tile] * 3,
        out_shape=[
            jax.ShapeDtypeStruct((tokens, width), bf16),
            jax.ShapeDtypeStruct((tokens, width), f32),
            jax.ShapeDtypeStruct((tokens, width), bf16),
        ],
        scratch_shapes=stores(len(wanted), width),
        compiler_params=params,
        cost_estimate=cost(0.2),
        name="after_cross_back",
    )(table, dq, dk, dv, grad, first, inverse, share, gains, *pieces)


def input_kernel(wanted, table_ref, dq_ref, dk_ref, dv_ref, pre_ref, *refs):
    *pieces, out_ref, store, sems = refs

    @pl.when(pl.program_id(0) == 0)
    def load():
        start_loading(pieces, table_ref, wanted, store, sems)

    total = pre_ref[...]
    for slot, ref in enumerate((dq_ref, dk_ref, dv_ref)):
        loaded_once(store, sems, slot)
        total += contract(ref[...], store[slot], 1, 1)
    out_ref[...] = total.astype(bf16)


def input_gradient(dq, dk, dv, pre, table, pieces, wanted):
    tokens, width = pre.shape
    rows = tokens // 4
    tile = pl.BlockSpec((rows, width), lambda i: (i, 0))
    return pl.pallas_call(
        functools.partial(input_kernel, wanted),
        grid=(tokens // rows,),
        in_specs=[smem()] + [tile] * 4 + [in_place() for piece in pieces],
        out_specs=tile,
        out_shape=jax.ShapeDtypeStruct((tokens, width), bf16),
        scratch_shapes=stores(len(wanted), width),
        compiler_params=params,
        cost_estimate=cost(0.2),
        name="input_gradient",
    )(table, dq, dk, dv, pre, *pieces)


def adamw_kernel(*refs):
    for ins, outs in ((refs[0:4], refs[8:13]), (refs[4:8], refs[13:18])):
        master, first_moment, second_moment, gradient = (ref[...] for ref in ins)
        first_new = beta_first * first_moment + (1.0 - beta_first) * gradient
        second_new = beta_second * second_moment + (1.0 - beta_second) * gradient * gradient
        first_hat = first_new / (1.0 - beta_first**STEP)
        second_hat = second_new / (1.0 - beta_second**STEP)
        master_new = master - learn_rate * (
            first_hat / (jnp.sqrt(second_hat) + epsilon_adam) + weight_decay * master
        )
        for ref, value in zip(outs, (gradient, first_new, second_new, master_new, master_new.astype(bf16))):
            ref[...] = value


def adamw(down, up):
    steps = 2

    def spec(array):
        return pl.BlockSpec((array.shape[0] // steps, array.shape[1]), lambda i: (i, 0))

    ins = (*down, *up)
    shapes = [
        jax.ShapeDtypeStruct(arrays[0].shape, kind)
        for arrays in (down, up)
        for kind in (f32, f32, f32, f32, bf16)
    ]
    return pl.pallas_call(
        adamw_kernel,
        grid=(steps,),
        in_specs=[spec(array) for array in ins],
        out_specs=[spec(shape) for shape in shapes],
        out_shape=shapes,
        compiler_params=params,
        cost_estimate=cost(10),
        name="adamw",
    )(*ins)


def pack_kernel(*refs):
    *shards, out_ref = refs
    for i, shard in enumerate(shards):
        out_ref[i] = shard[...]


def pack(shards):
    return pl.pallas_call(
        pack_kernel,
        out_shape=jax.ShapeDtypeStruct((len(shards),) + shards[0].shape, bf16),
        compiler_params=params,
        cost_estimate=cost(2),
        name="pack",
    )(*shards)


def pack_pair_kernel(table_ref, *refs):
    *shards, own_ref, other_ref = refs
    half = len(shards) // 2

    def both(first_ref, second_ref):
        for i in range(half):
            first_ref[i] = shards[i][...]
            second_ref[i] = shards[half + i][...]

    pl.when(table_ref[3, 0] == 0)(functools.partial(both, own_ref, other_ref))
    pl.when(table_ref[3, 0] != 0)(functools.partial(both, other_ref, own_ref))


def pack_pair(table, shards):
    shape = jax.ShapeDtypeStruct((len(shards) // 2,) + shards[0].shape, bf16)
    vmem = pl.BlockSpec(memory_space=pltpu.VMEM)
    return pl.pallas_call(
        pack_pair_kernel,
        in_specs=[smem()] + [vmem] * len(shards),
        out_specs=[vmem, vmem],
        out_shape=[shape, shape],
        compiler_params=params,
        cost_estimate=cost(2),
        name="pack_pair",
    )(table, *shards)


def pack_feed_kernel(first_ref, second_ref, out_ref):
    blocks, rows, width = out_ref.shape
    blocks //= 2
    for i in range(blocks):
        out_ref[i] = first_ref[:, i * width : (i + 1) * width]
        out_ref[blocks + i] = second_ref[i * rows : (i + 1) * rows]


def pack_feed(first, second):
    rows, width = first.shape[0], second.shape[1]
    blocks = (first.size + second.size) // (rows * width)
    return pl.pallas_call(
        pack_feed_kernel,
        out_shape=jax.ShapeDtypeStruct((blocks, rows, width), bf16),
        compiler_params=params,
        cost_estimate=cost(3),
        name="pack_feed",
    )(first, second)


def after_kernel(*refs):
    done_ref = refs[-1]
    done_ref[0] = 0


def after(values, *sooner):
    if not sooner:
        return values
    return pl.pallas_call(
        after_kernel,
        in_specs=[in_place()] * (1 + len(sooner)),
        out_specs=[in_place(), smem()],
        out_shape=[jax.ShapeDtypeStruct(values.shape, values.dtype), jax.ShapeDtypeStruct((1,), jnp.int32)],
        input_output_aliases={0: 0},
        compiler_params=params,
        cost_estimate=cost(0.01),
        name="after",
    )(values, *sooner)[0]


AXES = ("fsdp", "dp")


def ring_order(size):
    return list(range(0, size, 2)) + list(range(size - 1, 0, -2))


class Links:
    def __init__(self, shard_rows):
        self.size, self.parts = lax.axis_size("fsdp"), lax.axis_size("dp")
        order = ring_order(self.size)
        after = {order[i]: order[(i + 1) % self.size] for i in range(self.size)}
        before = {later: sooner for sooner, later in after.items()}
        every = [(f, d) for f in range(self.size) for d in range(self.parts)]
        flat = lambda f, d: f * self.parts + d
        self.onward = [(flat(f, d), flat((before if d % 2 else after)[f], d)) for f, d in every]
        self.sibling = [(flat(f, d), flat(f, d ^ 1)) for f, d in every]
        self.across = [(flat(f, d), flat(f, d ^ 2)) for f, d in every]
        self.core = lax.axis_index("dp") % 2
        self.hops = self.size // 2

        rows, table = shard_rows, []
        for f, d in every:
            place, core, plane = order.index(f), d % 2, d // 2 % 2
            toward = 1 - 2 * core
            shards, inside = [f], [0]
            for hop in range(1, self.hops + 1):
                for sign in (-1, 1):
                    shards.append(order[(place + sign * toward * hop) % self.size])
                    late = core if sign == -1 else 1 - core
                    inside.append(late * (rows // 2) if hop == self.hops else 0)
            first = [shard * rows + at for shard, at in zip(shards, inside)]
            table.append([first, shards, inside, [plane] * len(first)])
        self.table = lax.dynamic_index_in_dim(
            jnp.array(table, jnp.int32), lax.axis_index(AXES), 0, keepdims=False
        )

    def send(self, values, pairs):
        return lax.ppermute(values, AXES, pairs)

    def last(self, values):
        half = values.shape[1] // 2
        return lax.dynamic_slice_in_dim(values, self.core * half, half, 1)


class Gather:
    def __init__(self, links, own, other=None):
        self.links, self.moving, self.count, self.quarter, self.pieces = links, own, 0, 0, []
        self.rest = [] if other is None else [other]

    def share(self, *sooner):
        self.moving = after(self.moving, *sooner)
        self.shared = self.moving
        self.pieces.append(self.moving)
        if self.count:
            self.pieces.append(self.links.send(self.moving, self.links.sibling))
            if self.rest:
                self.crossed = self.links.send(self.moving, self.links.across)
                if self.count < self.links.hops:
                    self.hand_over()

    def hand_over(self, *sooner):
        crossed = after(self.crossed, *sooner)
        self.rest += [crossed, self.links.send(crossed, self.links.sibling)]

    def hop(self, *sooner, chained=False):
        links = self.links
        self.quarter += 1
        while self.count < self.quarter * links.hops // 4:
            if chained and len(self.pieces) > 1:
                sooner = (*sooner, self.pieces[-1], *self.rest[2:][-1:])
            self.share(*sooner)
            sooner = ()
            self.count += 1
            moving = links.last(self.moving) if self.count == links.hops else self.moving
            self.moving = links.send(moving, links.onward)


def body(
    inputs, encoder, cotangent, buckets, lengths, self_query, self_key, self_value, self_output,
    cross_query, cross_key, cross_value, cross_output, fc_first, fc_second, norm_gains,
    down_master, up_master, down_first, down_second, up_first, up_second,
):
    rows, width = self_query.shape
    links = Links(rows)
    table = links.table
    sq, sk, sv, so = ((None, i) for i in range(4))
    ck, cv, cq, co = (0, 0), (0, 1), (1, 0), (1, 1)
    one = Gather(links, pack((self_query, self_key, self_value, self_output)))
    two = Gather(links, *pack_pair(table, (cross_key, cross_value, cross_query, cross_output)))
    late = Gather(links, pack_feed(fc_first, fc_second))
    two_own, late_own = two.moving, late.moving
    one.hop(chained=True)
    two.hop(chained=True)
    one.hop(two_own, late_own, chained=True)
    two.hop(chained=True)
    one.hop(chained=True)
    two.hop(chained=True)
    one.hop(chained=True)
    two.hop(chained=True)
    fourth = one.moving
    one.share()
    two.share()
    late.hop(fourth)

    qkv = project(inputs, table, one.pieces * 3, (sq, sk, sv), query_scale, (late.shared,))
    two.hand_over(qkv)
    pieces = one.pieces + two.pieces + two.rest
    kv = project(encoder, table, two.pieces + two.pieces + two.rest, (ck, cv), 1.0, (qkv,))
    self_packs = [(qkv, 0), (qkv, 1), (qkv, 2)]
    half = width // PAIR // 2
    late.hop(qkv, kv)
    *self_half, done = attend(buckets, lengths, *self_packs, True, 0, half, (), (late.shared,))
    self_out, self_rest, self_weight, self_share, done = attend(
        buckets, lengths, *self_packs, True, half, 2 * half, self_half
    )
    late.hop(done)
    first, first_inverse, query_cross = after_self(
        inputs, self_out, norm_gains, table, pieces, (so, cq), (late.shared,)
    )
    cross_packs = [(query_cross, 0), (kv, 0), (kv, 1)]
    *cross_half, done = attend(buckets, lengths, *cross_packs, False, 0, half)
    late.hop(done)
    cross_out, cross_rest, cross_weight, cross_share, done = attend(
        buckets, lengths, *cross_packs, False, half, 2 * half, cross_half, (late.shared,)
    )
    late.share(done)

    outputs, grad_third, slope, second_normal, second_inverse, adapter, down_local, up_local = feed(
        buckets, lengths, table, first, cross_out, cotangent, norm_gains, down_master, up_master, pieces, co,
        late.pieces,
    )
    down_grad, up_grad = lax.psum((down_local, up_local), ("fsdp", "dp"))

    grad_cross_pre, grad_cross_out = feed_back(
        table, grad_third, slope, second_normal, second_inverse, adapter, cross_share, norm_gains, down_master,
        pieces, co, late.pieces,
    )
    dq, dk, dv = attend_back(*cross_packs, grad_cross_out, cross_out, cross_rest, cross_weight, False)
    encoder_grad, grad_self_pre, grad_self_out = after_cross_back(
        dq, dk, dv, grad_cross_pre, first, first_inverse, self_share, norm_gains, table, pieces, (cq, ck, cv, so)
    )
    dq, dk, dv = attend_back(*self_packs, grad_self_out, self_out, self_rest, self_weight, True)
    input_grad = input_gradient(dq, dk, dv, grad_self_pre, table, pieces, (sq, sk, sv))

    (
        down_grad, down_first_new, down_second_new, down_master_new, down_weight,
        up_grad, up_first_new, up_second_new, up_master_new, up_weight,
    ) = adamw(
        (down_master, down_first, down_second, down_grad), (up_master, up_first, up_second, up_grad)
    )
    return (
        outputs,
        input_grad,
        encoder_grad,
        down_grad,
        up_grad,
        down_first_new,
        down_second_new,
        up_first_new,
        up_second_new,
        down_master_new,
        up_master_new,
        down_weight,
        up_weight,
    )


def solution(mesh):
    tokens, matrix = P(("fsdp", "dp"), None), P("fsdp", None)
    return jax.shard_map(
        body,
        mesh=mesh,
        in_specs=(tokens, tokens, tokens, P(("fsdp", "dp")), tokens) + (matrix,) * 10 + (P(),) * 7,
        out_specs=(tokens,) * 3 + (P(),) * 10,
        check_vma=False,
    )
```

```python
import functools
import math

import jax
import jax.numpy as jnp
from jax import lax
from jax.experimental import pallas as pl
from jax.experimental.pallas import tpu as pltpu
from jax.sharding import PartitionSpec as P

HEAD_DIM = 64
PAIR = 2 * HEAD_DIM
STEP = 10
SLOTS = 4

epsilon_norm = 1e-05
beta_first = 0.9
beta_second = 0.999
learn_rate = 0.05
weight_decay = 0.01
epsilon_adam = 1e-08

f32, bf16 = jnp.float32, jnp.bfloat16
query_scale = HEAD_DIM ** (-0.5)
log2_e = math.log2(math.e)
forbidden = -(2.0**100)
least_sum, most_sum = 2.0**-40, 2.0**60

params = pltpu.CompilerParams(vmem_limit_bytes=63 * 2**20)


def contract(left, right, left_dim, right_dim):
    return lax.dot_general(
        left, right, (((left_dim,), (right_dim,)), ((), ())), preferred_element_type=f32
    )


def start_loading(pieces, table_ref, wanted, store, sems, start=0):
    count = len(pieces) // 3

    def copies(group, slot, i):
        for p, piece in enumerate(pieces[group * count : (group + 1) * count]):
            rows = piece.shape[1]
            at = pl.multiple_of(table_ref[0, p], 16)
            pltpu.make_async_copy(
                piece.at[i], store.at[slot, pl.ds(at, rows)], sems.at[slot]
            ).start()

    for slot, (kind, i) in list(enumerate(wanted))[start:]:
        if kind is None:
            copies(0, slot, i)
        else:
            pl.when(table_ref[3, 0] == kind)(functools.partial(copies, 1, slot, i))
            pl.when(table_ref[3, 0] != kind)(functools.partial(copies, 2, slot, i))


def loaded(store, sems, slot):
    pltpu.make_async_copy(store.at[slot], store.at[slot], sems.at[slot]).wait()


def loaded_once(store, sems, slot):
    @pl.when(pl.program_id(0) == 0)
    def wait():
        loaded(store, sems, slot)


def cost(microseconds):
    return pl.CostEstimate(flops=int(microseconds * 1.15e9), bytes_accessed=10**5, transcendentals=0)


def share_spec(share, rows):
    return pl.BlockSpec(share.shape[:2] + (rows,), lambda i: (0, 0, i))


def in_place():
    return pl.BlockSpec(memory_space=pl.ANY)


def stores(count, width):
    return [pltpu.VMEM((count, width, width), bf16), pltpu.SemaphoreType.DMA((count,))]


smem = functools.partial(pl.BlockSpec, memory_space=pltpu.SMEM)


def spread(share_ref, width):
    pairs, two, rows = share_ref.shape
    rest = share_ref[...].reshape(pairs * two, rows)
    member = (
        lax.broadcasted_iota(jnp.int32, (pairs * two, width), 0)
        == lax.broadcasted_iota(jnp.int32, (pairs * two, width), 1) >> 6
    ).astype(bf16)
    parts = []
    for i in range(3):
        parts.append(rest.astype(bf16))
        rest = rest - parts[-1].astype(f32)
    return contract(jnp.concatenate(parts, axis=0), jnp.concatenate([member] * 3, axis=0), 0, 0)


def normalise(values):
    centre = values - jnp.mean(values, axis=-1, keepdims=True)
    inverse = lax.rsqrt(jnp.mean(centre * centre, axis=-1, keepdims=True) + epsilon_norm)
    return centre * inverse, inverse


def normalise_back(scaled, normal, inverse):
    return inverse * (
        scaled
        - jnp.mean(scaled, axis=-1, keepdims=True)
        - normal * jnp.mean(scaled * normal, axis=-1, keepdims=True)
    )


def gelu_and_slope(u):
    bell = jnp.exp2(u * u * (-0.5 * math.log2(math.e)) - 0.5 * math.log2(2.0 * math.pi))
    below = 0.5 + 0.5 * lax.erf(u * math.sqrt(0.5))
    return u * below, below + u * bell


def project_kernel(wanted, scale, count, x_ref, table_ref, *refs):
    pieces = refs[:count]
    out_ref, store, sems = refs[-3:]
    step = pl.program_id(0)

    @pl.when(step == 0)
    def begin():
        start_loading(pieces, table_ref, wanted[:1], store, sems)
        loaded(store, sems, 0)
        start_loading(pieces, table_ref, wanted, store, sems, 1)
        out = contract(x_ref[...], store[0], 1, 0)
        out_ref[0] = (out if scale == 1.0 else out * scale).astype(bf16)

    @pl.when(step > 0)
    def more():
        loaded(store, sems, step)
        out_ref[0] = contract(x_ref[...], store[step], 1, 0).astype(bf16)


def project(x, table, pieces, wanted, scale, sooner=()):
    tokens, width = x.shape
    count = len(wanted)
    return pl.pallas_call(
        functools.partial(project_kernel, wanted, scale, len(pieces)),
        grid=(count,),
        in_specs=[pl.BlockSpec((tokens, width), lambda i: (0, 0)), smem()]
        + [in_place() for piece in (*pieces, *sooner)],
        out_specs=pl.BlockSpec((1, tokens, width), lambda i: (i, 0, 0)),
        out_shape=jax.ShapeDtypeStruct((count, tokens, width), bf16),
        scratch_shapes=stores(count, width),
        compiler_params=params,
        cost_estimate=cost(4 * count),
        name="project",
    )(x, table, *pieces, *sooner)


def low_half(rows):
    return lax.broadcasted_iota(jnp.int32, (rows, PAIR), 1) < HEAD_DIM


def choose(head, low):
    if head == 0:
        return lambda own, other: jnp.where(low, own, other)
    return lambda own, other: jnp.where(low, other, own)


def item_shift(bucket, tokens):
    return bucket + (tokens.bit_length() - 1 - 2)


def item_length(item, lengths_ref):
    length = jnp.zeros_like(item)
    for slot in range(SLOTS):
        length = jnp.where(item == slot, lengths_ref[0, slot], length)
    return length


def attend_kernel(
    causal, bucket_ref, lengths_ref, q_ref, k_ref, v_ref, *refs
):
    out_ref, rest_ref, weight_ref, share_ref, done_ref, qmark, kmark = refs[-7:]
    done_ref[...] = jnp.zeros_like(done_ref)
    tokens = q_ref.shape[-2]
    low = low_half(tokens)

    @pl.when(pl.program_id(0) == 0)
    def marks():
        shift = item_shift(bucket_ref[0], tokens)
        lane = lax.broadcasted_iota(jnp.int32, (tokens, PAIR), 1) & (HEAD_DIM - 1)
        row = lax.broadcasted_iota(jnp.int32, (tokens, PAIR), 0)
        item = row >> shift
        own = lane == item
        qmark[...] = jnp.where(own, 1.0, 0.0).astype(bf16)
        allowed = own & (row - (item << shift) < item_length(item, lengths_ref))
        kmark[...] = jnp.where((lane < SLOTS) & ~allowed, forbidden, 0.0).astype(bf16)

    q, k, v = q_ref[0], k_ref[0], v_ref[0]
    one = jnp.ones((tokens, PAIR), bf16)

    def operands(head):
        own = choose(head, low)
        return own(q, qmark[...]), own(k, kmark[...]), own(v, one)

    def finish(sums):
        even, odd = sums
        even_share, odd_share = 1.0 / even[HEAD_DIM : HEAD_DIM + 8], 1.0 / odd[:8]
        out = jnp.concatenate(
            [even[:HEAD_DIM] * even_share[:1], odd[HEAD_DIM:] * odd_share[:1]], axis=0
        )
        high = out.astype(bf16)
        out_ref[...] = high.T
        rest_ref[...] = (out - high.astype(f32)).astype(bf16).T
        share_ref[0, 0:1] = even_share[:1]
        share_ref[0, 1:2] = odd_share[:1]
        return even[HEAD_DIM : HEAD_DIM + 1], odd[:1]

    def direct():
        sums = []
        for head in range(2):
            queries, keys, values = operands(head)
            if not causal:
                weight = jnp.exp2(contract(keys, queries, 1, 1) * log2_e).astype(bf16)
                weight_ref[head] = weight
                sums.append(contract(values, weight, 0, 0))
                continue
            step = tokens // 2
            before = lax.broadcasted_iota(jnp.int32, (step, step), 0) <= lax.broadcasted_iota(
                jnp.int32, (step, step), 1
            )
            nothing = jnp.zeros((), bf16)
            top = jnp.exp2(contract(keys[:step], queries, 1, 1) * log2_e).astype(bf16)
            top = jnp.concatenate(
                [jnp.where(before, top[:, :step], nothing), top[:, step:]], axis=1
            )
            weight_ref[head, :step] = top
            total = contract(values[:step], top, 0, 0)
            low_part = jnp.exp2(contract(keys[step:], queries[step:], 1, 1) * log2_e).astype(bf16)
            low_part = jnp.where(before, low_part, nothing)
            weight_ref[head, step:, step:] = low_part
            rest = contract(values[step:], low_part, 0, 0)
            sums.append(jnp.concatenate([total[:, :step], total[:, step:] + rest], axis=1))
        return finish(sums)

    totals = jnp.concatenate(direct(), axis=0)
    sound = (jnp.min(totals) >= least_sum) & (jnp.max(totals) <= most_sum)

    @pl.when(jnp.logical_not(sound))
    def shifted():
        sums = []
        for head in range(2):
            queries, keys, values = operands(head)
            scores = contract(keys, queries, 1, 1)
            if causal:
                before = lax.broadcasted_iota(
                    jnp.int32, scores.shape, 0
                ) <= lax.broadcasted_iota(jnp.int32, scores.shape, 1)
                scores = jnp.where(before, scores, forbidden)
            scores = scores - jnp.max(scores, axis=0, keepdims=True)
            weight = jnp.exp2(scores * log2_e).astype(bf16)
            weight_ref[head] = weight
            sums.append(contract(values, weight, 0, 0))
        finish(sums)


def attend(bucket, lengths, q_pack, k_pack, v_pack, causal, start, stop, so_far=(), sooner=()):
    (q, q_at), (k, k_at), (v, v_at) = q_pack, k_pack, v_pack
    tokens, width = q.shape[1:]
    pairs = width // PAIR
    pair_spec = lambda at: pl.BlockSpec((1, tokens, PAIR), lambda j: (at, 0, start + j))
    flat_spec = pl.BlockSpec((tokens, PAIR), lambda j: (0, start + j))
    return pl.pallas_call(
        functools.partial(attend_kernel, causal),
        grid=(stop - start,),
        in_specs=[smem(), smem(), pair_spec(q_at), pair_spec(k_at), pair_spec(v_at)]
        + [in_place() for array in (*so_far, *sooner)],
        out_specs=[
            flat_spec,
            flat_spec,
            pl.BlockSpec((2, tokens, tokens), lambda j: (start + j, 0, 0)),
            pl.BlockSpec((1, 2, tokens), lambda j: (start + j, 0, 0)),
            pl.BlockSpec((8, PAIR), lambda j: (0, 0)),
        ],
        out_shape=[
            jax.ShapeDtypeStruct((tokens, width), bf16),
            jax.ShapeDtypeStruct((tokens, width), bf16),
            jax.ShapeDtypeStruct((2 * pairs, tokens, tokens), bf16),
            jax.ShapeDtypeStruct((pairs, 2, tokens), f32),
            jax.ShapeDtypeStruct((8, PAIR), f32),
        ],
        input_output_aliases={5 + i: i for i in range(len(so_far))},
        scratch_shapes=[pltpu.VMEM((tokens, PAIR), bf16), pltpu.VMEM((tokens, PAIR), bf16)],
        compiler_params=params,
        cost_estimate=cost(0.05 * (stop - start)),
        name="attend",
    )(bucket, lengths, q, k, v, *so_far, *sooner)


def attend_back_kernel(
    causal, q_ref, k_ref, v_ref, grad_ref, out_ref, rest_ref, weight_ref, dq_ref, dk_ref, dv_ref
):
    tokens = q_ref.shape[-2]
    low = low_half(tokens)
    q, k, v, grad = q_ref[0], k_ref[0], v_ref[0], grad_ref[...]
    nothing = jnp.zeros((tokens, PAIR), bf16)
    minus = jnp.full((tokens, PAIR), -1.0, bf16)
    swap = (
        (lax.broadcasted_iota(jnp.int32, (PAIR, PAIR), 0) < HEAD_DIM)
        != (lax.broadcasted_iota(jnp.int32, (PAIR, PAIR), 1) < HEAD_DIM)
    ).astype(bf16)
    product = grad.astype(f32) * (out_ref[...].astype(f32) + rest_ref[...].astype(f32))
    high = product.astype(bf16)
    centre = contract(high, swap, 1, 0) + contract((product - high.astype(f32)).astype(bf16), swap, 1, 0)
    high = centre.astype(bf16)
    rest = (centre - high.astype(f32)).astype(bf16)
    lane = lax.broadcasted_iota(jnp.int32, (tokens, PAIR), 1) & (HEAD_DIM - 1)
    centre = jnp.where(lane == 0, high, jnp.where(lane == 1, rest, nothing))

    step = tokens // 2 if causal else tokens
    dq_turned = None
    for tile in range(tokens // step):
        at = tile * step
        rows = slice(at, at + step)
        dk = dv = None
        turned = []
        for head in range(2):
            own = choose(head, low)
            weight = weight_ref[head, rows, at:]
            dweight = contract(own(v, minus)[rows], own(grad, centre)[at:], 1, 1)
            dscore = weight * dweight.astype(bf16)
            dv_own = contract(weight, own(grad, nothing)[at:], 1, 0)
            dk_own = contract(dscore, own(q, nothing)[at:], 1, 0)
            dv = dv_own if head == 0 else dv + dv_own
            dk = dk_own if head == 0 else dk + dk_own
            turned.append(contract(k[rows], dscore, 0, 0)[head * HEAD_DIM : (head + 1) * HEAD_DIM])
        dv_ref[rows] = dv.astype(bf16)
        dk_ref[rows] = dk.astype(bf16)
        turned = jnp.concatenate(turned, axis=0)
        if tile == 0:
            dq_turned = turned
        else:
            dq_turned = jnp.concatenate([dq_turned[:, :at], dq_turned[:, at:] + turned], axis=1)
    dq_ref[...] = (dq_turned * HEAD_DIM ** (-0.5)).T.astype(bf16)


def attend_back(q_pack, k_pack, v_pack, grad, out, rest, weight, causal):
    (q, q_at), (k, k_at), (v, v_at) = q_pack, k_pack, v_pack
    tokens, width = q.shape[1:]
    pairs = width // PAIR
    pair_spec = lambda at: pl.BlockSpec((1, tokens, PAIR), lambda j: (at, 0, j))
    flat_spec = pl.BlockSpec((tokens, PAIR), lambda j: (0, j))
    return pl.pallas_call(
        functools.partial(attend_back_kernel, causal),
        grid=(pairs,),
        in_specs=[
            pair_spec(q_at),
            pair_spec(k_at),
            pair_spec(v_at),
            flat_spec,
            flat_spec,
            flat_spec,
            pl.BlockSpec((2, tokens, tokens), lambda j: (j, 0, 0)),
        ],
        out_specs=[flat_spec] * 3,
        out_shape=[jax.ShapeDtypeStruct((tokens, width), bf16)] * 3,
        compiler_params=params,
        cost_estimate=cost(0.2),
        name="attend_back",
    )(q, k, v, grad, out, rest, weight)


def first_kernel(wanted, count, table_ref, x_ref, out_ref, gains_ref, *refs):
    pieces = refs[:count]
    first_ref, inverse_ref, q_ref, store, sems = refs[-5:]
    step = pl.program_id(0)

    @pl.when(step == 0)
    def load():
        start_loading(pieces, table_ref, wanted, store, sems)

    loaded_once(store, sems, 0)
    z = x_ref[...].astype(f32) + contract(out_ref[...], store[0], 1, 0)
    normal, inverse = normalise(z)
    first = normal * gains_ref[0:1]
    first_ref[...] = first
    inverse_ref[...] = jnp.broadcast_to(inverse, inverse_ref.shape)
    loaded_once(store, sems, 1)
    q = (contract(first.astype(bf16), store[1], 1, 0) * query_scale).astype(bf16)
    q_ref[0] = q


def after_self(x, out, gains, table, pieces, wanted, sooner):
    tokens, width = x.shape
    rows = tokens // 4
    tile = pl.BlockSpec((rows, width), lambda i: (i, 0))
    return pl.pallas_call(
        functools.partial(first_kernel, wanted, len(pieces)),
        grid=(tokens // rows,),
        in_specs=[smem(), tile, tile, pl.BlockSpec(gains.shape, lambda i: (0, 0))]
        + [in_place() for piece in (*pieces, *sooner)],
        out_specs=[
            tile,
            pl.BlockSpec((rows, PAIR), lambda i: (i, 0)),
            pl.BlockSpec((1, rows, width), lambda i: (0, i, 0)),
        ],
        out_shape=[
            jax.ShapeDtypeStruct((tokens, width), f32),
            jax.ShapeDtypeStruct((tokens, PAIR), f32),
            jax.ShapeDtypeStruct((1, tokens, width), bf16),
        ],
        scratch_shapes=stores(len(wanted), width),
        compiler_params=params,
        cost_estimate=cost(0.2),
        name="after_self",
    )(table, x, out, gains, *pieces, *sooner)


def load_feed(feed_pieces, table_ref, kinds, feed_store, feed_sems):
    blocks = feed_store.shape[2]
    for kind in kinds:
        for p, piece in enumerate(feed_pieces):
            rows_at = pl.ds(pl.multiple_of(table_ref[2, p], 16), piece.shape[1])
            pltpu.make_async_copy(
                piece.at[pl.ds(kind * blocks, blocks)],
                feed_store.at[kind, table_ref[1, p], :, rows_at],
                feed_sems.at[kind],
            ).start()


def first_block(feed_store, i):
    return feed_store[0, :, i].reshape(-1, feed_store.shape[-1])


def second_block(feed_store, i):
    devices, blocks = feed_store.shape[1:3]
    return feed_store[1, i * devices // blocks : (i + 1) * devices // blocks].reshape(
        -1, feed_store.shape[-1]
    )


def feed_kernel(
    wanted, count, bucket_ref, lengths_ref, table_ref, first_ref, out_ref, cotangent_ref, gains_ref, down_ref,
    up_ref, *refs,
):
    pieces, feed_pieces = refs[: 3 * count], refs[3 * count : 4 * count]
    (outputs_ref, third_ref, slope_ref, normal_ref, inverse_ref, adapter_ref, down_grad_ref, up_grad_ref,
     down_low, up_low, store, sems, feed_store, feed_sems) = refs[4 * count :]
    rows, width = first_ref.shape
    tokens = rows * pl.num_programs(0)
    step = pl.program_id(0)

    @pl.when(step == 0)
    def begin():
        start_loading(pieces, table_ref, wanted, store, sems)
        load_feed(feed_pieces, table_ref, (0, 1), feed_store, feed_sems)
        down_low[...] = down_ref[...].astype(bf16)
        up_low[...] = up_ref[...].astype(bf16)
        down_grad_ref[...] = jnp.zeros_like(down_grad_ref)
        up_grad_ref[...] = jnp.zeros_like(up_grad_ref)

    loaded_once(store, sems, 0)
    z = first_ref[...] + contract(out_ref[...], store[0], 1, 0)
    second_normal, second_inverse = normalise(z)
    normal_ref[...] = second_normal.astype(bf16)
    inverse_ref[...] = jnp.broadcast_to(second_inverse, inverse_ref.shape)
    second = second_normal * gains_ref[1:2]
    second_low = second.astype(bf16)

    adapter_act, adapter_slope = gelu_and_slope(contract(second_low, down_low[...], 1, 0))
    adapter_act = adapter_act.astype(bf16)
    total = second + 4.0 * contract(adapter_act, up_low[...], 1, 0)
    loaded_once(feed_store, feed_sems, 0)
    loaded_once(feed_store, feed_sems, 1)
    for i in range(feed_store.shape[2]):
        active, slope = gelu_and_slope(contract(second_low, first_block(feed_store, i), 1, 0))
        slope_ref[i] = slope.astype(bf16)
        total += contract(active.astype(bf16), second_block(feed_store, i), 1, 0)

    third_normal, third_inverse = normalise(total)
    outputs_ref[...] = (third_normal * gains_ref[2:3]).astype(bf16)

    shift = item_shift(bucket_ref[0], tokens)
    row = lax.broadcasted_iota(jnp.int32, (rows, 1), 0) + step * rows
    item = row >> shift
    valid = row - (item << shift) < item_length(item, lengths_ref)
    upstream = jnp.where(valid, cotangent_ref[...].astype(f32), 0.0)
    grad_third = normalise_back(upstream * gains_ref[2:3], third_normal, third_inverse)
    third_ref[...] = grad_third

    grad_adapter_out = (4.0 * grad_third).astype(bf16)
    up_grad_ref[...] += contract(adapter_act, grad_adapter_out, 0, 0)
    grad_adapter_pre = (contract(grad_adapter_out, up_low[...], 1, 1) * adapter_slope).astype(bf16)
    adapter_ref[...] = grad_adapter_pre
    down_grad_ref[...] += contract(second_low, grad_adapter_pre, 0, 0)


def feed(bucket, lengths, table, first, out, cotangent, gains, down, up, pieces, output_at, feed_pieces):
    tokens, width = first.shape
    rows = tokens // 4
    chunks, shard_rows = feed_pieces[0].shape[0] // 2, feed_pieces[0].shape[1]
    tile = pl.BlockSpec((rows, width), lambda i: (i, 0))
    fixed = lambda a: pl.BlockSpec(a.shape, lambda i: (0,) * a.ndim, pipeline_mode=pl.Buffered(1))
    return pl.pallas_call(
        functools.partial(feed_kernel, (output_at,), len(feed_pieces)),
        grid=(tokens // rows,),
        in_specs=[smem(), smem(), smem(), tile, tile, tile, fixed(gains), fixed(down), fixed(up)]
        + [in_place() for piece in pieces + feed_pieces],
        out_specs=[
            tile,
            tile,
            pl.BlockSpec((chunks, rows, width), lambda i: (0, i, 0)),
            tile,
            pl.BlockSpec((rows, PAIR), lambda i: (i, 0)),
            pl.BlockSpec((rows, down.shape[1]), lambda i: (i, 0)),
            fixed(down),
            fixed(up),
        ],
        out_shape=[
            jax.ShapeDtypeStruct((tokens, width), bf16),
            jax.ShapeDtypeStruct((tokens, width), f32),
            jax.ShapeDtypeStruct((chunks, tokens, width), bf16),
            jax.ShapeDtypeStruct((tokens, width), bf16),
            jax.ShapeDtypeStruct((tokens, PAIR), f32),
            jax.ShapeDtypeStruct((tokens, down.shape[1]), bf16),
            jax.ShapeDtypeStruct(down.shape, f32),
            jax.ShapeDtypeStruct(up.shape, f32),
        ],
        scratch_shapes=[
            pltpu.VMEM(down.shape, bf16),
            pltpu.VMEM(up.shape, bf16),
            *stores(1, width),
            pltpu.VMEM((2, width // shard_rows, chunks, shard_rows, width), bf16),
            pltpu.SemaphoreType.DMA((2,)),
        ],
        compiler_params=params,
        cost_estimate=cost(0.2),
        name="feed",
    )(bucket, lengths, table, first, out, cotangent, gains, down, up, *pieces, *feed_pieces)


def feed_back_kernel(
    wanted, count, table_ref, third_ref, slope_ref, normal_ref, inverse_ref, adapter_ref, share_ref, gains_ref,
    down_ref, *refs,
):
    pieces, feed_pieces = refs[: 3 * count], refs[3 * count : 4 * count]
    grad_ref, grad_out_ref, down_low, store, sems, feed_store, feed_sems = refs[4 * count :]

    @pl.when(pl.program_id(0) == 0)
    def begin():
        load_feed(feed_pieces, table_ref, (1, 0), feed_store, feed_sems)
        start_loading(pieces, table_ref, wanted, store, sems)
        down_low[...] = down_ref[...].astype(bf16)

    grad_third = third_ref[...]
    grad_feed = grad_third.astype(bf16)
    grad_second = grad_third + contract(adapter_ref[...], down_low[...], 1, 1)
    loaded_once(feed_store, feed_sems, 1)
    loaded_once(feed_store, feed_sems, 0)
    for i in range(feed_store.shape[2]):
        grad_inner = contract(grad_feed, second_block(feed_store, i), 1, 1)
        grad_inner = (grad_inner * slope_ref[i].astype(f32)).astype(bf16)
        grad_second += contract(grad_inner, first_block(feed_store, i), 1, 1)

    grad_pre = normalise_back(
        grad_second * gains_ref[1:2], normal_ref[...].astype(f32), inverse_ref[:, 0:1]
    )
    grad_ref[...] = grad_pre
    loaded_once(store, sems, 0)
    grad_out_ref[...] = (
        contract(grad_pre.astype(bf16), store[0], 1, 1) * spread(share_ref, grad_pre.shape[1])
    ).astype(bf16)


def feed_back(table, third, slope, normal, inverse, adapter, share, gains, down, pieces, output_at, feed_pieces):
    tokens, width = third.shape
    rows = tokens // 4
    chunks, shard_rows = feed_pieces[0].shape[0] // 2, feed_pieces[0].shape[1]
    tile = pl.BlockSpec((rows, width), lambda i: (i, 0))
    fixed = lambda a: pl.BlockSpec(a.shape, lambda i: (0,) * a.ndim, pipeline_mode=pl.Buffered(1))
    return pl.pallas_call(
        functools.partial(feed_back_kernel, (output_at,), len(feed_pieces)),
        grid=(tokens // rows,),
        in_specs=[
            smem(),
            tile,
            pl.BlockSpec((chunks, rows, width), lambda i: (0, i, 0)),
            tile,
            pl.BlockSpec((rows, PAIR), lambda i: (i, 0)),
            pl.BlockSpec((rows, down.shape[1]), lambda i: (i, 0)),
            share_spec(share, rows),
            fixed(gains),
            fixed(down),
        ]
        + [in_place() for piece in pieces + feed_pieces],
        out_specs=[tile, tile],
        out_shape=[
            jax.ShapeDtypeStruct((tokens, width), f32),
            jax.ShapeDtypeStruct((tokens, width), bf16),
        ],
        scratch_shapes=[
            pltpu.VMEM(down.shape, bf16),
            *stores(1, width),
            pltpu.VMEM((2, width // shard_rows, chunks, shard_rows, width), bf16),
            pltpu.SemaphoreType.DMA((2,)),
        ],
        compiler_params=params,
        cost_estimate=cost(0.2),
        name="feed_back",
    )(table, third, slope, normal, inverse, adapter, share, gains, down, *pieces, *feed_pieces)


def cross_back_kernel(
    wanted, table_ref, dq_ref, dk_ref, dv_ref, grad_ref, first_ref, inverse_ref, share_ref, gains_ref,
    *refs,
):
    *pieces, encoder_ref, pre_ref, grad_out_ref, store, sems = refs

    @pl.when(pl.program_id(0) == 0)
    def load():
        start_loading(pieces, table_ref, wanted, store, sems)

    loaded_once(store, sems, 0)
    grad_first = grad_ref[...] + contract(dq_ref[...], store[0], 1, 1)
    loaded_once(store, sems, 1)
    encoder = contract(dk_ref[...], store[1], 1, 1)
    loaded_once(store, sems, 2)
    encoder_ref[...] = (encoder + contract(dv_ref[...], store[2], 1, 1)).astype(bf16)
    gain = gains_ref[0:1]
    grad_pre = normalise_back(grad_first * gain, first_ref[...] / gain, inverse_ref[:, 0:1])
    pre_ref[...] = grad_pre
    loaded_once(store, sems, 3)
    grad_out_ref[...] = (
        contract(grad_pre.astype(bf16), store[3], 1, 1) * spread(share_ref, grad_pre.shape[1])
    ).astype(bf16)


def after_cross_back(dq, dk, dv, grad, first, inverse, share, gains, table, pieces, wanted):
    tokens, width = first.shape
    rows = tokens // 4
    tile = pl.BlockSpec((rows, width), lambda i: (i, 0))
    return pl.pallas_call(
        functools.partial(cross_back_kernel, wanted),
        grid=(tokens // rows,),
        in_specs=[smem()]
        + [tile] * 5
        + [pl.BlockSpec((rows, PAIR), lambda i: (i, 0)), share_spec(share, rows), pl.BlockSpec(gains.shape, lambda i: (0, 0))]
        + [in_place() for piece in pieces],
        out_specs=[tile] * 3,
        out_shape=[
            jax.ShapeDtypeStruct((tokens, width), bf16),
            jax.ShapeDtypeStruct((tokens, width), f32),
            jax.ShapeDtypeStruct((tokens, width), bf16),
        ],
        scratch_shapes=stores(len(wanted), width),
        compiler_params=params,
        cost_estimate=cost(0.2),
        name="after_cross_back",
    )(table, dq, dk, dv, grad, first, inverse, share, gains, *pieces)


def input_kernel(wanted, table_ref, dq_ref, dk_ref, dv_ref, pre_ref, *refs):
    *pieces, out_ref, store, sems = refs

    @pl.when(pl.program_id(0) == 0)
    def load():
        start_loading(pieces, table_ref, wanted, store, sems)

    total = pre_ref[...]
    for slot, ref in enumerate((dq_ref, dk_ref, dv_ref)):
        loaded_once(store, sems, slot)
        total += contract(ref[...], store[slot], 1, 1)
    out_ref[...] = total.astype(bf16)


def input_gradient(dq, dk, dv, pre, table, pieces, wanted):
    tokens, width = pre.shape
    rows = tokens // 4
    tile = pl.BlockSpec((rows, width), lambda i: (i, 0))
    return pl.pallas_call(
        functools.partial(input_kernel, wanted),
        grid=(tokens // rows,),
        in_specs=[smem()] + [tile] * 4 + [in_place() for piece in pieces],
        out_specs=tile,
        out_shape=jax.ShapeDtypeStruct((tokens, width), bf16),
        scratch_shapes=stores(len(wanted), width),
        compiler_params=params,
        cost_estimate=cost(0.2),
        name="input_gradient",
    )(table, dq, dk, dv, pre, *pieces)


def adamw_kernel(*refs):
    for ins, outs in ((refs[0:4], refs[8:13]), (refs[4:8], refs[13:18])):
        master, first_moment, second_moment, gradient = (ref[...] for ref in ins)
        first_new = beta_first * first_moment + (1.0 - beta_first) * gradient
        second_new = beta_second * second_moment + (1.0 - beta_second) * gradient * gradient
        first_hat = first_new / (1.0 - beta_first**STEP)
        second_hat = second_new / (1.0 - beta_second**STEP)
        master_new = master - learn_rate * (
            first_hat / (jnp.sqrt(second_hat) + epsilon_adam) + weight_decay * master
        )
        for ref, value in zip(outs, (gradient, first_new, second_new, master_new, master_new.astype(bf16))):
            ref[...] = value


def adamw(down, up):
    steps = 2

    def spec(array):
        return pl.BlockSpec((array.shape[0] // steps, array.shape[1]), lambda i: (i, 0))

    ins = (*down, *up)
    shapes = [
        jax.ShapeDtypeStruct(arrays[0].shape, kind)
        for arrays in (down, up)
        for kind in (f32, f32, f32, f32, bf16)
    ]
    return pl.pallas_call(
        adamw_kernel,
        grid=(steps,),
        in_specs=[spec(array) for array in ins],
        out_specs=[spec(shape) for shape in shapes],
        out_shape=shapes,
        compiler_params=params,
        cost_estimate=cost(10),
        name="adamw",
    )(*ins)


def pack_kernel(*refs):
    *shards, out_ref = refs
    for i, shard in enumerate(shards):
        out_ref[i] = shard[...]


def pack(shards):
    return pl.pallas_call(
        pack_kernel,
        out_shape=jax.ShapeDtypeStruct((len(shards),) + shards[0].shape, bf16),
        compiler_params=params,
        cost_estimate=cost(2),
        name="pack",
    )(*shards)


def pack_pair_kernel(table_ref, *refs):
    *shards, own_ref, other_ref = refs
    half = len(shards) // 2

    def both(first_ref, second_ref):
        for i in range(half):
            first_ref[i] = shards[i][...]
            second_ref[i] = shards[half + i][...]

    pl.when(table_ref[3, 0] == 0)(functools.partial(both, own_ref, other_ref))
    pl.when(table_ref[3, 0] != 0)(functools.partial(both, other_ref, own_ref))


def pack_pair(table, shards):
    shape = jax.ShapeDtypeStruct((len(shards) // 2,) + shards[0].shape, bf16)
    vmem = pl.BlockSpec(memory_space=pltpu.VMEM)
    return pl.pallas_call(
        pack_pair_kernel,
        in_specs=[smem()] + [vmem] * len(shards),
        out_specs=[vmem, vmem],
        out_shape=[shape, shape],
        compiler_params=params,
        cost_estimate=cost(2),
        name="pack_pair",
    )(table, *shards)


def pack_feed_kernel(first_ref, second_ref, out_ref):
    blocks, rows, width = out_ref.shape
    blocks //= 2
    for i in range(blocks):
        out_ref[i] = first_ref[:, i * width : (i + 1) * width]
        out_ref[blocks + i] = second_ref[i * rows : (i + 1) * rows]


def pack_feed(first, second):
    rows, width = first.shape[0], second.shape[1]
    blocks = (first.size + second.size) // (rows * width)
    return pl.pallas_call(
        pack_feed_kernel,
        out_shape=jax.ShapeDtypeStruct((blocks, rows, width), bf16),
        compiler_params=params,
        cost_estimate=cost(3),
        name="pack_feed",
    )(first, second)


def after_kernel(*refs):
    done_ref = refs[-1]
    done_ref[0] = 0


def after(values, *sooner):
    if not sooner:
        return values
    return pl.pallas_call(
        after_kernel,
        in_specs=[in_place()] * (1 + len(sooner)),
        out_specs=[in_place(), smem()],
        out_shape=[jax.ShapeDtypeStruct(values.shape, values.dtype), jax.ShapeDtypeStruct((1,), jnp.int32)],
        input_output_aliases={0: 0},
        compiler_params=params,
        cost_estimate=cost(0.01),
        name="after",
    )(values, *sooner)[0]


AXES = ("fsdp", "dp")


def ring_order(size):
    return list(range(0, size, 2)) + list(range(size - 1, 0, -2))


class Links:
    def __init__(self, shard_rows):
        self.size, self.parts = lax.axis_size("fsdp"), lax.axis_size("dp")
        order = ring_order(self.size)
        after = {order[i]: order[(i + 1) % self.size] for i in range(self.size)}
        before = {later: sooner for sooner, later in after.items()}
        every = [(f, d) for f in range(self.size) for d in range(self.parts)]
        flat = lambda f, d: f * self.parts + d
        self.onward = [(flat(f, d), flat((before if d % 2 else after)[f], d)) for f, d in every]
        self.sibling = [(flat(f, d), flat(f, d ^ 1)) for f, d in every]
        self.across = [(flat(f, d), flat(f, d ^ 2)) for f, d in every]
        self.core = lax.axis_index("dp") % 2
        self.hops = self.size // 2

        rows, table = shard_rows, []
        for f, d in every:
            place, core, plane = order.index(f), d % 2, d // 2 % 2
            toward = 1 - 2 * core
            shards, inside = [f], [0]
            for hop in range(1, self.hops + 1):
                for sign in (-1, 1):
                    shards.append(order[(place + sign * toward * hop) % self.size])
                    late = core if sign == -1 else 1 - core
                    inside.append(late * (rows // 2) if hop == self.hops else 0)
            first = [shard * rows + at for shard, at in zip(shards, inside)]
            table.append([first, shards, inside, [plane] * len(first)])
        self.table = lax.dynamic_index_in_dim(
            jnp.array(table, jnp.int32), lax.axis_index(AXES), 0, keepdims=False
        )

    def send(self, values, pairs):
        return lax.ppermute(values, AXES, pairs)

    def last(self, values):
        half = values.shape[1] // 2
        return lax.dynamic_slice_in_dim(values, self.core * half, half, 1)


class Gather:
    def __init__(self, links, own, other=None):
        self.links, self.moving, self.count, self.quarter, self.pieces = links, own, 0, 0, []
        self.rest = [] if other is None else [other]

    def share(self, *sooner):
        self.moving = after(self.moving, *sooner)
        self.shared = self.moving
        self.pieces.append(self.moving)
        if self.count:
            self.pieces.append(self.links.send(self.moving, self.links.sibling))
            if self.rest:
                self.crossed = self.links.send(self.moving, self.links.across)
                if self.count < self.links.hops:
                    self.hand_over()

    def hand_over(self, *sooner):
        crossed = after(self.crossed, *sooner)
        self.rest += [crossed, self.links.send(crossed, self.links.sibling)]

    def hop(self, *sooner, chained=False):
        links = self.links
        self.quarter += 1
        while self.count < self.quarter * links.hops // 4:
            if chained and len(self.pieces) > 1:
                sooner = (*sooner, self.pieces[-1], *self.rest[2:][-1:])
            final = self.count + 1 == links.hops
            half = links.last(self.moving) if final and self.rest else None
            self.share(*sooner, *(() if half is None else (half,)))
            sooner = ()
            self.count += 1
            if half is None:
                half = links.last(self.moving) if final else self.moving
            self.moving = links.send(half, links.onward)


def body(
    inputs, encoder, cotangent, buckets, lengths, self_query, self_key, self_value, self_output,
    cross_query, cross_key, cross_value, cross_output, fc_first, fc_second, norm_gains,
    down_master, up_master, down_first, down_second, up_first, up_second,
):
    rows, width = self_query.shape
    links = Links(rows)
    table = links.table
    sq, sk, sv, so = ((None, i) for i in range(4))
    ck, cv, cq, co = (0, 0), (0, 1), (1, 0), (1, 1)
    one = Gather(links, pack((self_query, self_key, self_value, self_output)))
    two = Gather(links, *pack_pair(table, (cross_key, cross_value, cross_query, cross_output)))
    late = Gather(links, pack_feed(fc_first, fc_second))
    two_own, late_own = two.moving, late.moving
    one.hop(chained=True)
    two.hop(chained=True)
    one.hop(two_own, late_own, chained=True)
    two.hop(chained=True)
    one.hop(chained=True)
    two.hop(chained=True)
    one.hop(chained=True)
    two.hop(chained=True)
    fourth = one.moving
    one.share()
    two.share()
    late.hop(fourth)

    qkv = project(inputs, table, one.pieces * 3, (sq, sk, sv), query_scale, (late.shared,))
    two.hand_over(qkv)
    pieces = one.pieces + two.pieces + two.rest
    kv = project(encoder, table, two.pieces + two.pieces + two.rest, (ck, cv), 1.0, (qkv,))
    self_packs = [(qkv, 0), (qkv, 1), (qkv, 2)]
    half = width // PAIR // 2
    late.hop(qkv, kv)
    *self_half, done = attend(buckets, lengths, *self_packs, True, 0, half, (), (late.shared,))
    self_out, self_rest, self_weight, self_share, done = attend(
        buckets, lengths, *self_packs, True, half, 2 * half, self_half
    )
    late.hop(done)
    first, first_inverse, query_cross = after_self(
        inputs, self_out, norm_gains, table, pieces, (so, cq), (late.shared,)
    )
    cross_packs = [(query_cross, 0), (kv, 0), (kv, 1)]
    *cross_half, done = attend(buckets, lengths, *cross_packs, False, 0, half)
    late.hop(done)
    cross_out, cross_rest, cross_weight, cross_share, done = attend(
        buckets, lengths, *cross_packs, False, half, 2 * half, cross_half, (late.shared,)
    )
    late.share(done)

    outputs, grad_third, slope, second_normal, second_inverse, adapter, down_local, up_local = feed(
        buckets, lengths, table, first, cross_out, cotangent, norm_gains, down_master, up_master, pieces, co,
        late.pieces,
    )
    down_grad, up_grad = lax.psum((down_local, up_local), ("fsdp", "dp"))

    grad_cross_pre, grad_cross_out = feed_back(
        table, grad_third, slope, second_normal, second_inverse, adapter, cross_share, norm_gains, down_master,
        pieces, co, late.pieces,
    )
    dq, dk, dv = attend_back(*cross_packs, grad_cross_out, cross_out, cross_rest, cross_weight, False)
    encoder_grad, grad_self_pre, grad_self_out = after_cross_back(
        dq, dk, dv, grad_cross_pre, first, first_inverse, self_share, norm_gains, table, pieces, (cq, ck, cv, so)
    )
    dq, dk, dv = attend_back(*self_packs, grad_self_out, self_out, self_rest, self_weight, True)
    input_grad = input_gradient(dq, dk, dv, grad_self_pre, table, pieces, (sq, sk, sv))

    (
        down_grad, down_first_new, down_second_new, down_master_new, down_weight,
        up_grad, up_first_new, up_second_new, up_master_new, up_weight,
    ) = adamw(
        (down_master, down_first, down_second, down_grad), (up_master, up_first, up_second, up_grad)
    )
    return (
        outputs,
        input_grad,
        encoder_grad,
        down_grad,
        up_grad,
        down_first_new,
        down_second_new,
        up_first_new,
        up_second_new,
        down_master_new,
        up_master_new,
        down_weight,
        up_weight,
    )


def solution(mesh):
    tokens, matrix = P(("fsdp", "dp"), None), P("fsdp", None)
    return jax.shard_map(
        body,
        mesh=mesh,
        in_specs=(tokens, tokens, tokens, P(("fsdp", "dp")), tokens) + (matrix,) * 10 + (P(),) * 7,
        out_specs=(tokens,) * 3 + (P(),) * 10,
        check_vma=False,
    )
```
